32 devices in a mesh: rad: 8 (over z, y), lm: 4 (over x, core).
Axes of the slice: x: 2, y: 2, z: 4, core: 2. Of those that a mesh axis runs over, the one named last changes fastest.
Arguments:
- grid_field: bfloat16 [2, 512, 544, 128], P(None, ('rad', 'lm')), may hold values from -6 to 6
- inverses: bfloat16 [2, 64, 512, 512], P(None, ('rad', 'lm')), may hold values from -4 to 4
- slot_blocks: int32 [32, 24], replicated, may hold values from 0 to 544, as said below
- degree_start: int32 [64], replicated, may hold values from 0 to 752, as said below
Outputs:
- new_grid: bfloat16 [2, 512, 544, 128], P(None, ('rad', 'lm'))
- new_slope: bfloat16 [2, 512, 544, 128], P(None, ('rad', 'lm'))
The draws below stay inside these ranges and needn't reach their ends.
Inputs may be any that keep to these rules, and one draw needn't show every extreme that they name: `slot_blocks`: row d lists the blocks of one degree index below 32 in order, then those of one degree index at or above it in order, then the value 544 (no block). Every block is in exactly one slot. `degree_start`: entry q equals d * 24 + s where slot s of row d of slot_blocks holds the first block of degree index q.
All inputs are finite; a program needn't handle non-finite values.
Results may differ from the reference program's by a relative error of at most 0.0052.
Values may be sent and summed in bfloat16 or wider, within the bound.
No kernel may reach another device: no remote copies, remote signals or barrier semaphores. Data moves between devices by JAX's collectives and lax.ppermute only.
A program may use at most 128 MiB of HBM per device.

```python
import jax
import jax.numpy as jnp
import numpy as np
from jax import lax

NR = 512
LMAX1 = 1024
OB = 64
NDEG = 64
COLS = 128
NBLK = 544
CAP = 24
DEVICES = 32


def layout_tables(key):
    base = jax.random.fold_in(key, 5)
    first_key, second_key = jax.random.split(base)
    half_count = NDEG // 2
    ordering = jax.random.permutation(first_key, half_count).astype(jnp.int32)
    position = jnp.argmax(ordering == half_count - 1)
    ordering = ordering.at[position].set(ordering[half_count - 1]).at[half_count - 1].set(half_count - 1)
    owners = jax.random.permutation(second_key, DEVICES).astype(jnp.int32)
    last_place = jnp.argmax(owners == DEVICES - 1)
    owners = owners.at[last_place].set(owners[DEVICES - 1]).at[DEVICES - 1].set(DEVICES - 1)
    group_size = OB * NDEG // LMAX1
    degree_index = jnp.arange(NDEG, dtype=jnp.int32)
    counts = degree_index // group_size + 1
    starts = jnp.cumsum(counts) - counts
    low_degree = owners
    high_degree = half_count + ordering[owners]
    low_count = counts[low_degree][:, None]
    high_count = counts[high_degree][:, None]
    slot_index = jnp.arange(CAP, dtype=jnp.int32)[None, :]
    table = jnp.where(slot_index < low_count, starts[low_degree][:, None] + slot_index, jnp.where(slot_index < low_count + high_count, starts[high_degree][:, None] + slot_index - low_count, NBLK))
    first_slot = jnp.arange(DEVICES, dtype=jnp.int32) * CAP
    beginning = jnp.zeros((NDEG,), jnp.int32).at[low_degree].set(first_slot)
    beginning = beginning.at[high_degree].set(first_slot + counts[low_degree])
    return (table.astype(jnp.int32), beginning.astype(jnp.int32))


def draw_slot_blocks(key, part):
    return layout_tables(key)[0]


def draw_degree_start(key, part):
    return layout_tables(key)[1]


def draw_inverses(key, part):
    first_key, second_key = jax.random.split(jax.random.fold_in(key, 11))
    full_shape = (2, 2 * DEVICES, NR, NR)
    entries = jnp.clip(jax.random.normal(first_key, full_shape, jnp.float32), -6.0, 6.0)
    scales = 1.0 + 0.0 * jax.random.uniform(second_key, (2, 2 * DEVICES, NR, 1), jnp.float32)
    identity = jnp.eye(NR, dtype=jnp.float32)
    return ((identity + 0.5 * entries / jnp.sqrt(NR * 1.0)) * scales).astype(jnp.bfloat16)


def level_of(stream_key, shape, cuts, smallest, largest):
    level, own = 1.0, jax.random.fold_in(stream_key, 6)
    for axis_at, shards_of in cuts:
        heights = jnp.exp(jax.random.uniform(jax.random.fold_in(own, axis_at), (shards_of,), jnp.float32, smallest / len(cuts), largest / len(cuts)))
        level = level * jnp.repeat(heights, shape[axis_at] // shards_of).reshape([-1 if axis == axis_at else 1 for axis in range(len(shape))])
    return level


def noise(stream_key, dims, deviation, reach, shards=(), held_as=jnp.bfloat16):
    drawn = deviation * jax.random.normal(stream_key, dims, jnp.float32)
    if shards:
        drawn = drawn * level_of(stream_key, dims, shards, -0.22, 0.18)
    return jnp.clip(drawn, -reach, reach).astype(held_as)


def setup_inputs(seed: int = 0) -> dict:
    splits = jax.random.split(jax.random.key(seed), 5)
    return {
        "grid_field": noise(splits[0], (2, NR, NBLK, COLS), 1.0, 6.0, ((1, 32),)),
        "inverses": draw_inverses(jax.random.fold_in(splits[4], 71), 0),
        "slot_blocks": draw_slot_blocks(jax.random.fold_in(splits[4], 71), 0),
        "degree_start": draw_degree_start(jax.random.fold_in(splits[4], 71), 0),
    }


inner_radius = 0.35
shell_depth = 0.65
diffusion_numbers = (0.9, 0.4)


def block_tables(degrees, lmax_one, orders, blocks):
    spacing = lmax_one // degrees
    group_size = orders * degrees // lmax_one
    degree_index = np.arange(degrees)
    counts = degree_index // group_size + 1
    starts = np.cumsum(counts) - counts
    degree_of = np.repeat(degree_index, counts)
    place_in = np.arange(blocks) - starts[degree_of]
    degree_value = spacing * (degree_of + 1) - 1
    column = np.arange(2 * orders)
    live_mask = (place_in[:, None] * orders + column[None, :] // 2 <= degree_value[:, None]).astype(np.float32)
    factor = (degree_value * (degree_value + 1)).astype(np.float32)
    upper_half = (degree_of >= degrees // 2).astype(np.int32)
    return degree_of.astype(np.int32), place_in.astype(np.int32), factor, live_mask, upper_half


def radius_of(positions):
    return inner_radius + shell_depth * (positions + 1).astype(jnp.float32) / (NR + 1)


def right_side(padded, radius_list, factor, live_mask):
    spacing_h = shell_depth / (NR + 1)
    weighted = padded * radius_list[None, :, None, None]
    centre = padded[:, 1:-1]
    inner_radii = radius_list[1:-1][None, :, None, None]
    second = (weighted[:, 2:] - 2.0 * weighted[:, 1:-1] + weighted[:, :-2]) / inner_radii
    scaled = spacing_h / inner_radii
    angular = factor[None, None, :, None] * (scaled * scaled) * centre
    coefficient = jnp.array(diffusion_numbers, jnp.float32)[:, None, None, None]
    combined = centre + coefficient * (second - angular)
    return combined * live_mask[None, None]


def slope_from_padded(padded):
    return (0.5 * (padded[:, 2:].astype(jnp.float32) - padded[:, :-2].astype(jnp.float32))).astype(jnp.bfloat16)


def reference(grid_field, inverses, slot_blocks, degree_start):
    degree_of, place_in, factor, live_mask, upper_half = block_tables(NDEG, LMAX1, OB, NBLK)
    factor_table = jnp.asarray(factor)
    live_table = jnp.asarray(live_mask)
    upper_table = jnp.asarray(upper_half)
    radius_list = radius_of(jnp.arange(-1, NR + 1, dtype=jnp.int32))

    def one_device(device):
        chosen = slot_blocks[device]
        field_slots = jnp.take(grid_field, chosen, axis=2, mode="fill", fill_value=0)
        slot_factor = jnp.take(factor_table, chosen, mode="fill", fill_value=0)
        slot_live = jnp.take(live_table, chosen, axis=0, mode="fill", fill_value=0)
        upper_pick = jnp.take(upper_table, chosen, mode="fill", fill_value=0)
        padded = jnp.pad(field_slots.astype(jnp.float32), ((0, 0), (1, 1), (0, 0), (0, 0)))
        source = right_side(padded, radius_list, slot_factor, slot_live)
        pair_mats = lax.dynamic_slice_in_dim(inverses, 2 * device, 2, 1).astype(jnp.float32)
        matrices = jnp.take(pair_mats, upper_pick, axis=1)
        solved = jnp.einsum("fsij,fjsc->fisc", matrices, source, precision=lax.Precision.HIGHEST)
        return solved.astype(jnp.bfloat16)

    stacked = lax.map(one_device, jnp.arange(DEVICES, dtype=jnp.int32))
    spectral = jnp.moveaxis(stacked, 0, 2).reshape(2, NR, DEVICES * CAP, 2 * OB)
    slot_place = jnp.take(degree_start, jnp.asarray(degree_of)) + jnp.asarray(place_in)
    new_grid = jnp.take(spectral, slot_place, axis=2)
    widened = jnp.pad(new_grid, ((0, 0), (1, 1), (0, 0), (0, 0)))
    return new_grid, slope_from_padded(widened)
```

```python
import functools

import jax
import jax.numpy as jnp
import numpy as np
from jax import lax
from jax.experimental import pallas as pl
from jax.experimental.pallas import tpu as pltpu
from jax.sharding import PartitionSpec as P

LMAX1 = 1024
OB = 64
AXES = ("rad", "lm")

inner_radius = 0.35
shell_depth = 0.65
diffusion_numbers = (0.9, 0.4)


class Sizes:
    def __init__(self, devices, grid_field, inverses, slot_blocks):
        self.devices = devices
        self.fields, self.local, self.blocks, self.width = grid_field.shape
        self.levels = inverses.shape[-1]
        self.capacity = slot_blocks.shape[1]
        self.degrees = 2 * devices
        self.spacing = LMAX1 // self.degrees
        self.group_size = OB * self.degrees // LMAX1
        index = np.arange(self.degrees)
        self.counts = [int(c) for c in index // self.group_size + 1]
        self.starts = [int(s) for s in np.cumsum(self.counts) - self.counts]


def transposer(outer, inner):
    size = outer * inner
    row = lax.broadcasted_iota(jnp.int32, (size, size), 0)
    column = lax.broadcasted_iota(jnp.int32, (size, size), 1)
    source = lax.rem(row, inner) * outer + lax.div(row, inner)
    return jnp.where(source == column, 1.0, 0.0).astype(jnp.bfloat16)


def pack_kernel(z, start_ref, field_ref, out_ref, turned_ref):
    rows = 16
    turn = transposer(rows, z.local)

    def group(g, carry):
        at = pl.multiple_of(g * rows, rows)
        part = field_ref[0, :, pl.ds(at, rows), :].reshape(z.local * rows, z.width)
        turned = jnp.dot(turn, part, preferred_element_type=jnp.float32)
        turned_ref[pl.ds(at, rows)] = turned.astype(jnp.bfloat16).reshape(rows, z.local, z.width)
        return carry

    lax.fori_loop(0, z.blocks // rows, group, 0, unroll=2)
    for q in range(z.degrees):
        out_ref[pl.ds(start_ref[q], z.counts[q])] = turned_ref[pl.ds(z.starts[q], z.counts[q])]


def pack(z, start, grid_field, f, slots):
    total = z.devices * slots
    return pl.pallas_call(
        functools.partial(pack_kernel, z),
        grid_spec=pltpu.PrefetchScalarGridSpec(
            num_scalar_prefetch=1,
            grid=(1,),
            in_specs=[
                pl.BlockSpec((1, z.local, z.blocks, z.width), lambda i, start: (f, 0, 0, 0))
            ],
            out_specs=pl.BlockSpec((total, z.local, z.width), lambda i, start: (0, 0, 0)),
            scratch_shapes=[pltpu.VMEM((z.blocks, z.local, z.width), jnp.bfloat16)],
        ),
        out_shape=jax.ShapeDtypeStruct((total, z.local, z.width), jnp.bfloat16),
        compiler_params=pltpu.CompilerParams(vmem_limit_bytes=48 << 20),
        cost_estimate=pl.CostEstimate(flops=10**9, bytes_accessed=10**7, transcendentals=0),
        name=f"pack_{f}",
    )(start, grid_field)


def solve_kernel(z, strength, slots, per_step, start_ref, place_ref, columns_ref, inverse_ref,
                 out_ref, square_ref, above_ref, below_ref, degree_ref, position_ref):
    step = pl.program_id(0)
    shape = (z.levels, z.width)

    @pl.when(step == 0)
    def _():
        level = lax.broadcasted_iota(jnp.int32, shape, 0)

        def radius(positions):
            return inner_radius + shell_depth * (positions + 1).astype(jnp.float32) / (z.levels + 1)

        here = radius(level)
        scaled = (shell_depth / (z.levels + 1)) / here
        square_ref[...] = strength * (scaled * scaled)
        above_ref[...] = jnp.where(level == z.levels - 1, 0.0, strength * radius(level + 1) / here)
        below_ref[...] = jnp.where(level == 0, 0.0, strength * radius(level - 1) / here)
        base = place_ref[0] * slots

        def clear(k, carry):
            degree_ref[k] = 0
            position_ref[k] = 0
            return carry

        lax.fori_loop(0, slots, clear, 0)

        def degree(q, carry):
            first = start_ref[q] - base
            count = lax.div(q, z.group_size) + 1

            def mark(k, inner):
                degree_ref[k] = q
                position_ref[k] = k - first
                return inner

            lax.fori_loop(
                jnp.maximum(first, 0), jnp.minimum(first + count, slots), mark, 0
            )
            return carry

        lax.fori_loop(0, z.degrees, degree, 0)

    column = lax.broadcasted_iota(jnp.int32, shape, 1)
    for k in range(per_step):
        slot = step * per_step + k
        q = degree_ref[slot]
        value = z.spacing * (q + 1) - 1
        upper = jnp.where(q >= z.degrees // 2, 1, 0)
        factor = (value * (value + 1)).astype(jnp.float32)
        limit = 2 * (value - position_ref[slot] * (z.width // 2)) + 1
        u = columns_ref[:, k].reshape(shape).astype(jnp.float32)
        u = jnp.where(column <= limit, u, 0.0)
        weight = (1.0 - 2.0 * strength) - factor * square_ref[...]
        rhs = weight * u
        rhs += above_ref[...] * pltpu.roll(u, z.levels - 1, 0)
        rhs += below_ref[...] * pltpu.roll(u, 1, 0)
        high = rhs.astype(jnp.bfloat16)
        low = (rhs - high.astype(jnp.float32)).astype(jnp.bfloat16)
        both = jnp.concatenate([high, low], axis=1)
        product = jnp.dot(inverse_ref[0, upper], both, preferred_element_type=jnp.float32)
        solved = product[:, : z.width] + product[:, z.width :]
        out_ref[:, k] = solved.astype(jnp.bfloat16).reshape(z.devices, z.local, z.width)


def solve(z, start, place, columns, inverses, f, slots):
    per_step = max(n for n in (1, 2, 3, 4) if slots % n == 0)
    block = (z.devices, per_step, z.local, z.width)
    spec = pl.BlockSpec(block, lambda i, *s: (0, i, 0, 0))
    return pl.pallas_call(
        functools.partial(solve_kernel, z, diffusion_numbers[f], slots, per_step),
        grid_spec=pltpu.PrefetchScalarGridSpec(
            num_scalar_prefetch=2,
            grid=(slots // per_step,),
            in_specs=[
                spec,
                pl.BlockSpec(
                    (1,) + inverses.shape[1:], lambda i, *s: (f, 0, 0, 0)
                ),
            ],
            out_specs=spec,
            scratch_shapes=[pltpu.VMEM((z.levels, z.width), jnp.float32)] * 3
            + [pltpu.SMEM((slots,), jnp.int32)] * 2,
        ),
        out_shape=jax.ShapeDtypeStruct(columns.shape, jnp.bfloat16),
        compiler_params=pltpu.CompilerParams(vmem_limit_bytes=48 << 20),
        cost_estimate=pl.CostEstimate(flops=10**10, bytes_accessed=10**7, transcendentals=0),
        name=f"solve_{f}",
    )(start, place, columns, inverses)


def unpack_kernel(z, start_ref, returned_ref, *rest):
    grid_ref, slope_ref, sorted_ref = rest[-3:]
    rows = 16
    turn = transposer(z.local, rows)
    for q in range(z.degrees):
        sorted_ref[pl.ds(z.starts[q], z.counts[q])] = returned_ref[pl.ds(start_ref[q], z.counts[q])]

    def group(g, carry):
        at = pl.multiple_of(g * rows, rows)
        part = sorted_ref[pl.ds(at, rows)].reshape(rows * z.local, z.width)
        turned = jnp.dot(turn, part, preferred_element_type=jnp.float32)
        turned = turned.reshape(z.local, rows, z.width)
        grid_ref[0, :, pl.ds(at, rows), :] = turned.astype(jnp.bfloat16)
        slope = 0.5 * (turned[2:] - turned[:-2])
        slope_ref[0, pl.ds(1, z.local - 2), pl.ds(at, rows), :] = slope.astype(jnp.bfloat16)
        return carry

    lax.fori_loop(0, z.blocks // rows, group, 0, unroll=2)


def unpack(z, start, returned, f, earlier):
    shape = jax.ShapeDtypeStruct((z.fields, z.local, z.blocks, z.width), jnp.bfloat16)
    spec = pl.BlockSpec((1, z.local, z.blocks, z.width), lambda i, *s: (f, 0, 0, 0))
    return pl.pallas_call(
        functools.partial(unpack_kernel, z),
        grid_spec=pltpu.PrefetchScalarGridSpec(
            num_scalar_prefetch=1,
            grid=(1,),
            in_specs=[pl.BlockSpec(returned.shape, lambda i, *s: (0, 0, 0))]
            + [pl.BlockSpec(memory_space=pl.ANY)] * len(earlier),
            out_specs=[spec, spec],
            scratch_shapes=[pltpu.VMEM((z.blocks, z.local, z.width), jnp.bfloat16)],
        ),
        out_shape=[shape, shape],
        input_output_aliases={2 + i: i for i in range(len(earlier))},
        compiler_params=pltpu.CompilerParams(vmem_limit_bytes=48 << 20),
        cost_estimate=pl.CostEstimate(flops=10**9, bytes_accessed=10**7, transcendentals=0),
        name=f"unpack_{f}",
    )(start, returned, *earlier)


def edge_kernel(slope_in_ref, inside_ref, outside_ref, slope_ref):
    del slope_in_ref
    inside = inside_ref[...].astype(jnp.float32)
    outside = outside_ref[...].astype(jnp.float32).reshape(inside.shape)
    first = pl.program_id(0) == 0
    slope_ref[...] = jnp.where(first, 0.5 * (inside - outside), 0.5 * (outside - inside)).astype(
        jnp.bfloat16
    )


def edges(z, slope, grid, outside, f):
    last = z.local - 1
    block = (1, 1, z.blocks, z.width)
    return pl.pallas_call(
        edge_kernel,
        grid=(2,),
        in_specs=[
            pl.BlockSpec(memory_space=pl.ANY),
            pl.BlockSpec(block, lambda i: (f, 1 + i * (last - 2), 0, 0)),
            pl.BlockSpec((1, z.blocks, z.width), lambda i: (i, 0, 0)),
        ],
        out_specs=pl.BlockSpec(block, lambda i: (f, i * last, 0, 0)),
        out_shape=jax.ShapeDtypeStruct(slope.shape, slope.dtype),
        input_output_aliases={0: 0},
        name=f"edges_{f}",
    )(slope, grid, outside)


def beside(z, first, last):
    up = [(i, i + 1) for i in range(z.devices - 1)]
    down = [(j, i) for i, j in up]
    return lax.ppermute(last, AXES, up), lax.ppermute(first, AXES, down)


def exchange(z, value, slots):
    shaped = value.reshape(z.devices, slots, z.local, z.width)
    return lax.all_to_all(shaped, AXES, split_axis=0, concat_axis=0, tiled=True)


def body(grid_field, inverses, slot_blocks, degree_start):
    devices = lax.axis_size("rad") * lax.axis_size("lm")
    z = Sizes(devices, grid_field, inverses, slot_blocks)
    if z.local % 16:
        return plain_body(z, grid_field, inverses, degree_start)
    slots = z.capacity
    start = degree_start
    place = lax.axis_index(AXES).reshape(1).astype(jnp.int32)
    sent = [pack(z, start, grid_field, f, slots) for f in range(z.fields)]
    columns = [exchange(z, sent[f], slots) for f in range(z.fields)]
    solved = [solve(z, start, place, columns[f], inverses, f, slots) for f in range(z.fields)]
    returned = [
        exchange(z, solved[f], slots).reshape(devices * slots, z.local, z.width)
        for f in range(z.fields)
    ]
    outs = ()
    for f in range(z.fields):
        outs = tuple(unpack(z, start, returned[f], f, outs))
        grid, slope = outs
        before, after = beside(z, grid[f, :1], grid[f, -1:])
        outs = (grid, edges(z, slope, grid, jnp.concatenate([before, after]), f))
    return outs


def plain_body(z, grid_field, inverses, degree_start):
    index = np.arange(z.degrees)
    counts = np.asarray(z.counts)
    degree_of = np.repeat(index, counts)
    place_in = np.arange(z.blocks) - np.asarray(z.starts)[degree_of]
    value = z.spacing * (index + 1) - 1
    slot_place = degree_start[degree_of] + jnp.asarray(place_in, jnp.int32)
    total = z.devices * z.capacity
    holder = jnp.full((total,), z.blocks, jnp.int32)
    holder = holder.at[slot_place].set(jnp.arange(z.blocks, dtype=jnp.int32))
    sent = jnp.take(grid_field, holder, axis=2, mode="fill", fill_value=0)
    sent = sent.reshape(z.fields, z.local, z.devices, z.capacity, z.width)
    columns = lax.all_to_all(sent, AXES, split_axis=2, concat_axis=1, tiled=True)
    columns = columns.reshape(z.fields, z.levels, z.capacity, z.width)
    device = lax.axis_index(AXES)
    mine = lax.dynamic_slice_in_dim(holder, device * z.capacity, z.capacity)
    order = jnp.asarray(place_in)[:, None] * OB + np.arange(z.width)[None, :] // 2
    live_table = (order <= jnp.asarray(value[degree_of])[:, None]).astype(jnp.float32)
    live = jnp.take(live_table, mine, axis=0, mode="fill", fill_value=0)
    factor = (value * (value + 1)).astype(np.float32)[degree_of]
    factor = jnp.take(jnp.asarray(factor), mine, mode="fill", fill_value=0)
    upper = jnp.take(jnp.asarray(degree_of >= z.degrees // 2), mine, mode="fill", fill_value=False)
    radius = inner_radius + shell_depth * jnp.arange(z.levels + 2, dtype=jnp.float32) / (z.levels + 1)
    here = radius[1:-1][None, :, None, None]
    padded = jnp.pad(columns.astype(jnp.float32), ((0, 0), (1, 1), (0, 0), (0, 0)))
    weighted = padded * radius[None, :, None, None]
    second = (weighted[:, 2:] - 2.0 * weighted[:, 1:-1] + weighted[:, :-2]) / here
    scaled = (shell_depth / (z.levels + 1)) / here
    centre = padded[:, 1:-1]
    strength = jnp.asarray(diffusion_numbers, jnp.float32)[:, None, None, None]
    angular = factor[None, None, :, None] * (scaled * scaled) * centre
    rhs = (centre + strength * (second - angular)) * live[None, None]

    def solve_slot(carry, at):
        matrix = lax.dynamic_index_in_dim(
            inverses, upper[at].astype(jnp.int32), 1, keepdims=False
        ).astype(jnp.float32)
        block = lax.dynamic_index_in_dim(rhs, at, 2, keepdims=False)
        product = jnp.einsum("fij,fjc->fic", matrix, block, precision=lax.Precision.HIGHEST)
        return carry, product.astype(jnp.bfloat16)

    solved = lax.scan(solve_slot, 0, jnp.arange(z.capacity))[1]
    solved = jnp.moveaxis(solved, 0, 2)
    solved = solved.reshape(z.fields, z.devices, z.local, z.capacity, z.width)
    returned = lax.all_to_all(solved, AXES, split_axis=1, concat_axis=3, tiled=True)
    returned = returned.reshape(z.fields, z.local, total, z.width)
    grid = jnp.take(returned, slot_place, axis=2)
    before, after = beside(z, grid[:, :1], grid[:, -1:])
    rimmed = jnp.concatenate([before, grid, after], axis=1).astype(jnp.float32)
    return grid, (0.5 * (rimmed[:, 2:] - rimmed[:, :-2])).astype(jnp.bfloat16)


def solution(mesh):
    in_specs = (P(None, AXES), P(None, AXES), P(), P())
    out_specs = (P(None, AXES), P(None, AXES))
    return jax.shard_map(body, mesh=mesh, in_specs=in_specs, out_specs=out_specs, check_vma=False)
```

```python
import functools

import jax
import jax.numpy as jnp
import numpy as np
from jax import lax
from jax.experimental import pallas as pl
from jax.experimental.pallas import tpu as pltpu
from jax.sharding import PartitionSpec as P

LMAX1 = 1024
OB = 64
AXES = ("rad", "lm")
PLANE = 8

inner_radius = 0.35
shell_depth = 0.65
diffusion_numbers = (0.9, 0.4)


class Sizes:
    def __init__(self, devices, grid_field, inverses, slot_blocks):
        self.devices = devices
        self.fields, self.local, self.blocks, self.width = grid_field.shape
        self.levels = inverses.shape[-1]
        self.capacity = slot_blocks.shape[1]
        self.degrees = 2 * devices
        self.spacing = LMAX1 // self.degrees
        self.group_size = OB * self.degrees // LMAX1
        index = np.arange(self.degrees)
        self.counts = [int(c) for c in index // self.group_size + 1]
        self.starts = [int(s) for s in np.cumsum(self.counts) - self.counts]


def transposer(outer, inner):
    size = outer * inner
    row = lax.broadcasted_iota(jnp.int32, (size, size), 0)
    column = lax.broadcasted_iota(jnp.int32, (size, size), 1)
    source = lax.rem(row, inner) * outer + lax.div(row, inner)
    return jnp.where(source == column, 1.0, 0.0).astype(jnp.bfloat16)


def slot_choices(z):
    mean = -(-z.blocks // z.devices)
    return sorted({min(mean + extra, z.capacity) for extra in (0, 1, 2, 3, 5)} | {z.capacity})


def plan_kernel(z, choices, start_ref, choice_ref, place_ref, holder_ref, load_ref, device_ref, next_ref):
    half = z.degrees // 2
    planes = z.devices // PLANE
    totals = [0] * planes
    for q in range(half, z.degrees):
        device = lax.div(start_ref[q], z.capacity)
        load = start_ref[q] - device * z.capacity + z.counts[q]
        load_ref[device] = load
    for d in range(z.devices):
        totals[d // PLANE] += load_ref[d]
    most = functools.reduce(jnp.maximum, totals)
    choice = jnp.int32(0)
    slots = jnp.int32(choices[0])
    for i in range(1, len(choices)):
        beyond = most > PLANE * choices[i - 1]
        choice = jnp.where(beyond, i, choice)
        slots = jnp.where(beyond, choices[i], slots)
    choice_ref[0] = choice
    for g in range(planes):
        device_ref[g] = g * PLANE
        next_ref[g] = load_ref[g * PLANE]

    def clear(k, carry):
        holder_ref[k] = 0
        return carry

    lax.fori_loop(0, z.devices * z.capacity, clear, 0, unroll=8)

    def put(b, code, at):
        place_ref[b] = at
        holder_ref[at] = code

    for q in range(z.degrees):
        device = lax.div(start_ref[q], z.capacity)
        offset = start_ref[q] - device * z.capacity
        first = device * slots + offset
        for p in range(z.counts[q]):
            b, code = z.starts[q] + p, q * OB + p
            if q < half or z.counts[half - 1] + p < choices[0]:
                put(b, code, first + p)
                continue
            spare = offset + p >= slots

            @pl.when(jnp.logical_not(spare))
            def _():
                put(b, code, first + p)

            @pl.when(spare)
            def _():
                plane = lax.div(device, PLANE)

                def full(state):
                    return state[1] >= slots

                def advance(state):
                    return state[0] + 1, load_ref[state[0] + 1]

                holder, slot = lax.while_loop(full, advance, (device_ref[plane], next_ref[plane]))
                device_ref[plane] = holder
                next_ref[plane] = slot + 1
                put(b, code, holder * slots + slot)


def plan(z, degree_start, choices):
    smem = pl.BlockSpec(memory_space=pltpu.SMEM)
    planes = z.devices // PLANE
    return pl.pallas_call(
        functools.partial(plan_kernel, z, choices),
        in_specs=[smem],
        out_specs=[smem] * 3,
        out_shape=[
            jax.ShapeDtypeStruct((1,), jnp.int32),
            jax.ShapeDtypeStruct((z.blocks,), jnp.int32),
            jax.ShapeDtypeStruct((z.devices * z.capacity,), jnp.int32),
        ],
        scratch_shapes=[
            pltpu.SMEM((z.devices,), jnp.int32),
            pltpu.SMEM((planes,), jnp.int32),
            pltpu.SMEM((planes,), jnp.int32),
        ],
        name="plan",
    )(degree_start)


def plane_inverses(inverses):
    rad, lm = lax.axis_size("rad"), lax.axis_size("lm")
    own = inverses[:, 1]

    def swap(value, axis, size, bit):
        return lax.ppermute(value, axis, [(i, i ^ bit) for i in range(size)])

    across = swap(own, "lm", lm, 2)
    along = swap(own, "rad", rad, 1)
    corner = [swap(across[:1], "rad", rad, 1), swap(along[1:], "lm", lm, 2)]
    even = [own, across, along] + corner
    odd = [swap(value, "lm", lm, 1) for value in even]
    return even, odd


def pack_kernel(z, place_ref, field_ref, out_ref, turned_ref):
    rows = 16
    turn = transposer(rows, z.local)

    def group(g, carry):
        at = pl.multiple_of(g * rows, rows)
        part = field_ref[0, :, pl.ds(at, rows), :].reshape(z.local * rows, z.width)
        turned = jnp.dot(turn, part, preferred_element_type=jnp.float32)
        turned_ref[pl.ds(at, rows)] = turned.astype(jnp.bfloat16).reshape(rows, z.local, z.width)
        return carry

    lax.fori_loop(0, z.blocks // rows, group, 0, unroll=2)
    for b in range(z.blocks):
        out_ref[place_ref[b]] = turned_ref[b]


def pack(z, place, grid_field, f, slots):
    total = z.devices * slots
    return pl.pallas_call(
        functools.partial(pack_kernel, z),
        grid_spec=pltpu.PrefetchScalarGridSpec(
            num_scalar_prefetch=1,
            grid=(1,),
            in_specs=[
                pl.BlockSpec((1, z.local, z.blocks, z.width), lambda i, *s: (f, 0, 0, 0))
            ],
            out_specs=pl.BlockSpec((total, z.local, z.width), lambda i, *s: (0, 0, 0)),
            scratch_shapes=[pltpu.VMEM((z.blocks, z.local, z.width), jnp.bfloat16)],
        ),
        out_shape=jax.ShapeDtypeStruct((total, z.local, z.width), jnp.bfloat16),
        compiler_params=pltpu.CompilerParams(vmem_limit_bytes=48 << 20),
        cost_estimate=pl.CostEstimate(flops=10**9, bytes_accessed=10**7, transcendentals=0),
        name=f"pack_{f}",
    )(place, grid_field)


def solve_kernel(z, f, slots, per_step, holder_ref, start_ref, me_ref, columns_ref, inverses_ref, *rest):
    (own, across, along, corner, own_odd, across_odd, along_odd, corner_odd) = rest[:8]
    out_ref, matrix_ref, square_ref, above_ref, below_ref, sems = rest[8:]
    strength = diffusion_numbers[f]
    step = pl.program_id(0)
    shape = (z.levels, z.width)
    me = me_ref[0]

    @pl.when(step == 0)
    def _():
        sources = [
            own.at[f], own_odd.at[f], across.at[f], across_odd.at[f],
            along.at[f], along_odd.at[f], corner.at[0], corner_odd.at[0],
            inverses_ref.at[f, 0],
        ]
        copies = [
            pltpu.make_async_copy(source, matrix_ref.at[i], sems.at[i])
            for i, source in enumerate(sources)
        ]
        for copy in copies:
            copy.start()
        level = lax.broadcasted_iota(jnp.int32, shape, 0)

        def radius(positions):
            return inner_radius + shell_depth * (positions + 1).astype(jnp.float32) / (z.levels + 1)

        here = radius(level)
        scaled = (shell_depth / (z.levels + 1)) / here
        square_ref[...] = strength * (scaled * scaled)
        above_ref[...] = jnp.where(level == z.levels - 1, 0.0, strength * radius(level + 1) / here)
        below_ref[...] = jnp.where(level == 0, 0.0, strength * radius(level - 1) / here)
        for copy in copies:
            copy.wait()

    column = lax.broadcasted_iota(jnp.int32, shape, 1)
    for k in range(per_step):
        slot = step * per_step + k
        code = holder_ref[me * slots + slot]
        q = lax.div(code, OB)
        value = z.spacing * (q + 1) - 1
        rank = lax.rem(lax.div(start_ref[q], z.capacity), PLANE)
        which = jnp.where(q >= z.degrees // 2, rank ^ lax.rem(me, PLANE), PLANE)
        factor = (value * (value + 1)).astype(jnp.float32)
        limit = 2 * (value - lax.rem(code, OB) * (z.width // 2)) + 1
        u = columns_ref[:, k].reshape(shape).astype(jnp.float32)
        u = jnp.where(column <= limit, u, 0.0)
        weight = (1.0 - 2.0 * strength) - factor * square_ref[...]
        rhs = weight * u
        rhs += above_ref[...] * pltpu.roll(u, z.levels - 1, 0)
        rhs += below_ref[...] * pltpu.roll(u, 1, 0)
        high = rhs.astype(jnp.bfloat16)
        low = (rhs - high.astype(jnp.float32)).astype(jnp.bfloat16)
        both = jnp.concatenate([high, low], axis=1)
        product = jnp.dot(matrix_ref[which], both, preferred_element_type=jnp.float32)
        solved = product[:, : z.width] + product[:, z.width :]
        out_ref[:, k] = solved.astype(jnp.bfloat16).reshape(z.devices, z.local, z.width)


def solve(z, holder, degree_start, me, columns, inverses, pieces, f, slots):
    per_step = max(n for n in (1, 2, 3, 4) if slots % n == 0)
    block = (z.devices, per_step, z.local, z.width)
    spec = pl.BlockSpec(block, lambda i, *s: (0, i, 0, 0))
    chosen = [part for side in pieces for part in (*side[:3], side[3 + f])]
    return pl.pallas_call(
        functools.partial(solve_kernel, z, f, slots, per_step),
        grid_spec=pltpu.PrefetchScalarGridSpec(
            num_scalar_prefetch=3,
            grid=(slots // per_step,),
            in_specs=[spec] + [pl.BlockSpec(memory_space=pl.ANY)] * (1 + len(chosen)),
            out_specs=spec,
            scratch_shapes=[pltpu.VMEM((PLANE + 1, z.levels, z.levels), jnp.bfloat16)]
            + [pltpu.VMEM((z.levels, z.width), jnp.float32)] * 3
            + [pltpu.SemaphoreType.DMA((PLANE + 1,))],
        ),
        out_shape=jax.ShapeDtypeStruct(columns.shape, jnp.bfloat16),
        compiler_params=pltpu.CompilerParams(vmem_limit_bytes=48 << 20),
        cost_estimate=pl.CostEstimate(flops=10**10, bytes_accessed=10**7, transcendentals=0),
        name=f"solve_{f}",
    )(holder, degree_start, me, columns, inverses, *chosen)


def unpack_kernel(z, place_ref, returned_ref, *rest):
    grid_ref, slope_ref, sorted_ref = rest[-3:]
    rows = 16
    turn = transposer(z.local, rows)
    for b in range(z.blocks):
        sorted_ref[b] = returned_ref[place_ref[b]]

    def group(g, carry):
        at = pl.multiple_of(g * rows, rows)
        part = sorted_ref[pl.ds(at, rows)].reshape(rows * z.local, z.width)
        turned = jnp.dot(turn, part, preferred_element_type=jnp.float32)
        turned = turned.reshape(z.local, rows, z.width)
        grid_ref[0, :, pl.ds(at, rows), :] = turned.astype(jnp.bfloat16)
        slope = 0.5 * (turned[2:] - turned[:-2])
        slope_ref[0, pl.ds(1, z.local - 2), pl.ds(at, rows), :] = slope.astype(jnp.bfloat16)
        return carry

    lax.fori_loop(0, z.blocks // rows, group, 0, unroll=2)


def unpack(z, place, returned, f, earlier):
    shape = jax.ShapeDtypeStruct((z.fields, z.local, z.blocks, z.width), jnp.bfloat16)
    spec = pl.BlockSpec((1, z.local, z.blocks, z.width), lambda i, *s: (f, 0, 0, 0))
    return pl.pallas_call(
        functools.partial(unpack_kernel, z),
        grid_spec=pltpu.PrefetchScalarGridSpec(
            num_scalar_prefetch=1,
            grid=(1,),
            in_specs=[pl.BlockSpec(returned.shape, lambda i, *s: (0, 0, 0))]
            + [pl.BlockSpec(memory_space=pl.ANY)] * len(earlier),
            out_specs=[spec, spec],
            scratch_shapes=[pltpu.VMEM((z.blocks, z.local, z.width), jnp.bfloat16)],
        ),
        out_shape=[shape, shape],
        input_output_aliases={2 + i: i for i in range(len(earlier))},
        compiler_params=pltpu.CompilerParams(vmem_limit_bytes=48 << 20),
        cost_estimate=pl.CostEstimate(flops=10**9, bytes_accessed=10**7, transcendentals=0),
        name=f"unpack_{f}",
    )(place, returned, *earlier)


def edge_kernel(slope_in_ref, inside_ref, outside_ref, slope_ref):
    del slope_in_ref
    inside = inside_ref[...].astype(jnp.float32)
    outside = outside_ref[...].astype(jnp.float32).reshape(inside.shape)
    first = pl.program_id(0) == 0
    slope_ref[...] = jnp.where(first, 0.5 * (inside - outside), 0.5 * (outside - inside)).astype(
        jnp.bfloat16
    )


def edges(z, slope, grid, outside, f):
    last = z.local - 1
    block = (1, 1, z.blocks, z.width)
    return pl.pallas_call(
        edge_kernel,
        grid=(2,),
        in_specs=[
            pl.BlockSpec(memory_space=pl.ANY),
            pl.BlockSpec(block, lambda i: (f, 1 + i * (last - 2), 0, 0)),
            pl.BlockSpec((1, z.blocks, z.width), lambda i: (i, 0, 0)),
        ],
        out_specs=pl.BlockSpec(block, lambda i: (f, i * last, 0, 0)),
        out_shape=jax.ShapeDtypeStruct(slope.shape, slope.dtype),
        input_output_aliases={0: 0},
        name=f"edges_{f}",
    )(slope, grid, outside)


def beside(z, first, last):
    up = [(i, i + 1) for i in range(z.devices - 1)]
    down = [(j, i) for i, j in up]
    return lax.ppermute(last, AXES, up), lax.ppermute(first, AXES, down)


def exchange(z, value, slots):
    shaped = value.reshape(z.devices, slots, z.local, z.width)
    return lax.all_to_all(shaped, AXES, split_axis=0, concat_axis=0, tiled=True)


def body(grid_field, inverses, slot_blocks, degree_start):
    rad, lm = lax.axis_size("rad"), lax.axis_size("lm")
    z = Sizes(rad * lm, grid_field, inverses, slot_blocks)
    choices = slot_choices(z)
    kernels = z.local % 16 == 0 and z.blocks % 16 == 0 and rad % 2 == 0 and lm == PLANE // 2
    if not kernels or z.counts[z.degrees // 2 - 1] > choices[0]:
        return plain_body(z, grid_field, inverses, degree_start)
    me = lax.axis_index(AXES).reshape(1).astype(jnp.int32)
    choice, place, holder = plan(z, degree_start, choices)
    routes = [functools.partial(route, z, slots) for slots in choices]
    return lax.switch(choice[0], routes, grid_field, inverses, degree_start, me, place, holder)


def route(z, slots, grid_field, inverses, degree_start, me, place, holder):
    sent = [pack(z, place, grid_field, f, slots) for f in range(z.fields)]
    pieces = plane_inverses(inverses)
    columns = [exchange(z, sent[f], slots) for f in range(z.fields)]
    solved = [
        solve(z, holder, degree_start, me, columns[f], inverses, pieces, f, slots)
        for f in range(z.fields)
    ]
    returned = [
        exchange(z, solved[f], slots).reshape(z.devices * slots, z.local, z.width)
        for f in range(z.fields)
    ]
    outs = ()
    for f in range(z.fields):
        outs = tuple(unpack(z, place, returned[f], f, outs))
        grid, slope = outs
        before, after = beside(z, grid[f, :1], grid[f, -1:])
        outs = (grid, edges(z, slope, grid, jnp.concatenate([before, after]), f))
    return outs


def plain_body(z, grid_field, inverses, degree_start):
    index = np.arange(z.degrees)
    counts = np.asarray(z.counts)
    degree_of = np.repeat(index, counts)
    place_in = np.arange(z.blocks) - np.asarray(z.starts)[degree_of]
    value = z.spacing * (index + 1) - 1
    slot_place = degree_start[degree_of] + jnp.asarray(place_in, jnp.int32)
    total = z.devices * z.capacity
    holder = jnp.full((total,), z.blocks, jnp.int32)
    holder = holder.at[slot_place].set(jnp.arange(z.blocks, dtype=jnp.int32))
    sent = jnp.take(grid_field, holder, axis=2, mode="fill", fill_value=0)
    sent = sent.reshape(z.fields, z.local, z.devices, z.capacity, z.width)
    columns = lax.all_to_all(sent, AXES, split_axis=2, concat_axis=1, tiled=True)
    columns = columns.reshape(z.fields, z.levels, z.capacity, z.width)
    device = lax.axis_index(AXES)
    mine = lax.dynamic_slice_in_dim(holder, device * z.capacity, z.capacity)
    order = jnp.asarray(place_in)[:, None] * OB + np.arange(z.width)[None, :] // 2
    live_table = (order <= jnp.asarray(value[degree_of])[:, None]).astype(jnp.float32)
    live = jnp.take(live_table, mine, axis=0, mode="fill", fill_value=0)
    factor = (value * (value + 1)).astype(np.float32)[degree_of]
    factor = jnp.take(jnp.asarray(factor), mine, mode="fill", fill_value=0)
    upper = jnp.take(jnp.asarray(degree_of >= z.degrees // 2), mine, mode="fill", fill_value=False)
    radius = inner_radius + shell_depth * jnp.arange(z.levels + 2, dtype=jnp.float32) / (z.levels + 1)
    here = radius[1:-1][None, :, None, None]
    padded = jnp.pad(columns.astype(jnp.float32), ((0, 0), (1, 1), (0, 0), (0, 0)))
    weighted = padded * radius[None, :, None, None]
    second = (weighted[:, 2:] - 2.0 * weighted[:, 1:-1] + weighted[:, :-2]) / here
    scaled = (shell_depth / (z.levels + 1)) / here
    centre = padded[:, 1:-1]
    strength = jnp.asarray(diffusion_numbers, jnp.float32)[:, None, None, None]
    angular = factor[None, None, :, None] * (scaled * scaled) * centre
    rhs = (centre + strength * (second - angular)) * live[None, None]

    def solve_slot(carry, at):
        matrix = lax.dynamic_index_in_dim(
            inverses, upper[at].astype(jnp.int32), 1, keepdims=False
        ).astype(jnp.float32)
        block = lax.dynamic_index_in_dim(rhs, at, 2, keepdims=False)
        product = jnp.einsum("fij,fjc->fic", matrix, block, precision=lax.Precision.HIGHEST)
        return carry, product.astype(jnp.bfloat16)

    solved = lax.scan(solve_slot, 0, jnp.arange(z.capacity))[1]
    solved = jnp.moveaxis(solved, 0, 2)
    solved = solved.reshape(z.fields, z.devices, z.local, z.capacity, z.width)
    returned = lax.all_to_all(solved, AXES, split_axis=1, concat_axis=3, tiled=True)
    returned = returned.reshape(z.fields, z.local, total, z.width)
    grid = jnp.take(returned, slot_place, axis=2)
    before, after = beside(z, grid[:, :1], grid[:, -1:])
    rimmed = jnp.concatenate([before, grid, after], axis=1).astype(jnp.float32)
    return grid, (0.5 * (rimmed[:, 2:] - rimmed[:, :-2])).astype(jnp.bfloat16)


def solution(mesh):
    in_specs = (P(None, AXES), P(None, AXES), P(), P())
    out_specs = (P(None, AXES), P(None, AXES))
    return jax.shard_map(body, mesh=mesh, in_specs=in_specs, out_specs=out_specs, check_vma=False)
```

```python
import functools

import jax
import jax.numpy as jnp
import numpy as np
from jax import lax
from jax.experimental import pallas as pl
from jax.experimental.pallas import tpu as pltpu
from jax.sharding import PartitionSpec as P

LMAX1 = 1024
OB = 64
AXES = ("rad", "lm")
PLANE = 8
GROUP = 16

inner_radius = 0.35
shell_depth = 0.65
diffusion_numbers = (0.9, 0.4)


class Sizes:
    def __init__(self, devices, grid_field, inverses, slot_blocks):
        self.devices = devices
        self.fields, self.local, self.blocks, self.width = grid_field.shape
        self.levels = inverses.shape[-1]
        self.capacity = slot_blocks.shape[1]
        self.degrees = 2 * devices
        self.spacing = LMAX1 // self.degrees
        self.group_size = OB * self.degrees // LMAX1
        index = np.arange(self.degrees)
        self.counts = [int(c) for c in index // self.group_size + 1]
        self.starts = [int(s) for s in np.cumsum(self.counts) - self.counts]


def slot_choices(z):
    mean = -(-z.blocks // z.devices)
    return sorted({min(mean + extra, z.capacity) for extra in (1, 2, 3, 4)} | {z.capacity})


def plan_kernel(z, choices, start_ref, choice_ref, place_ref, load_ref, device_ref, next_ref):
    half = z.degrees // 2
    planes = z.devices // PLANE
    owner = [lax.div(start_ref[q], z.capacity) for q in range(z.degrees)]
    for q in range(half, z.degrees):
        load_ref[owner[q]] = start_ref[q] - owner[q] * z.capacity + z.counts[q]
    totals = [sum(load_ref[g * PLANE + e] for e in range(PLANE)) for g in range(planes)]
    most = functools.reduce(jnp.maximum, totals)
    choice = jnp.int32(0)
    slots = jnp.int32(choices[0])
    for i in range(1, len(choices)):
        beyond = most > PLANE * choices[i - 1]
        choice = jnp.where(beyond, i, choice)
        slots = jnp.where(beyond, choices[i], slots)
    choice_ref[0] = choice
    for g in range(planes):
        device_ref[g] = g * PLANE
        next_ref[g] = load_ref[g * PLANE]
    for q in range(z.degrees):
        first = start_ref[q] + owner[q] * (slots - z.capacity)
        for p in range(z.counts[q]):
            place_ref[z.starts[q] + p] = first + p
    for q in range(half, z.degrees):
        if z.counts[half - 1] + z.counts[q] <= choices[0]:
            continue
        plane = lax.div(owner[q], PLANE)
        room = slots - (start_ref[q] - owner[q] * z.capacity)

        def move(p, carry, plane=plane, q=q):
            def full(state):
                return state[1] >= slots

            def advance(state):
                return state[0] + 1, load_ref[state[0] + 1]

            holder, slot = lax.while_loop(full, advance, (device_ref[plane], next_ref[plane]))
            device_ref[plane] = holder
            next_ref[plane] = slot + 1
            place_ref[z.starts[q] + p] = holder * slots + slot
            return carry

        lax.fori_loop(jnp.minimum(room, z.counts[q]), z.counts[q], move, 0)


def plan(z, degree_start, choices):
    smem = pl.BlockSpec(memory_space=pltpu.SMEM)
    planes = z.devices // PLANE
    return pl.pallas_call(
        functools.partial(plan_kernel, z, choices),
        in_specs=[smem],
        out_specs=[smem] * 2,
        out_shape=[
            jax.ShapeDtypeStruct((1,), jnp.int32),
            jax.ShapeDtypeStruct((z.blocks,), jnp.int32),
        ],
        scratch_shapes=[
            pltpu.SMEM((z.devices,), jnp.int32),
            pltpu.SMEM((planes,), jnp.int32),
            pltpu.SMEM((planes,), jnp.int32),
        ],
        name="plan",
    )(degree_start)


def swap(value, axis, bit):
    size = lax.axis_size(axis)
    return lax.ppermute(value, axis, [(i, i ^ bit) for i in range(size)])


def straight_inverses(inverses):
    own = inverses[:, 1]
    return own, swap(own, "lm", 2), swap(own, "rad", 1)


def plane_inverses(own, across, along):
    corner = [swap(across[:1], "rad", 1), swap(along[1:], "lm", 2)]
    even = [own, across, along] + corner
    return even, [swap(value, "lm", 1) for value in even]


def pack_kernel(z, place_ref, field_ref, out_ref, *rest):
    wide_ref = rest[-1]
    pitch = z.blocks + 1
    for level in range(z.local):
        wide_ref[pl.ds(level * pitch, z.blocks), :] = field_ref[0, level].astype(jnp.float32)

    def group(g, carry):
        for k in range(GROUP):
            b = g * GROUP + k
            tile = wide_ref[pl.ds(b, z.local, stride=pitch), :]
            out_ref[place_ref[b]] = tile.astype(jnp.bfloat16)
        return carry

    lax.fori_loop(0, z.blocks // GROUP, group, 0)
    if len(rest) == 1:
        return
    holder_ref = rest[0]

    def clear(k, carry):
        holder_ref[k] = 0
        return carry

    lax.fori_loop(0, z.devices * z.capacity, clear, 0, unroll=8)

    def degree(q, b):
        def block(p, inner):
            holder_ref[place_ref[b + p]] = q * OB + p
            return inner

        count = lax.div(q, z.group_size) + 1
        lax.fori_loop(0, count, block, 0)
        return b + count

    lax.fori_loop(0, z.degrees, degree, 0)


def pack(z, place, grid_field, f, slots, with_holder):
    total = z.devices * slots
    out_specs = [pl.BlockSpec((total, z.local, z.width), lambda i, *s: (0, 0, 0))]
    out_shape = [jax.ShapeDtypeStruct((total, z.local, z.width), jnp.bfloat16)]
    if with_holder:
        out_specs.append(pl.BlockSpec(memory_space=pltpu.SMEM))
        out_shape.append(jax.ShapeDtypeStruct((z.devices * z.capacity,), jnp.int32))
    return pl.pallas_call(
        functools.partial(pack_kernel, z),
        grid_spec=pltpu.PrefetchScalarGridSpec(
            num_scalar_prefetch=1,
            grid=(1,),
            in_specs=[
                pl.BlockSpec((1, z.local, z.blocks, z.width), lambda i, *s: (f, 0, 0, 0))
            ],
            out_specs=out_specs,
            scratch_shapes=[pltpu.VMEM((z.local * (z.blocks + 1), z.width), jnp.float32)],
        ),
        out_shape=out_shape,
        compiler_params=pltpu.CompilerParams(vmem_limit_bytes=48 << 20),
        cost_estimate=pl.CostEstimate(flops=10**9, bytes_accessed=10**7, transcendentals=0),
        name=f"pack_{f}",
    )(place, grid_field)


def solve_kernel(z, f, slots, per_step, holder_ref, start_ref, me_ref, columns_ref, inverses_ref, *rest):
    (own, across, along, corner, own_odd, across_odd, along_odd, corner_odd) = rest[:8]
    out_ref, matrix_ref, square_ref, above_ref, below_ref, sems = rest[8:]
    strength = diffusion_numbers[f]
    step = pl.program_id(0)
    shape = (z.levels, z.width)
    me = me_ref[0]

    @pl.when(step == 0)
    def _():
        sources = [
            own.at[f], own_odd.at[f], across.at[f], across_odd.at[f],
            along.at[f], along_odd.at[f], corner.at[0], corner_odd.at[0],
            inverses_ref.at[f, 0],
        ]
        copies = [
            pltpu.make_async_copy(source, matrix_ref.at[i], sems.at[i])
            for i, source in enumerate(sources)
        ]
        for copy in copies:
            copy.start()
        level = lax.broadcasted_iota(jnp.int32, shape, 0)

        def radius(positions):
            return inner_radius + shell_depth * (positions + 1).astype(jnp.float32) / (z.levels + 1)

        here = radius(level)
        scaled = (shell_depth / (z.levels + 1)) / here
        square_ref[...] = strength * (scaled * scaled)
        above_ref[...] = jnp.where(level == z.levels - 1, 0.0, strength * radius(level + 1) / here)
        below_ref[...] = jnp.where(level == 0, 0.0, strength * radius(level - 1) / here)
        for copy in copies:
            copy.wait()

    column = lax.broadcasted_iota(jnp.int32, shape, 1)
    for k in range(per_step):
        slot = jnp.minimum(step * per_step + k, slots - 1)
        code = holder_ref[me * slots + slot]
        q = lax.div(code, OB)
        value = z.spacing * (q + 1) - 1
        rank = lax.rem(lax.div(start_ref[q], z.capacity), PLANE)
        which = jnp.where(q >= z.degrees // 2, rank ^ lax.rem(me, PLANE), PLANE)
        factor = (value * (value + 1)).astype(jnp.float32)
        limit = 2 * (value - lax.rem(code, OB) * (z.width // 2)) + 1
        u = columns_ref[:, k].reshape(shape).astype(jnp.float32)
        u = jnp.where(column <= limit, u, 0.0)
        weight = (1.0 - 2.0 * strength) - factor * square_ref[...]
        rhs = weight * u
        rhs += above_ref[...] * pltpu.roll(u, z.levels - 1, 0)
        rhs += below_ref[...] * pltpu.roll(u, 1, 0)
        high = rhs.astype(jnp.bfloat16)
        low = (rhs - high.astype(jnp.float32)).astype(jnp.bfloat16)
        both = jnp.concatenate([high, low], axis=1)
        product = jnp.dot(matrix_ref[which], both, preferred_element_type=jnp.float32)
        solved = product[:, : z.width] + product[:, z.width :]
        out_ref[:, k] = solved.astype(jnp.bfloat16).reshape(z.devices, z.local, z.width)


def solve(z, holder, degree_start, me, columns, inverses, pieces, f, slots):
    steps = pl.cdiv(slots, 5)
    per_step = pl.cdiv(slots, steps)
    block = (z.devices, per_step, z.local, z.width)
    spec = pl.BlockSpec(block, lambda i, *s: (0, i, 0, 0))
    chosen = [part for side in pieces for part in (*side[:3], side[3 + f])]
    return pl.pallas_call(
        functools.partial(solve_kernel, z, f, slots, per_step),
        grid_spec=pltpu.PrefetchScalarGridSpec(
            num_scalar_prefetch=3,
            grid=(steps,),
            in_specs=[spec] + [pl.BlockSpec(memory_space=pl.ANY)] * (1 + len(chosen)),
            out_specs=spec,
            scratch_shapes=[pltpu.VMEM((PLANE + 1, z.levels, z.levels), jnp.bfloat16)]
            + [pltpu.VMEM((z.levels, z.width), jnp.float32)] * 3
            + [pltpu.SemaphoreType.DMA((PLANE + 1,))],
        ),
        out_shape=jax.ShapeDtypeStruct(columns.shape, jnp.bfloat16),
        compiler_params=pltpu.CompilerParams(vmem_limit_bytes=48 << 20),
        cost_estimate=pl.CostEstimate(flops=10**10, bytes_accessed=10**7, transcendentals=0),
        name=f"solve_{f}",
    )(holder, degree_start, me, columns, inverses, *chosen)


def unpack_kernel(z, place_ref, returned_ref, *rest):
    grid_ref, slope_ref, first_ref, last_ref, wide_ref = rest[-5:]
    pitch = z.blocks + 1

    def gather(g, carry):
        for k in range(GROUP):
            b = g * GROUP + k
            tile = returned_ref[place_ref[b]].astype(jnp.float32)
            wide_ref[pl.ds(b, z.local, stride=pitch), :] = tile
        return carry

    lax.fori_loop(0, z.blocks // GROUP, gather, 0)

    def group(g, carry):
        at = pl.multiple_of(g * GROUP, GROUP)
        rows = pl.ds(at, GROUP)
        value = [wide_ref[pl.ds(at + i * pitch, GROUP), :] for i in range(z.local)]
        for i in range(z.local):
            grid_ref[0, i, rows, :] = value[i].astype(jnp.bfloat16)
        for i in range(1, z.local - 1):
            slope = 0.5 * (value[i + 1] - value[i - 1])
            slope_ref[0, i, rows, :] = slope.astype(jnp.bfloat16)
        first_ref[0, rows, :] = value[0].astype(jnp.bfloat16)
        last_ref[0, rows, :] = value[-1].astype(jnp.bfloat16)
        return carry

    lax.fori_loop(0, z.blocks // GROUP, group, 0, unroll=2)


def unpack(z, place, returned, f, earlier):
    whole = jax.ShapeDtypeStruct((z.fields, z.local, z.blocks, z.width), jnp.bfloat16)
    level = jax.ShapeDtypeStruct((1, z.blocks, z.width), jnp.bfloat16)
    spec = pl.BlockSpec((1, z.local, z.blocks, z.width), lambda i, *s: (f, 0, 0, 0))
    level_spec = pl.BlockSpec(level.shape, lambda i, *s: (0, 0, 0))
    return pl.pallas_call(
        functools.partial(unpack_kernel, z),
        grid_spec=pltpu.PrefetchScalarGridSpec(
            num_scalar_prefetch=1,
            grid=(1,),
            in_specs=[pl.BlockSpec(returned.shape, lambda i, *s: (0, 0, 0))]
            + [pl.BlockSpec(memory_space=pl.ANY)] * len(earlier),
            out_specs=[spec, spec, level_spec, level_spec],
            scratch_shapes=[pltpu.VMEM((z.local * (z.blocks + 1), z.width), jnp.float32)],
        ),
        out_shape=[whole, whole, level, level],
        input_output_aliases={2 + i: i for i in range(len(earlier))},
        compiler_params=pltpu.CompilerParams(vmem_limit_bytes=48 << 20),
        cost_estimate=pl.CostEstimate(flops=10**9, bytes_accessed=10**7, transcendentals=0),
        name=f"unpack_{f}",
    )(place, returned, *earlier)


def edge_kernel(z, f, second_ref, before_last_ref, before_ref, after_ref, slope_in_ref, slope_ref,
                edge_ref, sems):
    del slope_in_ref

    def wide(ref):
        return ref[...].reshape(z.blocks, z.width).astype(jnp.float32)

    slopes = [wide(second_ref) - wide(before_ref), wide(after_ref) - wide(before_last_ref)]
    copies = []
    for i, level in enumerate((0, z.local - 1)):
        edge_ref[i] = (0.5 * slopes[i]).astype(jnp.bfloat16)
        copies.append(pltpu.make_async_copy(edge_ref.at[i], slope_ref.at[f, level], sems.at[i]))
        copies[i].start()
    for copy in copies:
        copy.wait()


def edges(z, slope, grid, before, after, f):
    block = (1, 1, z.blocks, z.width)
    beside_spec = pl.BlockSpec((1, z.blocks, z.width), lambda i: (0, 0, 0))
    return pl.pallas_call(
        functools.partial(edge_kernel, z, f),
        grid=(1,),
        in_specs=[
            pl.BlockSpec(block, lambda i: (f, 1, 0, 0)),
            pl.BlockSpec(block, lambda i: (f, z.local - 2, 0, 0)),
            beside_spec,
            beside_spec,
            pl.BlockSpec(memory_space=pl.ANY),
        ],
        out_specs=pl.BlockSpec(memory_space=pl.ANY),
        out_shape=jax.ShapeDtypeStruct(slope.shape, slope.dtype),
        scratch_shapes=[
            pltpu.VMEM((2, z.blocks, z.width), jnp.bfloat16),
            pltpu.SemaphoreType.DMA((2,)),
        ],
        input_output_aliases={4: 0},
        name=f"edges_{f}",
    )(grid, grid, before, after, slope)


def beside(z, first, last):
    up = [(i, i + 1) for i in range(z.devices - 1)]
    down = [(j, i) for i, j in up]
    return lax.ppermute(last, AXES, up), lax.ppermute(first, AXES, down)


def exchange(z, value, slots):
    shaped = value.reshape(z.devices, slots, z.local, z.width)
    return lax.all_to_all(shaped, AXES, split_axis=0, concat_axis=0, tiled=True)


def body(grid_field, inverses, slot_blocks, degree_start):
    rad, lm = lax.axis_size("rad"), lax.axis_size("lm")
    z = Sizes(rad * lm, grid_field, inverses, slot_blocks)
    choices = slot_choices(z)
    kernels = z.local % 16 == 0 and z.blocks % GROUP == 0 and rad % 2 == 0 and lm == PLANE // 2
    if not kernels or z.counts[z.degrees // 2 - 1] > choices[0]:
        return plain_body(z, grid_field, inverses, degree_start)
    me = lax.axis_index(AXES).reshape(1).astype(jnp.int32)
    choice, place = plan(z, degree_start, choices)
    routes = [functools.partial(route, z, slots) for slots in choices]
    return lax.switch(choice[0], routes, grid_field, inverses, degree_start, me, place)


def route(z, slots, grid_field, inverses, degree_start, me, place):
    (sent_0,) = pack(z, place, grid_field, 0, slots, False)
    sent_1, holder = pack(z, place, grid_field, 1, slots, True)
    straight = lax.optimization_barrier((sent_1, *straight_inverses(inverses)))
    columns = [exchange(z, sent, slots) for sent in (sent_0, straight[0])]
    pieces = lax.optimization_barrier(plane_inverses(*straight[1:]))
    solved = [
        solve(z, holder, degree_start, me, columns[f], inverses, pieces, f, slots)
        for f in range(z.fields)
    ]
    returned = [
        exchange(z, solved[f], slots).reshape(z.devices * slots, z.local, z.width)
        for f in range(z.fields)
    ]
    outs = ()
    for f in range(z.fields):
        grid, slope, first, last = unpack(z, place, returned[f], f, outs)
        outs = (grid, edges(z, slope, grid, *beside(z, first, last), f))
    return outs


def plain_body(z, grid_field, inverses, degree_start):
    index = np.arange(z.degrees)
    counts = np.asarray(z.counts)
    degree_of = np.repeat(index, counts)
    place_in = np.arange(z.blocks) - np.asarray(z.starts)[degree_of]
    value = z.spacing * (index + 1) - 1
    slot_place = degree_start[degree_of] + jnp.asarray(place_in, jnp.int32)
    total = z.devices * z.capacity
    holder = jnp.full((total,), z.blocks, jnp.int32)
    holder = holder.at[slot_place].set(jnp.arange(z.blocks, dtype=jnp.int32))
    sent = jnp.take(grid_field, holder, axis=2, mode="fill", fill_value=0)
    sent = sent.reshape(z.fields, z.local, z.devices, z.capacity, z.width)
    columns = lax.all_to_all(sent, AXES, split_axis=2, concat_axis=1, tiled=True)
    columns = columns.reshape(z.fields, z.levels, z.capacity, z.width)
    device = lax.axis_index(AXES)
    mine = lax.dynamic_slice_in_dim(holder, device * z.capacity, z.capacity)
    order = jnp.asarray(place_in)[:, None] * OB + np.arange(z.width)[None, :] // 2
    live_table = (order <= jnp.asarray(value[degree_of])[:, None]).astype(jnp.float32)
    live = jnp.take(live_table, mine, axis=0, mode="fill", fill_value=0)
    factor = (value * (value + 1)).astype(np.float32)[degree_of]
    factor = jnp.take(jnp.asarray(factor), mine, mode="fill", fill_value=0)
    upper = jnp.take(jnp.asarray(degree_of >= z.degrees // 2), mine, mode="fill", fill_value=False)
    radius = inner_radius + shell_depth * jnp.arange(z.levels + 2, dtype=jnp.float32) / (z.levels + 1)
    here = radius[1:-1][None, :, None, None]
    padded = jnp.pad(columns.astype(jnp.float32), ((0, 0), (1, 1), (0, 0), (0, 0)))
    weighted = padded * radius[None, :, None, None]
    second = (weighted[:, 2:] - 2.0 * weighted[:, 1:-1] + weighted[:, :-2]) / here
    scaled = (shell_depth / (z.levels + 1)) / here
    centre = padded[:, 1:-1]
    strength = jnp.asarray(diffusion_numbers, jnp.float32)[:, None, None, None]
    angular = factor[None, None, :, None] * (scaled * scaled) * centre
    rhs = (centre + strength * (second - angular)) * live[None, None]

    def solve_slot(carry, at):
        matrix = lax.dynamic_index_in_dim(
            inverses, upper[at].astype(jnp.int32), 1, keepdims=False
        ).astype(jnp.float32)
        block = lax.dynamic_index_in_dim(rhs, at, 2, keepdims=False)
        product = jnp.einsum("fij,fjc->fic", matrix, block, precision=lax.Precision.HIGHEST)
        return carry, product.astype(jnp.bfloat16)

    solved = lax.scan(solve_slot, 0, jnp.arange(z.capacity))[1]
    solved = jnp.moveaxis(solved, 0, 2)
    solved = solved.reshape(z.fields, z.devices, z.local, z.capacity, z.width)
    returned = lax.all_to_all(solved, AXES, split_axis=1, concat_axis=3, tiled=True)
    returned = returned.reshape(z.fields, z.local, total, z.width)
    grid = jnp.take(returned, slot_place, axis=2)
    before, after = beside(z, grid[:, :1], grid[:, -1:])
    rimmed = jnp.concatenate([before, grid, after], axis=1).astype(jnp.float32)
    return grid, (0.5 * (rimmed[:, 2:] - rimmed[:, :-2])).astype(jnp.bfloat16)


def solution(mesh):
    in_specs = (P(None, AXES), P(None, AXES), P(), P())
    out_specs = (P(None, AXES), P(None, AXES))
    return jax.shard_map(body, mesh=mesh, in_specs=in_specs, out_specs=out_specs, check_vma=False)
```

```python
import functools

import jax
import jax.numpy as jnp
import numpy as np
from jax import lax
from jax.experimental import pallas as pl
from jax.experimental.pallas import tpu as pltpu
from jax.sharding import PartitionSpec as P

LMAX1 = 1024
OB = 64
AXES = ("rad", "lm")
PLANE = 8
GIFT = 8
GROUP = 16
VMEM = 48 << 20

inner_radius = 0.35
shell_depth = 0.65
diffusion_numbers = (0.9, 0.4)


class Sizes:
    def __init__(self, devices, grid_field, inverses, slot_blocks):
        self.devices = devices
        self.fields, self.local, self.blocks, self.width = grid_field.shape
        self.levels = inverses.shape[-1]
        self.capacity = slot_blocks.shape[1]
        self.degrees = 2 * devices
        self.spacing = LMAX1 // self.degrees
        self.group_size = OB * self.degrees // LMAX1
        index = np.arange(self.degrees)
        self.counts = [int(c) for c in index // self.group_size + 1]
        self.starts = [int(s) for s in np.cumsum(self.counts) - self.counts]


def slot_choices(z):
    mean = -(-z.blocks // z.devices)
    return sorted({min(mean + extra, z.capacity) for extra in (0, 1, 2, 3)} | {z.capacity})


def plan_kernel(z, choices, start_ref, choice_ref, place_ref, load_ref, room_ref, device_ref, next_ref):
    half = z.degrees // 2
    planes = z.devices // PLANE
    owner = [lax.div(start_ref[q], z.capacity) for q in range(z.degrees)]
    for q in range(half, z.degrees):
        load_ref[owner[q]] = start_ref[q] - owner[q] * z.capacity + z.counts[q]
    loads = [load_ref[d] for d in range(z.devices)]
    totals = [sum(loads[g * PLANE : (g + 1) * PLANE]) for g in range(planes)]
    most = functools.reduce(jnp.maximum, [totals[g] + totals[g + 1] for g in range(0, planes, 2)])
    choice = jnp.int32(0)
    slots = jnp.int32(choices[0])
    highest = functools.reduce(jnp.maximum, totals)
    for i in range(1, len(choices)):
        tried = choices[i - 1]
        beyond = (most > 2 * PLANE * tried) | (highest > PLANE * tried + GIFT * PLANE // 2)
        choice = jnp.where(beyond, i, choice)
        slots = jnp.where(beyond, choices[i], slots)
    choice_ref[0] = choice
    for d in range(z.devices):
        excess = totals[d // PLANE] - PLANE * slots - GIFT * (d % PLANE // 2)
        gift = jnp.int32(0) if d % 2 else jnp.clip(excess, 0, GIFT)
        load_ref[d] = loads[d] - gift
        room_ref[d ^ PLANE] = slots - gift
    for g in range(planes):
        device_ref[g] = g * PLANE
        next_ref[g] = load_ref[g * PLANE]
    for q in range(z.degrees):
        first = start_ref[q] + owner[q] * (slots - z.capacity)
        for p in range(z.counts[q]):
            place_ref[z.starts[q] + p] = first + p
    for q in range(half, z.degrees):
        plane = lax.div(owner[q], PLANE)
        offset = start_ref[q] - owner[q] * z.capacity
        kept = load_ref[owner[q]] - offset

        def move(p, carry, plane=plane, q=q):
            def full(state):
                return state[1] >= room_ref[state[0]]

            def advance(state):
                return state[0] + 1, load_ref[state[0] + 1]

            holder, slot = lax.while_loop(full, advance, (device_ref[plane], next_ref[plane]))
            device_ref[plane] = holder
            next_ref[plane] = slot + 1
            place_ref[z.starts[q] + p] = holder * slots + slot
            return carry

        lax.fori_loop(jnp.minimum(room_ref[owner[q]] - offset, kept), kept, move, 0)
        other = owner[q] ^ PLANE
        given = other * slots + room_ref[other] - kept

        def give(p, carry, given=given, q=q):
            place_ref[z.starts[q] + p] = given + p
            return carry

        lax.fori_loop(kept, z.counts[q], give, 0)


def plan(z, degree_start, choices):
    smem = pl.BlockSpec(memory_space=pltpu.SMEM)
    planes = z.devices // PLANE
    return pl.pallas_call(
        functools.partial(plan_kernel, z, choices),
        in_specs=[smem],
        out_specs=[smem] * 2,
        out_shape=[
            jax.ShapeDtypeStruct((1,), jnp.int32),
            jax.ShapeDtypeStruct((z.blocks,), jnp.int32),
        ],
        scratch_shapes=[
            pltpu.SMEM((z.devices,), jnp.int32),
            pltpu.SMEM((z.devices,), jnp.int32),
            pltpu.SMEM((planes,), jnp.int32),
            pltpu.SMEM((planes,), jnp.int32),
        ],
        name="plan",
    )(degree_start)


def swap(value, axis, bit):
    size = lax.axis_size(axis)
    return lax.ppermute(value, axis, [(i, i ^ bit) for i in range(size)])


def straight_inverses(inverses):
    own = inverses[:, 1]
    rad, lm = lax.axis_size("rad"), lax.axis_size("lm")
    facing = [(d, d ^ PLANE) for d in range(0, rad * lm, 2)]
    return own, swap(own, "lm", 2), swap(own, "rad", 1), lax.ppermute(own, AXES, facing)


def other_core(values):
    return [swap(value, "lm", 1) for value in values]


def pack_kernel(z, place_ref, field_ref, out_ref, *rest):
    wide_ref = rest[-1]
    pitch = z.blocks + 1
    for level in range(z.local):
        wide_ref[pl.ds(level * pitch, z.blocks), :] = field_ref[0, level].astype(jnp.float32)

    def group(g, carry):
        for k in range(GROUP):
            b = g * GROUP + k
            tile = wide_ref[pl.ds(b, z.local, stride=pitch), :]
            out_ref[place_ref[b]] = tile.astype(jnp.bfloat16)
        return carry

    lax.fori_loop(0, z.blocks // GROUP, group, 0)
    if len(rest) == 1:
        return
    holder_ref = rest[0]

    def clear(k, carry):
        holder_ref[k] = 0
        return carry

    lax.fori_loop(0, z.devices * z.capacity, clear, 0, unroll=8)

    def degree(q, b):
        def block(p, inner):
            holder_ref[place_ref[b + p]] = q * OB + p
            return inner

        count = lax.div(q, z.group_size) + 1
        lax.fori_loop(0, count, block, 0)
        return b + count

    lax.fori_loop(0, z.degrees, degree, 0)


def pack(z, place, grid_field, f, slots, with_holder):
    total = z.devices * slots
    out_specs = [pl.BlockSpec((total, z.local, z.width), lambda i, *s: (0, 0, 0))]
    out_shape = [jax.ShapeDtypeStruct((total, z.local, z.width), jnp.bfloat16)]
    if with_holder:
        out_specs.append(pl.BlockSpec(memory_space=pltpu.SMEM))
        out_shape.append(jax.ShapeDtypeStruct((z.devices * z.capacity,), jnp.int32))
    return pl.pallas_call(
        functools.partial(pack_kernel, z),
        grid_spec=pltpu.PrefetchScalarGridSpec(
            num_scalar_prefetch=1,
            grid=(1,),
            in_specs=[
                pl.BlockSpec((1, z.local, z.blocks, z.width), lambda i, *s: (f, 0, 0, 0))
            ],
            out_specs=out_specs,
            scratch_shapes=[pltpu.VMEM((z.local * (z.blocks + 1), z.width), jnp.float32)],
        ),
        out_shape=out_shape,
        compiler_params=pltpu.CompilerParams(vmem_limit_bytes=VMEM),
        cost_estimate=pl.CostEstimate(flops=10**9, bytes_accessed=10**7, transcendentals=0),
        name=f"pack_{f}",
    )(place, grid_field)


def solve_kernel(z, f, slots, per_step, holder_ref, start_ref, me_ref, columns_ref, inverses_ref, *rest):
    (own, across, along, corner, own_odd, across_odd, along_odd, corner_odd, far) = rest[:9]
    out_ref, matrix_ref, square_ref, above_ref, below_ref, sems = rest[9:]
    strength = diffusion_numbers[f]
    step = pl.program_id(0)
    shape = (z.levels, z.width)
    me = me_ref[0]

    @pl.when(step == 0)
    def _():
        sources = [
            own.at[f], own_odd.at[f], across.at[f], across_odd.at[f],
            along.at[f], along_odd.at[f], corner.at[0], corner_odd.at[0],
            inverses_ref.at[f, 0], far.at[f],
        ]
        copies = [
            pltpu.make_async_copy(source, matrix_ref.at[i], sems.at[i])
            for i, source in enumerate(sources)
        ]
        for copy in copies:
            copy.start()
        level = lax.broadcasted_iota(jnp.int32, shape, 0)

        def radius(positions):
            return inner_radius + shell_depth * (positions + 1).astype(jnp.float32) / (z.levels + 1)

        here = radius(level)
        scaled = (shell_depth / (z.levels + 1)) / here
        square_ref[...] = strength * (scaled * scaled)
        above_ref[...] = jnp.where(level == z.levels - 1, 0.0, strength * radius(level + 1) / here)
        below_ref[...] = jnp.where(level == 0, 0.0, strength * radius(level - 1) / here)
        for copy in copies:
            copy.wait()

    column = lax.broadcasted_iota(jnp.int32, shape, 1)
    for k in range(per_step):
        slot = jnp.minimum(step * per_step + k, slots - 1)
        code = holder_ref[me * slots + slot]
        q = lax.div(code, OB)
        value = z.spacing * (q + 1) - 1
        offset = lax.div(start_ref[q], z.capacity) ^ me
        which = jnp.where(offset < PLANE, offset, PLANE + 1)
        which = jnp.where(q >= z.degrees // 2, which, PLANE)
        factor = (value * (value + 1)).astype(jnp.float32)
        limit = 2 * (value - lax.rem(code, OB) * (z.width // 2)) + 1
        u = columns_ref[:, k].reshape(shape).astype(jnp.float32)
        u = jnp.where(column <= limit, u, 0.0)
        weight = (1.0 - 2.0 * strength) - factor * square_ref[...]
        rhs = weight * u
        rhs += above_ref[...] * pltpu.roll(u, z.levels - 1, 0)
        rhs += below_ref[...] * pltpu.roll(u, 1, 0)
        high = rhs.astype(jnp.bfloat16)
        low = (rhs - high.astype(jnp.float32)).astype(jnp.bfloat16)
        both = jnp.concatenate([high, low], axis=1)
        product = jnp.dot(matrix_ref[which], both, preferred_element_type=jnp.float32)
        solved = product[:, : z.width] + product[:, z.width :]
        out_ref[:, k] = solved.astype(jnp.bfloat16).reshape(z.devices, z.local, z.width)


def solve(z, holder, degree_start, me, columns, inverses, pieces, f, slots):
    steps = pl.cdiv(slots, 5)
    per_step = pl.cdiv(slots, steps)
    block = (z.devices, per_step, z.local, z.width)
    spec = pl.BlockSpec(block, lambda i, *s: (0, i, 0, 0))
    return pl.pallas_call(
        functools.partial(solve_kernel, z, f, slots, per_step),
        grid_spec=pltpu.PrefetchScalarGridSpec(
            num_scalar_prefetch=3,
            grid=(steps,),
            in_specs=[spec] + [pl.BlockSpec(memory_space=pl.ANY)] * (1 + len(pieces)),
            out_specs=spec,
            scratch_shapes=[pltpu.VMEM((PLANE + 2, z.levels, z.levels), jnp.bfloat16)]
            + [pltpu.VMEM((z.levels, z.width), jnp.float32)] * 3
            + [pltpu.SemaphoreType.DMA((PLANE + 2,))],
        ),
        out_shape=jax.ShapeDtypeStruct(columns.shape, jnp.bfloat16),
        compiler_params=pltpu.CompilerParams(vmem_limit_bytes=VMEM),
        cost_estimate=pl.CostEstimate(flops=10**10, bytes_accessed=10**7, transcendentals=0),
        name=f"solve_{f}",
    )(holder, degree_start, me, columns, inverses, *pieces)


def unpack_kernel(z, place_ref, returned_ref, *rest):
    grid_ref, slope_ref, first_ref, last_ref, wide_ref = rest[-5:]
    pitch = z.blocks + 1

    def gather(g, carry):
        for k in range(GROUP):
            b = g * GROUP + k
            tile = returned_ref[place_ref[b]].astype(jnp.float32)
            wide_ref[pl.ds(b, z.local, stride=pitch), :] = tile
        return carry

    lax.fori_loop(0, z.blocks // GROUP, gather, 0)

    def group(g, carry):
        at = pl.multiple_of(g * GROUP, GROUP)
        rows = pl.ds(at, GROUP)
        value = [wide_ref[pl.ds(at + i * pitch, GROUP), :] for i in range(z.local)]
        for i in range(z.local):
            grid_ref[0, i, rows, :] = value[i].astype(jnp.bfloat16)
        for i in range(1, z.local - 1):
            slope = 0.5 * (value[i + 1] - value[i - 1])
            slope_ref[0, i, rows, :] = slope.astype(jnp.bfloat16)
        first_ref[0, rows, :] = value[0].astype(jnp.bfloat16)
        last_ref[0, rows, :] = value[-1].astype(jnp.bfloat16)
        return carry

    lax.fori_loop(0, z.blocks // GROUP, group, 0, unroll=2)


def unpack(z, place, returned, f, earlier):
    whole = jax.ShapeDtypeStruct((z.fields, z.local, z.blocks, z.width), jnp.bfloat16)
    level = jax.ShapeDtypeStruct((1, z.blocks, z.width), jnp.bfloat16)
    spec = pl.BlockSpec((1, z.local, z.blocks, z.width), lambda i, *s: (f, 0, 0, 0))
    level_spec = pl.BlockSpec(level.shape, lambda i, *s: (0, 0, 0))
    return pl.pallas_call(
        functools.partial(unpack_kernel, z),
        grid_spec=pltpu.PrefetchScalarGridSpec(
            num_scalar_prefetch=1,
            grid=(1,),
            in_specs=[pl.BlockSpec(returned.shape, lambda i, *s: (0, 0, 0))]
            + [pl.BlockSpec(memory_space=pl.ANY)] * len(earlier),
            out_specs=[spec, spec, level_spec, level_spec],
            scratch_shapes=[pltpu.VMEM((z.local * (z.blocks + 1), z.width), jnp.float32)],
        ),
        out_shape=[whole, whole, level, level],
        input_output_aliases={2 + i: i for i in range(len(earlier))},
        compiler_params=pltpu.CompilerParams(vmem_limit_bytes=VMEM if earlier else 60 << 20),
        cost_estimate=pl.CostEstimate(flops=10**9, bytes_accessed=10**7, transcendentals=0),
        name=f"unpack_{f}",
    )(place, returned, *earlier)


def edge_kernel(z, f, second_ref, before_last_ref, before_ref, after_ref, slope_in_ref, slope_ref,
                edge_ref, sems):
    del slope_in_ref

    def wide(ref):
        return ref[...].reshape(z.blocks, z.width).astype(jnp.float32)

    slopes = [wide(second_ref) - wide(before_ref), wide(after_ref) - wide(before_last_ref)]
    copies = []
    for i, level in enumerate((0, z.local - 1)):
        edge_ref[i] = (0.5 * slopes[i]).astype(jnp.bfloat16)
        copies.append(pltpu.make_async_copy(edge_ref.at[i], slope_ref.at[f, level], sems.at[i]))
        copies[i].start()
    for copy in copies:
        copy.wait()


def edges(z, slope, grid, before, after, f):
    block = (1, 1, z.blocks, z.width)
    beside_spec = pl.BlockSpec((1, z.blocks, z.width), lambda i: (0, 0, 0))
    return pl.pallas_call(
        functools.partial(edge_kernel, z, f),
        grid=(1,),
        in_specs=[
            pl.BlockSpec(block, lambda i: (f, 1, 0, 0)),
            pl.BlockSpec(block, lambda i: (f, z.local - 2, 0, 0)),
            beside_spec,
            beside_spec,
            pl.BlockSpec(memory_space=pl.ANY),
        ],
        out_specs=pl.BlockSpec(memory_space=pl.ANY),
        out_shape=jax.ShapeDtypeStruct(slope.shape, slope.dtype),
        scratch_shapes=[
            pltpu.VMEM((2, z.blocks, z.width), jnp.bfloat16),
            pltpu.SemaphoreType.DMA((2,)),
        ],
        input_output_aliases={4: 0},
        compiler_params=pltpu.CompilerParams(vmem_limit_bytes=VMEM),
        name=f"edges_{f}",
    )(grid, grid, before, after, slope)


def beside(z, first, last):
    up = [(i, i + 1) for i in range(z.devices - 1)]
    down = [(j, i) for i, j in up]
    return lax.ppermute(last, AXES, up), lax.ppermute(first, AXES, down)


def exchange(z, value, slots):
    shaped = value.reshape(z.devices, slots, z.local, z.width)
    return lax.all_to_all(shaped, AXES, split_axis=0, concat_axis=0, tiled=True)


def body(grid_field, inverses, slot_blocks, degree_start):
    rad, lm = lax.axis_size("rad"), lax.axis_size("lm")
    z = Sizes(rad * lm, grid_field, inverses, slot_blocks)
    choices = slot_choices(z)
    kernels = z.local % 16 == 0 and z.blocks % GROUP == 0 and rad % 4 == 0 and lm == PLANE // 2
    low, high = z.counts[z.degrees // 2 - 1 : z.degrees // 2 + 1]
    if not kernels or low + GIFT > choices[0] or high < GIFT or z.capacity - choices[0] > GIFT:
        return plain_body(z, grid_field, inverses, degree_start)
    me = lax.axis_index(AXES).reshape(1).astype(jnp.int32)
    choice, place = plan(z, degree_start, choices)
    routes = [functools.partial(route, z, slots) for slots in choices]
    return lax.switch(choice[0], routes, grid_field, inverses, degree_start, me, place)


def route(z, slots, grid_field, inverses, degree_start, me, place):
    (sent_0,) = pack(z, place, grid_field, 0, slots, False)
    sent_1, holder = pack(z, place, grid_field, 1, slots, True)
    sent_1, own, across, along, far = lax.optimization_barrier(
        (sent_1, *straight_inverses(inverses))
    )
    columns = [exchange(z, sent, slots) for sent in (sent_0, sent_1)]
    corner_0 = swap(across[:1], "rad", 1)
    even = [own, across, along]
    odd = other_core(even)
    pieces = lax.optimization_barrier((*even, corner_0, *odd, *other_core([corner_0]), far))
    solved_0 = solve(z, holder, degree_start, me, columns[0], inverses, pieces, 0, slots)
    corner_1 = swap(along[1:], "lm", 2)
    pieces = (*even, corner_1, *odd, *other_core([corner_1]), far)
    solved_1 = solve(z, holder, degree_start, me, columns[1], inverses, pieces, 1, slots)
    solved = [solved_0, solved_1]
    returned = [
        exchange(z, solved[f], slots).reshape(z.devices * slots, z.local, z.width)
        for f in range(z.fields)
    ]
    outs = ()
    for f in range(z.fields):
        grid, slope, first, last = unpack(z, place, returned[f], f, outs)
        outs = (grid, edges(z, slope, grid, *beside(z, first, last), f))
    return outs


def plain_body(z, grid_field, inverses, degree_start):
    index = np.arange(z.degrees)
    counts = np.asarray(z.counts)
    degree_of = np.repeat(index, counts)
    place_in = np.arange(z.blocks) - np.asarray(z.starts)[degree_of]
    value = z.spacing * (index + 1) - 1
    slot_place = degree_start[degree_of] + jnp.asarray(place_in, jnp.int32)
    total = z.devices * z.capacity
    holder = jnp.full((total,), z.blocks, jnp.int32)
    holder = holder.at[slot_place].set(jnp.arange(z.blocks, dtype=jnp.int32))
    sent = jnp.take(grid_field, holder, axis=2, mode="fill", fill_value=0)
    sent = sent.reshape(z.fields, z.local, z.devices, z.capacity, z.width)
    columns = lax.all_to_all(sent, AXES, split_axis=2, concat_axis=1, tiled=True)
    columns = columns.reshape(z.fields, z.levels, z.capacity, z.width)
    device = lax.axis_index(AXES)
    mine = lax.dynamic_slice_in_dim(holder, device * z.capacity, z.capacity)
    order = jnp.asarray(place_in)[:, None] * OB + np.arange(z.width)[None, :] // 2
    live_table = (order <= jnp.asarray(value[degree_of])[:, None]).astype(jnp.float32)
    live = jnp.take(live_table, mine, axis=0, mode="fill", fill_value=0)
    factor = (value * (value + 1)).astype(np.float32)[degree_of]
    factor = jnp.take(jnp.asarray(factor), mine, mode="fill", fill_value=0)
    upper = jnp.take(jnp.asarray(degree_of >= z.degrees // 2), mine, mode="fill", fill_value=False)
    radius = inner_radius + shell_depth * jnp.arange(z.levels + 2, dtype=jnp.float32) / (z.levels + 1)
    here = radius[1:-1][None, :, None, None]
    padded = jnp.pad(columns.astype(jnp.float32), ((0, 0), (1, 1), (0, 0), (0, 0)))
    weighted = padded * radius[None, :, None, None]
    second = (weighted[:, 2:] - 2.0 * weighted[:, 1:-1] + weighted[:, :-2]) / here
    scaled = (shell_depth / (z.levels + 1)) / here
    centre = padded[:, 1:-1]
    strength = jnp.asarray(diffusion_numbers, jnp.float32)[:, None, None, None]
    angular = factor[None, None, :, None] * (scaled * scaled) * centre
    rhs = (centre + strength * (second - angular)) * live[None, None]

    def solve_slot(carry, at):
        matrix = lax.dynamic_index_in_dim(
            inverses, upper[at].astype(jnp.int32), 1, keepdims=False
        ).astype(jnp.float32)
        block = lax.dynamic_index_in_dim(rhs, at, 2, keepdims=False)
        product = jnp.einsum("fij,fjc->fic", matrix, block, precision=lax.Precision.HIGHEST)
        return carry, product.astype(jnp.bfloat16)

    solved = lax.scan(solve_slot, 0, jnp.arange(z.capacity))[1]
    solved = jnp.moveaxis(solved, 0, 2)
    solved = solved.reshape(z.fields, z.devices, z.local, z.capacity, z.width)
    returned = lax.all_to_all(solved, AXES, split_axis=1, concat_axis=3, tiled=True)
    returned = returned.reshape(z.fields, z.local, total, z.width)
    grid = jnp.take(returned, slot_place, axis=2)
    before, after = beside(z, grid[:, :1], grid[:, -1:])
    rimmed = jnp.concatenate([before, grid, after], axis=1).astype(jnp.float32)
    return grid, (0.5 * (rimmed[:, 2:] - rimmed[:, :-2])).astype(jnp.bfloat16)


def solution(mesh):
    in_specs = (P(None, AXES), P(None, AXES), P(), P())
    out_specs = (P(None, AXES), P(None, AXES))
    return jax.shard_map(body, mesh=mesh, in_specs=in_specs, out_specs=out_specs, check_vma=False)
```

```python
import functools

import jax
import jax.numpy as jnp
import numpy as np
from jax import lax
from jax.experimental import pallas as pl
from jax.experimental.pallas import tpu as pltpu
from jax.sharding import PartitionSpec as P

LMAX1 = 1024
OB = 64
AXES = ("rad", "lm")
PLANE = 8
GIFT = 8
GROUP = 16
VMEM = 48 << 20
RIDES = 8

inner_radius = 0.35
shell_depth = 0.65
diffusion_numbers = (0.9, 0.4)


class Sizes:
    def __init__(self, devices, grid_field, inverses, slot_blocks):
        self.devices = devices
        self.fields, self.local, self.blocks, self.width = grid_field.shape
        self.levels = inverses.shape[-1]
        self.capacity = slot_blocks.shape[1]
        self.degrees = 2 * devices
        self.spacing = LMAX1 // self.degrees
        self.group_size = OB * self.degrees // LMAX1
        index = np.arange(self.degrees)
        self.counts = [int(c) for c in index // self.group_size + 1]
        self.starts = [int(s) for s in np.cumsum(self.counts) - self.counts]
        self.partial = [q for q in range(self.degrees) if (q + 1) % self.group_size]

    def last_block(self, q):
        turns = lax.div(q, self.group_size)
        rest = lax.rem(q, self.group_size)
        return self.group_size * lax.div(turns * (turns + 1), 2) + rest * (turns + 1) + turns

    def last_live(self, q):
        return 2 * self.spacing * (lax.rem(q, self.group_size) + 1)


def slot_choices(z):
    mean = -(-z.blocks // z.devices)
    return sorted({min(mean + extra, z.capacity) for extra in (0, 1, 2, 3)} | {z.capacity})


def plan_kernel(z, choices, start_ref, choice_ref, place_ref, mate_ref, load_ref, room_ref, device_ref,
                next_ref, count_ref, stack_ref):
    half = z.degrees // 2
    planes = z.devices // PLANE
    owner = [lax.div(start_ref[q], z.capacity) for q in range(z.degrees)]
    for q in range(half, z.degrees):
        load_ref[owner[q]] = start_ref[q] - owner[q] * z.capacity + z.counts[q]
    kinds = z.group_size
    for i in range(planes * kinds):
        count_ref[i] = 0
    for q in range(z.degrees):
        mate_ref[q] = -1
    for q in z.partial:
        if q < half:
            kind = lax.div(owner[q], PLANE) * kinds + q % kinds
            stack_ref[kind * PLANE + count_ref[kind]] = q
            count_ref[kind] += 1
    for q in sorted(z.partial, key=lambda q: -(q % kinds)):
        if q < half:
            continue
        first_kind = lax.div(owner[q], PLANE) * kinds
        kind = jnp.int32(-1)
        for i in range(kinds - 1 - q % kinds):
            kind = jnp.where(count_ref[first_kind + i] > 0, first_kind + i, kind)

        @pl.when(kind >= 0)
        def _(kind=kind, q=q):
            left = count_ref[kind] - 1
            count_ref[kind] = left
            host = stack_ref[kind * PLANE + left]
            mate_ref[q] = host
            mate_ref[host] = q
            load_ref[owner[q]] -= 1

    loads = [load_ref[d] for d in range(z.devices)]
    totals = [sum(loads[g * PLANE : (g + 1) * PLANE]) for g in range(planes)]
    most = functools.reduce(jnp.maximum, [totals[g] + totals[g + 1] for g in range(0, planes, 2)])
    choice = jnp.int32(0)
    slots = jnp.int32(choices[0])
    highest = functools.reduce(jnp.maximum, totals)
    for i in range(1, len(choices)):
        tried = choices[i - 1]
        beyond = (most > 2 * PLANE * tried) | (highest > PLANE * tried + GIFT * PLANE // 2)
        choice = jnp.where(beyond, i, choice)
        slots = jnp.where(beyond, choices[i], slots)
    choice_ref[0] = choice
    for d in range(z.devices):
        excess = totals[d // PLANE] - PLANE * slots - GIFT * (d % PLANE // 2)
        gift = jnp.int32(0) if d % 2 else jnp.clip(excess, 0, GIFT)
        load_ref[d] = loads[d] - gift
        room_ref[d ^ PLANE] = slots - gift
    for g in range(planes):
        device_ref[g] = g * PLANE
        next_ref[g] = load_ref[g * PLANE]
    for q in range(z.degrees):
        first = start_ref[q] + owner[q] * (slots - z.capacity)
        for p in range(z.counts[q]):
            place_ref[z.starts[q] + p] = first + p
    for q in range(half, z.degrees):
        plane = lax.div(owner[q], PLANE)
        offset = start_ref[q] - owner[q] * z.capacity
        kept = load_ref[owner[q]] - offset

        def move(p, carry, plane=plane, q=q):
            def full(state):
                return state[1] >= room_ref[state[0]]

            def advance(state):
                return state[0] + 1, load_ref[state[0] + 1]

            holder, slot = lax.while_loop(full, advance, (device_ref[plane], next_ref[plane]))
            device_ref[plane] = holder
            next_ref[plane] = slot + 1
            place_ref[z.starts[q] + p] = holder * slots + slot
            return carry

        lax.fori_loop(jnp.minimum(room_ref[owner[q]] - offset, kept), kept, move, 0)
        other = owner[q] ^ PLANE
        given = other * slots + room_ref[other] - kept

        def give(p, carry, given=given, q=q):
            place_ref[z.starts[q] + p] = given + p
            return carry

        host = mate_ref[q]
        lax.fori_loop(kept, z.counts[q] - jnp.where(host >= 0, 1, 0), give, 0)

        @pl.when(host >= 0)
        def _(host=host, q=q):
            home = start_ref[host] + lax.div(start_ref[host], z.capacity) * (slots - z.capacity)
            place_ref[z.starts[q] + z.counts[q] - 1] = home + lax.div(host, kinds)


def plan(z, degree_start, choices):
    smem = pl.BlockSpec(memory_space=pltpu.SMEM)
    planes = z.devices // PLANE
    return pl.pallas_call(
        functools.partial(plan_kernel, z, choices),
        in_specs=[smem],
        out_specs=[smem] * 3,
        out_shape=[
            jax.ShapeDtypeStruct((1,), jnp.int32),
            jax.ShapeDtypeStruct((z.blocks,), jnp.int32),
            jax.ShapeDtypeStruct((z.degrees,), jnp.int32),
        ],
        scratch_shapes=[
            pltpu.SMEM((z.devices,), jnp.int32),
            pltpu.SMEM((z.devices,), jnp.int32),
            pltpu.SMEM((planes,), jnp.int32),
            pltpu.SMEM((planes,), jnp.int32),
            pltpu.SMEM((planes * z.group_size,), jnp.int32),
            pltpu.SMEM((planes * z.group_size * PLANE,), jnp.int32),
        ],
        name="plan",
    )(degree_start)


def swap(value, axis, bit):
    size = lax.axis_size(axis)
    return lax.ppermute(value, axis, [(i, i ^ bit) for i in range(size)])


def straight_inverses(inverses):
    own = inverses[:, 1]
    rad, lm = lax.axis_size("rad"), lax.axis_size("lm")
    facing = [(d, d ^ PLANE) for d in range(0, rad * lm, 2)]
    return own, swap(own, "lm", 2), swap(own, "rad", 1), lax.ppermute(own, AXES, facing)


def other_core(values):
    return [swap(value, "lm", 1) for value in values]


def riding(z, mate_ref, q):
    b, host = z.last_block(q), mate_ref[q]
    rides = host >= 0
    host = jnp.maximum(host, 0)
    return b, jnp.where(rides, z.last_block(host), b), jnp.where(rides, z.last_live(host), z.width)


def pack_kernel(z, place_ref, mate_ref, field_ref, out_ref, *rest):
    wide_ref = rest[-1]
    pitch = z.blocks + 1
    for level in range(z.local):
        wide_ref[pl.ds(level * pitch, z.blocks), :] = field_ref[0, level].astype(jnp.float32)

    def group(g, carry):
        for k in range(GROUP):
            b = g * GROUP + k
            tile = wide_ref[pl.ds(b, z.local, stride=pitch), :]
            out_ref[place_ref[b]] = tile.astype(jnp.bfloat16)
        return carry

    lax.fori_loop(0, z.blocks // GROUP, group, 0)
    column = lax.broadcasted_iota(jnp.int32, (z.local, z.width), 1)

    def ride(q, carry):
        b, host_block, live = riding(z, mate_ref, q)
        rider = pltpu.roll(wide_ref[pl.ds(b, z.local, stride=pitch), :], live, 1)
        tile = wide_ref[pl.ds(host_block, z.local, stride=pitch), :]
        out_ref[place_ref[b]] = jnp.where(column < live, tile, rider).astype(jnp.bfloat16)
        return carry

    lax.fori_loop(z.degrees // 2, z.degrees, ride, 0, unroll=RIDES)
    if len(rest) == 1:
        return
    holder_ref = rest[0]

    def clear(k, carry):
        holder_ref[k] = 0
        return carry

    lax.fori_loop(0, z.devices * z.capacity, clear, 0, unroll=8)

    def degree(q, b):
        def block(p, inner):
            holder_ref[place_ref[b + p]] = q * OB + p
            return inner

        count = lax.div(q, z.group_size) + 1
        rides = (q >= z.degrees // 2) & (mate_ref[q] >= 0)
        lax.fori_loop(0, count - jnp.where(rides, 1, 0), block, 0)
        return b + count

    lax.fori_loop(0, z.degrees, degree, 0)


def pack(z, place, mate, grid_field, f, slots, with_holder):
    total = z.devices * slots
    out_specs = [pl.BlockSpec((total, z.local, z.width), lambda i, *s: (0, 0, 0))]
    out_shape = [jax.ShapeDtypeStruct((total, z.local, z.width), jnp.bfloat16)]
    if with_holder:
        out_specs.append(pl.BlockSpec(memory_space=pltpu.SMEM))
        out_shape.append(jax.ShapeDtypeStruct((z.devices * z.capacity,), jnp.int32))
    return pl.pallas_call(
        functools.partial(pack_kernel, z),
        grid_spec=pltpu.PrefetchScalarGridSpec(
            num_scalar_prefetch=2,
            grid=(1,),
            in_specs=[
                pl.BlockSpec((1, z.local, z.blocks, z.width), lambda i, *s: (f, 0, 0, 0))
            ],
            out_specs=out_specs,
            scratch_shapes=[pltpu.VMEM((z.local * (z.blocks + 1), z.width), jnp.float32)],
        ),
        out_shape=out_shape,
        compiler_params=pltpu.CompilerParams(vmem_limit_bytes=VMEM),
        cost_estimate=pl.CostEstimate(flops=10**9, bytes_accessed=10**7, transcendentals=0),
        name=f"pack_{f}",
    )(place, mate, grid_field)


def solve_kernel(z, f, slots, per_step, holder_ref, start_ref, mate_ref, me_ref, columns_ref, inverses_ref, *rest):
    (own, across, along, corner, own_odd, across_odd, along_odd, corner_odd, far) = rest[:9]
    out_ref, matrix_ref, square_ref, above_ref, below_ref, sems = rest[9:]
    strength = diffusion_numbers[f]
    step = pl.program_id(0)
    shape = (z.levels, z.width)
    me = me_ref[0]

    @pl.when(step == 0)
    def _():
        sources = [
            own.at[f], own_odd.at[f], across.at[f], across_odd.at[f],
            along.at[f], along_odd.at[f], corner.at[0], corner_odd.at[0],
            inverses_ref.at[f, 0], far.at[f],
        ]
        copies = [
            pltpu.make_async_copy(source, matrix_ref.at[i], sems.at[i])
            for i, source in enumerate(sources)
        ]
        for copy in copies:
            copy.start()
        level = lax.broadcasted_iota(jnp.int32, shape, 0)

        def radius(positions):
            return inner_radius + shell_depth * (positions + 1).astype(jnp.float32) / (z.levels + 1)

        here = radius(level)
        scaled = (shell_depth / (z.levels + 1)) / here
        square_ref[...] = strength * (scaled * scaled)
        above_ref[...] = jnp.where(level == z.levels - 1, 0.0, strength * radius(level + 1) / here)
        below_ref[...] = jnp.where(level == 0, 0.0, strength * radius(level - 1) / here)
        for copy in copies:
            copy.wait()

    column = lax.broadcasted_iota(jnp.int32, shape, 1)
    host = lax.div(holder_ref[me * slots], OB)
    rider = mate_ref[host]
    host_at = lax.div(host, z.group_size) - step * per_step
    rides = (rider >= 0) & (host_at >= 0) & (host_at < per_step)

    def block(i, carry):
        again = i >= per_step
        k = jnp.where(again, host_at, i)
        code = holder_ref[me * slots + jnp.minimum(step * per_step + k, slots - 1)]
        q = jnp.where(again, rider, lax.div(code, OB))
        value = z.spacing * (q + 1) - 1
        last = value - lax.rem(code, OB) * (z.width // 2)
        begin = jnp.where(again, z.last_live(host), 0)
        end = jnp.where(again, begin + z.last_live(rider), 2 * last + 2)
        offset = lax.div(start_ref[q], z.capacity) ^ me
        which = jnp.where(offset < PLANE, offset, PLANE + 1)
        which = jnp.where(q >= z.degrees // 2, which, PLANE)
        factor = (value * (value + 1)).astype(jnp.float32)
        u = columns_ref[:, k].reshape(shape).astype(jnp.float32)
        u = jnp.where((column >= begin) & (column < end), u, 0.0)
        weight = (1.0 - 2.0 * strength) - factor * square_ref[...]
        rhs = weight * u
        rhs += above_ref[...] * pltpu.roll(u, z.levels - 1, 0)
        rhs += below_ref[...] * pltpu.roll(u, 1, 0)
        high = rhs.astype(jnp.bfloat16)
        low = (rhs - high.astype(jnp.float32)).astype(jnp.bfloat16)
        both = jnp.concatenate([high, low], axis=1)
        product = jnp.dot(matrix_ref[which], both, preferred_element_type=jnp.float32)
        solved = product[:, : z.width] + product[:, z.width :]
        earlier = out_ref[:, k].reshape(shape).astype(jnp.float32)
        solved = jnp.where(column >= begin, solved, earlier).astype(jnp.bfloat16)
        out_ref[:, k] = solved.reshape(z.devices, z.local, z.width)
        return carry

    lax.fori_loop(0, per_step + jnp.where(rides, 1, 0), block, 0)


def solve(z, holder, degree_start, mate, me, columns, inverses, pieces, f, slots):
    steps = pl.cdiv(slots, 5)
    per_step = pl.cdiv(slots, steps)
    block = (z.devices, per_step, z.local, z.width)
    spec = pl.BlockSpec(block, lambda i, *s: (0, i, 0, 0))
    return pl.pallas_call(
        functools.partial(solve_kernel, z, f, slots, per_step),
        grid_spec=pltpu.PrefetchScalarGridSpec(
            num_scalar_prefetch=4,
            grid=(steps,),
            in_specs=[spec] + [pl.BlockSpec(memory_space=pl.ANY)] * (1 + len(pieces)),
            out_specs=spec,
            scratch_shapes=[pltpu.VMEM((PLANE + 2, z.levels, z.levels), jnp.bfloat16)]
            + [pltpu.VMEM((z.levels, z.width), jnp.float32)] * 3
            + [pltpu.SemaphoreType.DMA((PLANE + 2,))],
        ),
        out_shape=jax.ShapeDtypeStruct(columns.shape, jnp.bfloat16),
        compiler_params=pltpu.CompilerParams(vmem_limit_bytes=VMEM),
        cost_estimate=pl.CostEstimate(flops=10**10, bytes_accessed=10**7, transcendentals=0),
        name=f"solve_{f}",
    )(holder, degree_start, mate, me, columns, inverses, *pieces)


def unpack_kernel(z, place_ref, mate_ref, returned_ref, *rest):
    grid_ref, slope_ref, first_ref, last_ref, wide_ref = rest[-5:]
    pitch = z.blocks + 1

    def gather(g, carry):
        for k in range(GROUP):
            b = g * GROUP + k
            tile = returned_ref[place_ref[b]].astype(jnp.float32)
            wide_ref[pl.ds(b, z.local, stride=pitch), :] = tile
        return carry

    lax.fori_loop(0, z.blocks // GROUP, gather, 0)
    column = lax.broadcasted_iota(jnp.int32, (z.local, z.width), 1)

    def ride(q, carry):
        b, host_block, live = riding(z, mate_ref, q)
        tile = returned_ref[place_ref[b]].astype(jnp.float32)
        rider = pltpu.roll(tile, z.width - live, 1)
        host_rows = pl.ds(host_block, z.local, stride=pitch)
        wide_ref[host_rows, :] = jnp.where(column < live, tile, 0.0)
        rows = pl.ds(b, z.local, stride=pitch)
        wide_ref[rows, :] = jnp.where(column < z.last_live(q), rider, 0.0)
        return carry

    lax.fori_loop(z.degrees // 2, z.degrees, ride, 0, unroll=RIDES)

    def group(g, carry):
        at = pl.multiple_of(g * GROUP, GROUP)
        rows = pl.ds(at, GROUP)
        value = [wide_ref[pl.ds(at + i * pitch, GROUP), :] for i in range(z.local)]
        for i in range(z.local):
            grid_ref[0, i, rows, :] = value[i].astype(jnp.bfloat16)
        for i in range(1, z.local - 1):
            slope = 0.5 * (value[i + 1] - value[i - 1])
            slope_ref[0, i, rows, :] = slope.astype(jnp.bfloat16)
        first_ref[0, rows, :] = value[0].astype(jnp.bfloat16)
        last_ref[0, rows, :] = value[-1].astype(jnp.bfloat16)
        return carry

    lax.fori_loop(0, z.blocks // GROUP, group, 0, unroll=2)


def unpack(z, place, mate, returned, f, earlier):
    whole = jax.ShapeDtypeStruct((z.fields, z.local, z.blocks, z.width), jnp.bfloat16)
    level = jax.ShapeDtypeStruct((1, z.blocks, z.width), jnp.bfloat16)
    spec = pl.BlockSpec((1, z.local, z.blocks, z.width), lambda i, *s: (f, 0, 0, 0))
    level_spec = pl.BlockSpec(level.shape, lambda i, *s: (0, 0, 0))
    return pl.pallas_call(
        functools.partial(unpack_kernel, z),
        grid_spec=pltpu.PrefetchScalarGridSpec(
            num_scalar_prefetch=2,
            grid=(1,),
            in_specs=[pl.BlockSpec(returned.shape, lambda i, *s: (0, 0, 0))]
            + [pl.BlockSpec(memory_space=pl.ANY)] * len(earlier),
            out_specs=[spec, spec, level_spec, level_spec],
            scratch_shapes=[pltpu.VMEM((z.local * (z.blocks + 1), z.width), jnp.float32)],
        ),
        out_shape=[whole, whole, level, level],
        input_output_aliases={3 + i: i for i in range(len(earlier))},
        compiler_params=pltpu.CompilerParams(vmem_limit_bytes=VMEM if earlier else 60 << 20),
        cost_estimate=pl.CostEstimate(flops=10**9, bytes_accessed=10**7, transcendentals=0),
        name=f"unpack_{f}",
    )(place, mate, returned, *earlier)


def edge_kernel(z, f, second_ref, before_last_ref, before_ref, after_ref, slope_in_ref, slope_ref,
                edge_ref, sems):
    del slope_in_ref

    def wide(ref):
        return ref[...].reshape(z.blocks, z.width).astype(jnp.float32)

    slopes = [wide(second_ref) - wide(before_ref), wide(after_ref) - wide(before_last_ref)]
    copies = []
    for i, level in enumerate((0, z.local - 1)):
        edge_ref[i] = (0.5 * slopes[i]).astype(jnp.bfloat16)
        copies.append(pltpu.make_async_copy(edge_ref.at[i], slope_ref.at[f, level], sems.at[i]))
        copies[i].start()
    for copy in copies:
        copy.wait()


def edges(z, slope, grid, before, after, f):
    block = (1, 1, z.blocks, z.width)
    beside_spec = pl.BlockSpec((1, z.blocks, z.width), lambda i: (0, 0, 0))
    return pl.pallas_call(
        functools.partial(edge_kernel, z, f),
        grid=(1,),
        in_specs=[
            pl.BlockSpec(block, lambda i: (f, 1, 0, 0)),
            pl.BlockSpec(block, lambda i: (f, z.local - 2, 0, 0)),
            beside_spec,
            beside_spec,
            pl.BlockSpec(memory_space=pl.ANY),
        ],
        out_specs=pl.BlockSpec(memory_space=pl.ANY),
        out_shape=jax.ShapeDtypeStruct(slope.shape, slope.dtype),
        scratch_shapes=[
            pltpu.VMEM((2, z.blocks, z.width), jnp.bfloat16),
            pltpu.SemaphoreType.DMA((2,)),
        ],
        input_output_aliases={4: 0},
        compiler_params=pltpu.CompilerParams(vmem_limit_bytes=VMEM),
        name=f"edges_{f}",
    )(grid, grid, before, after, slope)


def beside(z, first, last):
    up = [(i, i + 1) for i in range(z.devices - 1)]
    down = [(j, i) for i, j in up]
    return lax.ppermute(last, AXES, up), lax.ppermute(first, AXES, down)


def exchange(z, value, slots):
    shaped = value.reshape(z.devices, slots, z.local, z.width)
    return lax.all_to_all(shaped, AXES, split_axis=0, concat_axis=0, tiled=True)


def body(grid_field, inverses, slot_blocks, degree_start):
    rad, lm = lax.axis_size("rad"), lax.axis_size("lm")
    z = Sizes(rad * lm, grid_field, inverses, slot_blocks)
    choices = slot_choices(z)
    kernels = z.local % 16 == 0 and z.blocks % GROUP == 0 and rad % 4 == 0 and lm == PLANE // 2
    low, high = z.counts[z.degrees // 2 - 1 : z.degrees // 2 + 1]
    if not kernels or low + GIFT > choices[0] or high <= GIFT or z.capacity - choices[0] > GIFT:
        return plain_body(z, grid_field, inverses, degree_start)
    me = lax.axis_index(AXES).reshape(1).astype(jnp.int32)
    choice, place, mate = plan(z, degree_start, choices)
    routes = [functools.partial(route, z, slots) for slots in choices]
    return lax.switch(choice[0], routes, grid_field, inverses, degree_start, me, place, mate)


def route(z, slots, grid_field, inverses, degree_start, me, place, mate):
    (sent_0,) = pack(z, place, mate, grid_field, 0, slots, False)
    sent_1, holder = pack(z, place, mate, grid_field, 1, slots, True)
    sent_1, own, across, along, far = lax.optimization_barrier(
        (sent_1, *straight_inverses(inverses))
    )
    columns = [exchange(z, sent, slots) for sent in (sent_0, sent_1)]
    corner_0 = swap(across[:1], "rad", 1)
    even = [own, across, along]
    odd = other_core(even)
    pieces = lax.optimization_barrier((*even, corner_0, *odd, *other_core([corner_0]), far))
    solved_0 = solve(z, holder, degree_start, mate, me, columns[0], inverses, pieces, 0, slots)
    corner_1 = swap(along[1:], "lm", 2)
    pieces = (*even, corner_1, *odd, *other_core([corner_1]), far)
    solved_1 = solve(z, holder, degree_start, mate, me, columns[1], inverses, pieces, 1, slots)
    solved = [solved_0, solved_1]
    returned = [
        exchange(z, solved[f], slots).reshape(z.devices * slots, z.local, z.width)
        for f in range(z.fields)
    ]
    outs = ()
    for f in range(z.fields):
        grid, slope, first, last = unpack(z, place, mate, returned[f], f, outs)
        outs = (grid, edges(z, slope, grid, *beside(z, first, last), f))
    return outs


def plain_body(z, grid_field, inverses, degree_start):
    index = np.arange(z.degrees)
    counts = np.asarray(z.counts)
    degree_of = np.repeat(index, counts)
    place_in = np.arange(z.blocks) - np.asarray(z.starts)[degree_of]
    value = z.spacing * (index + 1) - 1
    slot_place = degree_start[degree_of] + jnp.asarray(place_in, jnp.int32)
    total = z.devices * z.capacity
    holder = jnp.full((total,), z.blocks, jnp.int32)
    holder = holder.at[slot_place].set(jnp.arange(z.blocks, dtype=jnp.int32))
    sent = jnp.take(grid_field, holder, axis=2, mode="fill", fill_value=0)
    sent = sent.reshape(z.fields, z.local, z.devices, z.capacity, z.width)
    columns = lax.all_to_all(sent, AXES, split_axis=2, concat_axis=1, tiled=True)
    columns = columns.reshape(z.fields, z.levels, z.capacity, z.width)
    device = lax.axis_index(AXES)
    mine = lax.dynamic_slice_in_dim(holder, device * z.capacity, z.capacity)
    order = jnp.asarray(place_in)[:, None] * OB + np.arange(z.width)[None, :] // 2
    live_table = (order <= jnp.asarray(value[degree_of])[:, None]).astype(jnp.float32)
    live = jnp.take(live_table, mine, axis=0, mode="fill", fill_value=0)
    factor = (value * (value + 1)).astype(np.float32)[degree_of]
    factor = jnp.take(jnp.asarray(factor), mine, mode="fill", fill_value=0)
    upper = jnp.take(jnp.asarray(degree_of >= z.degrees // 2), mine, mode="fill", fill_value=False)
    radius = inner_radius + shell_depth * jnp.arange(z.levels + 2, dtype=jnp.float32) / (z.levels + 1)
    here = radius[1:-1][None, :, None, None]
    padded = jnp.pad(columns.astype(jnp.float32), ((0, 0), (1, 1), (0, 0), (0, 0)))
    weighted = padded * radius[None, :, None, None]
    second = (weighted[:, 2:] - 2.0 * weighted[:, 1:-1] + weighted[:, :-2]) / here
    scaled = (shell_depth / (z.levels + 1)) / here
    centre = padded[:, 1:-1]
    strength = jnp.asarray(diffusion_numbers, jnp.float32)[:, None, None, None]
    angular = factor[None, None, :, None] * (scaled * scaled) * centre
    rhs = (centre + strength * (second - angular)) * live[None, None]

    def solve_slot(carry, at):
        matrix = lax.dynamic_index_in_dim(
            inverses, upper[at].astype(jnp.int32), 1, keepdims=False
        ).astype(jnp.float32)
        block = lax.dynamic_index_in_dim(rhs, at, 2, keepdims=False)
        product = jnp.einsum("fij,fjc->fic", matrix, block, precision=lax.Precision.HIGHEST)
        return carry, product.astype(jnp.bfloat16)

    solved = lax.scan(solve_slot, 0, jnp.arange(z.capacity))[1]
    solved = jnp.moveaxis(solved, 0, 2)
    solved = solved.reshape(z.fields, z.devices, z.local, z.capacity, z.width)
    returned = lax.all_to_all(solved, AXES, split_axis=1, concat_axis=3, tiled=True)
    returned = returned.reshape(z.fields, z.local, total, z.width)
    grid = jnp.take(returned, slot_place, axis=2)
    before, after = beside(z, grid[:, :1], grid[:, -1:])
    rimmed = jnp.concatenate([before, grid, after], axis=1).astype(jnp.float32)
    return grid, (0.5 * (rimmed[:, 2:] - rimmed[:, :-2])).astype(jnp.bfloat16)


def solution(mesh):
    in_specs = (P(None, AXES), P(None, AXES), P(), P())
    out_specs = (P(None, AXES), P(None, AXES))
    return jax.shard_map(body, mesh=mesh, in_specs=in_specs, out_specs=out_specs, check_vma=False)
```

```python
import functools

import jax
import jax.numpy as jnp
import numpy as np
from jax import lax
from jax.experimental import pallas as pl
from jax.experimental.pallas import tpu as pltpu
from jax.sharding import PartitionSpec as P

LMAX1 = 1024
OB = 64
AXES = ("rad", "lm")
PLANE = 8
GIFT = 8
GROUP = 16
VMEM = 48 << 20
MORE_VMEM = 60 << 20
RIDES = 8

inner_radius = 0.35
shell_depth = 0.65
diffusion_numbers = (0.9, 0.4)


class Sizes:
    def __init__(self, devices, grid_field, inverses, slot_blocks):
        self.devices = devices
        self.fields, self.local, self.blocks, self.width = grid_field.shape
        self.levels = inverses.shape[-1]
        self.capacity = slot_blocks.shape[1]
        self.degrees = 2 * devices
        self.spacing = LMAX1 // self.degrees
        self.group_size = OB * self.degrees // LMAX1
        index = np.arange(self.degrees)
        self.counts = [int(c) for c in index // self.group_size + 1]
        self.starts = [int(s) for s in np.cumsum(self.counts) - self.counts]
        self.partial = [q for q in range(self.degrees) if (q + 1) % self.group_size]

    def last_block(self, q):
        turns = lax.div(q, self.group_size)
        rest = lax.rem(q, self.group_size)
        return self.group_size * lax.div(turns * (turns + 1), 2) + rest * (turns + 1) + turns

    def last_live(self, q):
        return 2 * self.spacing * (lax.rem(q, self.group_size) + 1)


def slot_choices(z):
    mean = -(-z.blocks // z.devices)
    return sorted({min(mean + extra, z.capacity) for extra in (0, 1, 2, 3)} | {z.capacity})


def plan_kernel(z, choices, start_ref, choice_ref, place_ref, mate_ref, load_ref, room_ref, device_ref,
                next_ref, count_ref, stack_ref):
    half = z.degrees // 2
    planes = z.devices // PLANE
    owner = [lax.div(start_ref[q], z.capacity) for q in range(z.degrees)]
    for q in range(half, z.degrees):
        load_ref[owner[q]] = start_ref[q] - owner[q] * z.capacity + z.counts[q]
    kinds = z.group_size
    for i in range(planes * kinds):
        count_ref[i] = 0
    for q in range(z.degrees):
        mate_ref[q] = -1
    for q in z.partial:
        if q < half:
            kind = lax.div(owner[q], PLANE) * kinds + q % kinds
            stack_ref[kind * PLANE + count_ref[kind]] = q
            count_ref[kind] += 1
    for q in sorted(z.partial, key=lambda q: -(q % kinds)):
        if q < half:
            continue
        first_kind = lax.div(owner[q], PLANE) * kinds
        kind = jnp.int32(-1)
        for i in range(kinds - 1 - q % kinds):
            kind = jnp.where(count_ref[first_kind + i] > 0, first_kind + i, kind)

        @pl.when(kind >= 0)
        def _(kind=kind, q=q):
            left = count_ref[kind] - 1
            count_ref[kind] = left
            host = stack_ref[kind * PLANE + left]
            mate_ref[q] = host
            mate_ref[host] = q
            load_ref[owner[q]] -= 1

    loads = [load_ref[d] for d in range(z.devices)]
    totals = [sum(loads[g * PLANE : (g + 1) * PLANE]) for g in range(planes)]
    most = functools.reduce(jnp.maximum, [totals[g] + totals[g + 1] for g in range(0, planes, 2)])
    choice = jnp.int32(0)
    slots = jnp.int32(choices[0])
    highest = functools.reduce(jnp.maximum, totals)
    for i in range(1, len(choices)):
        tried = choices[i - 1]
        beyond = (most > 2 * PLANE * tried) | (highest > PLANE * tried + GIFT * PLANE // 2)
        choice = jnp.where(beyond, i, choice)
        slots = jnp.where(beyond, choices[i], slots)
    choice_ref[0] = choice
    for d in range(z.devices):
        excess = totals[d // PLANE] - PLANE * slots - GIFT * (d % PLANE // 2)
        gift = jnp.int32(0) if d % 2 else jnp.clip(excess, 0, GIFT)
        load_ref[d] = loads[d] - gift
        room_ref[d ^ PLANE] = slots - gift
    for g in range(planes):
        device_ref[g] = g * PLANE
        next_ref[g] = load_ref[g * PLANE]
    for q in range(z.degrees):
        first = start_ref[q] + owner[q] * (slots - z.capacity)
        for p in range(z.counts[q]):
            place_ref[z.starts[q] + p] = first + p
    for q in range(half, z.degrees):
        plane = lax.div(owner[q], PLANE)
        offset = start_ref[q] - owner[q] * z.capacity
        kept = load_ref[owner[q]] - offset

        def move(p, carry, plane=plane, q=q):
            def full(state):
                return state[1] >= room_ref[state[0]]

            def advance(state):
                return state[0] + 1, load_ref[state[0] + 1]

            holder, slot = lax.while_loop(full, advance, (device_ref[plane], next_ref[plane]))
            device_ref[plane] = holder
            next_ref[plane] = slot + 1
            place_ref[z.starts[q] + p] = holder * slots + slot
            return carry

        lax.fori_loop(jnp.minimum(room_ref[owner[q]] - offset, kept), kept, move, 0)
        other = owner[q] ^ PLANE
        given = other * slots + room_ref[other] - kept

        def give(p, carry, given=given, q=q):
            place_ref[z.starts[q] + p] = given + p
            return carry

        host = mate_ref[q]
        lax.fori_loop(kept, z.counts[q] - jnp.where(host >= 0, 1, 0), give, 0)

        @pl.when(host >= 0)
        def _(host=host, q=q):
            home = start_ref[host] + lax.div(start_ref[host], z.capacity) * (slots - z.capacity)
            place_ref[z.starts[q] + z.counts[q] - 1] = home + lax.div(host, kinds)


def plan(z, degree_start, choices):
    smem = pl.BlockSpec(memory_space=pltpu.SMEM)
    planes = z.devices // PLANE
    return pl.pallas_call(
        functools.partial(plan_kernel, z, choices),
        in_specs=[smem],
        out_specs=[smem] * 3,
        out_shape=[
            jax.ShapeDtypeStruct((1,), jnp.int32),
            jax.ShapeDtypeStruct((z.blocks,), jnp.int32),
            jax.ShapeDtypeStruct((z.degrees,), jnp.int32),
        ],
        scratch_shapes=[
            pltpu.SMEM((z.devices,), jnp.int32),
            pltpu.SMEM((z.devices,), jnp.int32),
            pltpu.SMEM((planes,), jnp.int32),
            pltpu.SMEM((planes,), jnp.int32),
            pltpu.SMEM((planes * z.group_size,), jnp.int32),
            pltpu.SMEM((planes * z.group_size * PLANE,), jnp.int32),
        ],
        name="plan",
    )(degree_start)


def swap(value, axis, bit):
    size = lax.axis_size(axis)
    return lax.ppermute(value, axis, [(i, i ^ bit) for i in range(size)])


def straight_inverses(inverses):
    own = inverses[:, 1]
    rad, lm = lax.axis_size("rad"), lax.axis_size("lm")
    facing = [(d, d ^ PLANE) for d in range(0, rad * lm, 2)]
    return own, swap(own, "lm", 2), swap(own, "rad", 1), lax.ppermute(own, AXES, facing)


def other_core(values):
    return [swap(value, "lm", 1) for value in values]


def riding(z, mate_ref, q):
    b, host = z.last_block(q), mate_ref[q]
    rides = host >= 0
    host = jnp.maximum(host, 0)
    return b, jnp.where(rides, z.last_block(host), b), jnp.where(rides, z.last_live(host), z.width)


def pack_kernel(z, place_ref, mate_ref, field_ref, out_ref, *rest):
    wide_ref = rest[-1]
    pitch = z.blocks + 1
    for level in range(z.local):
        wide_ref[pl.ds(level * pitch, z.blocks), :] = field_ref[0, level].astype(jnp.float32)

    def group(g, carry):
        for k in range(GROUP):
            b = g * GROUP + k
            tile = wide_ref[pl.ds(b, z.local, stride=pitch), :]
            out_ref[place_ref[b]] = tile.astype(jnp.bfloat16)
        return carry

    lax.fori_loop(0, z.blocks // GROUP, group, 0)
    column = lax.broadcasted_iota(jnp.int32, (z.local, z.width), 1)

    def ride(q, carry):
        b, host_block, live = riding(z, mate_ref, q)
        rider = pltpu.roll(wide_ref[pl.ds(b, z.local, stride=pitch), :], live, 1)
        tile = wide_ref[pl.ds(host_block, z.local, stride=pitch), :]
        out_ref[place_ref[b]] = jnp.where(column < live, tile, rider).astype(jnp.bfloat16)
        return carry

    lax.fori_loop(z.degrees // 2, z.degrees, ride, 0, unroll=RIDES)
    if len(rest) == 1:
        return
    holder_ref = rest[0]

    def clear(k, carry):
        holder_ref[k] = 0
        return carry

    lax.fori_loop(0, z.devices * z.capacity, clear, 0, unroll=8)

    def degree(q, b):
        def block(p, inner):
            holder_ref[place_ref[b + p]] = q * OB + p
            return inner

        count = lax.div(q, z.group_size) + 1
        rides = (q >= z.degrees // 2) & (mate_ref[q] >= 0)
        lax.fori_loop(0, count - jnp.where(rides, 1, 0), block, 0)
        return b + count

    lax.fori_loop(0, z.degrees, degree, 0)


def pack(z, place, mate, grid_field, f, slots, with_holder):
    total = z.devices * slots
    out_specs = [pl.BlockSpec((total, z.local, z.width), lambda i, *s: (0, 0, 0))]
    out_shape = [jax.ShapeDtypeStruct((total, z.local, z.width), jnp.bfloat16)]
    if with_holder:
        out_specs.append(pl.BlockSpec(memory_space=pltpu.SMEM))
        out_shape.append(jax.ShapeDtypeStruct((z.devices * z.capacity,), jnp.int32))
    return pl.pallas_call(
        functools.partial(pack_kernel, z),
        grid_spec=pltpu.PrefetchScalarGridSpec(
            num_scalar_prefetch=2,
            grid=(1,),
            in_specs=[
                pl.BlockSpec((1, z.local, z.blocks, z.width), lambda i, *s: (f, 0, 0, 0))
            ],
            out_specs=out_specs,
            scratch_shapes=[pltpu.VMEM((z.local * (z.blocks + 1), z.width), jnp.float32)],
        ),
        out_shape=out_shape,
        compiler_params=pltpu.CompilerParams(vmem_limit_bytes=VMEM),
        cost_estimate=pl.CostEstimate(flops=10**9, bytes_accessed=10**7, transcendentals=0),
        name=f"pack_{f}",
    )(place, mate, grid_field)


def solve_kernel(z, f, slots, per_step, holder_ref, start_ref, mate_ref, me_ref, columns_ref, inverses_ref, *rest):
    (own, across, along, corner, own_odd, across_odd, along_odd, corner_odd, far) = rest[:9]
    out_ref, matrix_ref, square_ref, above_ref, below_ref, sems = rest[9:]
    strength = diffusion_numbers[f]
    step = pl.program_id(0)
    shape = (z.levels, z.width)
    me = me_ref[0]

    @pl.when(step == 0)
    def _():
        sources = [
            own.at[f], own_odd.at[f], across.at[f], across_odd.at[f],
            along.at[f], along_odd.at[f], corner.at[0], corner_odd.at[0],
            inverses_ref.at[f, 0], far.at[f],
        ]
        copies = [
            pltpu.make_async_copy(source, matrix_ref.at[i], sems.at[i])
            for i, source in enumerate(sources)
        ]
        for copy in copies:
            copy.start()
        level = lax.broadcasted_iota(jnp.int32, shape, 0)

        def radius(positions):
            return inner_radius + shell_depth * (positions + 1).astype(jnp.float32) / (z.levels + 1)

        here = radius(level)
        scaled = (shell_depth / (z.levels + 1)) / here
        square_ref[...] = strength * (scaled * scaled)
        above_ref[...] = jnp.where(level == z.levels - 1, 0.0, strength * radius(level + 1) / here)
        below_ref[...] = jnp.where(level == 0, 0.0, strength * radius(level - 1) / here)
        for copy in copies:
            copy.wait()

    column = lax.broadcasted_iota(jnp.int32, shape, 1)
    host = lax.div(holder_ref[me * slots], OB)
    rider = mate_ref[host]
    host_at = lax.div(host, z.group_size) - step * per_step
    rides = (rider >= 0) & (host_at >= 0) & (host_at < per_step)

    def block(i, carry):
        again = i >= per_step
        k = jnp.where(again, host_at, i)
        code = holder_ref[me * slots + jnp.minimum(step * per_step + k, slots - 1)]
        q = jnp.where(again, rider, lax.div(code, OB))
        value = z.spacing * (q + 1) - 1
        last = value - lax.rem(code, OB) * (z.width // 2)
        begin = jnp.where(again, z.last_live(host), 0)
        end = jnp.where(again, begin + z.last_live(rider), 2 * last + 2)
        offset = lax.div(start_ref[q], z.capacity) ^ me
        which = jnp.where(offset < PLANE, offset, PLANE + 1)
        which = jnp.where(q >= z.degrees // 2, which, PLANE)
        factor = (value * (value + 1)).astype(jnp.float32)
        u = columns_ref[:, k].reshape(shape).astype(jnp.float32)
        u = jnp.where((column >= begin) & (column < end), u, 0.0)
        weight = (1.0 - 2.0 * strength) - factor * square_ref[...]
        rhs = weight * u
        rhs += above_ref[...] * pltpu.roll(u, z.levels - 1, 0)
        rhs += below_ref[...] * pltpu.roll(u, 1, 0)
        high = rhs.astype(jnp.bfloat16)
        low = (rhs - high.astype(jnp.float32)).astype(jnp.bfloat16)
        both = jnp.concatenate([high, low], axis=1)
        product = jnp.dot(matrix_ref[which], both, preferred_element_type=jnp.float32)
        solved = product[:, : z.width] + product[:, z.width :]
        earlier = out_ref[:, k].reshape(shape).astype(jnp.float32)
        solved = jnp.where(column >= begin, solved, earlier).astype(jnp.bfloat16)
        out_ref[:, k] = solved.reshape(z.devices, z.local, z.width)
        return carry

    lax.fori_loop(0, per_step + jnp.where(rides, 1, 0), block, 0)


def solve(z, holder, degree_start, mate, me, columns, inverses, pieces, f, slots):
    steps = pl.cdiv(slots, 5)
    per_step = pl.cdiv(slots, steps)
    block = (z.devices, per_step, z.local, z.width)
    spec = pl.BlockSpec(block, lambda i, *s: (0, i, 0, 0))
    return pl.pallas_call(
        functools.partial(solve_kernel, z, f, slots, per_step),
        grid_spec=pltpu.PrefetchScalarGridSpec(
            num_scalar_prefetch=4,
            grid=(steps,),
            in_specs=[spec] + [pl.BlockSpec(memory_space=pl.ANY)] * (1 + len(pieces)),
            out_specs=spec,
            scratch_shapes=[pltpu.VMEM((PLANE + 2, z.levels, z.levels), jnp.bfloat16)]
            + [pltpu.VMEM((z.levels, z.width), jnp.float32)] * 3
            + [pltpu.SemaphoreType.DMA((PLANE + 2,))],
        ),
        out_shape=jax.ShapeDtypeStruct(columns.shape, jnp.bfloat16),
        compiler_params=pltpu.CompilerParams(vmem_limit_bytes=VMEM),
        cost_estimate=pl.CostEstimate(flops=10**10, bytes_accessed=10**7, transcendentals=0),
        name=f"solve_{f}",
    )(holder, degree_start, mate, me, columns, inverses, *pieces)


def unpack_kernel(z, place_ref, mate_ref, returned_ref, *rest):
    grid_ref, slope_ref, wide_ref = rest[-3:]
    pitch = z.blocks + 1

    def gather(g, carry):
        for k in range(GROUP):
            b = g * GROUP + k
            tile = returned_ref[place_ref[b]].astype(jnp.float32)
            wide_ref[pl.ds(b, z.local, stride=pitch), :] = tile
        return carry

    lax.fori_loop(0, z.blocks // GROUP, gather, 0)
    column = lax.broadcasted_iota(jnp.int32, (z.local, z.width), 1)

    def ride(q, carry):
        b, host_block, live = riding(z, mate_ref, q)
        tile = returned_ref[place_ref[b]].astype(jnp.float32)
        rider = pltpu.roll(tile, z.width - live, 1)
        host_rows = pl.ds(host_block, z.local, stride=pitch)
        wide_ref[host_rows, :] = jnp.where(column < live, tile, 0.0)
        rows = pl.ds(b, z.local, stride=pitch)
        wide_ref[rows, :] = jnp.where(column < z.last_live(q), rider, 0.0)
        return carry

    lax.fori_loop(z.degrees // 2, z.degrees, ride, 0, unroll=RIDES)

    def group(g, carry):
        at = pl.multiple_of(g * GROUP, GROUP)
        rows = pl.ds(at, GROUP)
        value = [wide_ref[pl.ds(at + i * pitch, GROUP), :] for i in range(z.local)]
        for i in range(z.local):
            grid_ref[0, i, rows, :] = value[i].astype(jnp.bfloat16)
        for i in range(1, z.local - 1):
            slope = 0.5 * (value[i + 1] - value[i - 1])
            slope_ref[0, i, rows, :] = slope.astype(jnp.bfloat16)
        return carry

    lax.fori_loop(0, z.blocks // GROUP, group, 0, unroll=2)


def unpack(z, place, mate, returned, f, earlier):
    whole = jax.ShapeDtypeStruct((z.fields, z.local, z.blocks, z.width), jnp.bfloat16)
    spec = pl.BlockSpec((1, z.local, z.blocks, z.width), lambda i, *s: (f, 0, 0, 0))
    return pl.pallas_call(
        functools.partial(unpack_kernel, z),
        grid_spec=pltpu.PrefetchScalarGridSpec(
            num_scalar_prefetch=2,
            grid=(1,),
            in_specs=[pl.BlockSpec(returned.shape, lambda i, *s: (0, 0, 0))]
            + [pl.BlockSpec(memory_space=pl.ANY)] * len(earlier),
            out_specs=[spec, spec],
            scratch_shapes=[pltpu.VMEM((z.local * (z.blocks + 1), z.width), jnp.float32)],
        ),
        out_shape=[whole, whole],
        input_output_aliases={3 + i: i for i in range(len(earlier))},
        compiler_params=pltpu.CompilerParams(vmem_limit_bytes=VMEM if earlier else MORE_VMEM),
        cost_estimate=pl.CostEstimate(flops=10**9, bytes_accessed=10**7, transcendentals=0),
        name=f"unpack_{f}",
    )(place, mate, returned, *earlier)


def rim_kernel(z, place_ref, mate_ref, returned_ref, first_ref, last_ref, first_wide_ref, last_wide_ref):
    sides = ((first_wide_ref, 0), (last_wide_ref, z.local - 1))

    def gather(g, carry):
        for k in range(GROUP):
            b = g * GROUP + k
            tile = returned_ref[place_ref[b]].astype(jnp.float32)
            for wide_ref, row in sides:
                wide_ref[pl.ds(b, 1), :] = tile[row : row + 1]
        return carry

    lax.fori_loop(0, z.blocks // GROUP, gather, 0)
    column = lax.broadcasted_iota(jnp.int32, (z.local, z.width), 1)

    def ride(q, carry):
        b, host_block, live = riding(z, mate_ref, q)
        tile = returned_ref[place_ref[b]].astype(jnp.float32)
        rider = pltpu.roll(tile, z.width - live, 1)
        rider = jnp.where(column < z.last_live(q), rider, 0.0)
        tile = jnp.where(column < live, tile, 0.0)
        for wide_ref, row in sides:
            wide_ref[pl.ds(host_block, 1), :] = tile[row : row + 1]
            wide_ref[pl.ds(b, 1), :] = rider[row : row + 1]
        return carry

    lax.fori_loop(z.degrees // 2, z.degrees, ride, 0, unroll=RIDES)
    first_ref[0] = first_wide_ref[...].astype(jnp.bfloat16)
    last_ref[0] = last_wide_ref[...].astype(jnp.bfloat16)


def rims(z, place, mate, returned, f):
    level = jax.ShapeDtypeStruct((1, z.blocks, z.width), jnp.bfloat16)
    spec = pl.BlockSpec(level.shape, lambda i, *s: (0, 0, 0))
    return pl.pallas_call(
        functools.partial(rim_kernel, z),
        grid_spec=pltpu.PrefetchScalarGridSpec(
            num_scalar_prefetch=2,
            grid=(1,),
            in_specs=[pl.BlockSpec(returned.shape, lambda i, *s: (0, 0, 0))],
            out_specs=[spec, spec],
            scratch_shapes=[pltpu.VMEM((z.blocks, z.width), jnp.float32)] * 2,
        ),
        out_shape=[level, level],
        compiler_params=pltpu.CompilerParams(vmem_limit_bytes=VMEM if f else MORE_VMEM),
        cost_estimate=pl.CostEstimate(flops=10**8, bytes_accessed=3 * 10**6, transcendentals=0),
        name=f"rims_{f}",
    )(place, mate, returned)


def edge_kernel(z, *refs):
    count = 4 * z.fields
    inner, outer, (_, slope_ref, edge_ref, sems) = refs[: count // 2], refs[count // 2 : count], refs[count:]
    copies = []
    for i in range(2 * z.fields):
        inside = inner[i][...].reshape(z.blocks, z.width).astype(jnp.float32)
        outside = outer[i][...].reshape(z.blocks, z.width).astype(jnp.float32)
        slope = inside - outside if i % 2 == 0 else outside - inside
        edge_ref[i] = (0.5 * slope).astype(jnp.bfloat16)
        level = i % 2 * (z.local - 1)
        copies.append(pltpu.make_async_copy(edge_ref.at[i], slope_ref.at[i // 2, level], sems.at[i]))
        copies[i].start()
    for copy in copies:
        copy.wait()


def edges(z, slope, grid, outside):
    def inner(f, level):
        return pl.BlockSpec((1, 1, z.blocks, z.width), lambda i: (f, level, 0, 0))

    inner_specs = [inner(f, level) for f in range(z.fields) for level in (1, z.local - 2)]
    outer_spec = pl.BlockSpec((1, z.blocks, z.width), lambda i: (0, 0, 0))
    count = len(inner_specs)
    return pl.pallas_call(
        functools.partial(edge_kernel, z),
        grid=(1,),
        in_specs=inner_specs + [outer_spec] * count + [pl.BlockSpec(memory_space=pl.ANY)],
        out_specs=pl.BlockSpec(memory_space=pl.ANY),
        out_shape=jax.ShapeDtypeStruct(slope.shape, slope.dtype),
        scratch_shapes=[
            pltpu.VMEM((count, z.blocks, z.width), jnp.bfloat16),
            pltpu.SemaphoreType.DMA((count,)),
        ],
        input_output_aliases={2 * count: 0},
        compiler_params=pltpu.CompilerParams(vmem_limit_bytes=VMEM),
        name="edges",
    )(*[grid] * count, *outside, slope)


def beside(z, first, last):
    up = [(i, i + 1) for i in range(z.devices - 1)]
    down = [(j, i) for i, j in up]
    return lax.ppermute(last, AXES, up), lax.ppermute(first, AXES, down)


def exchange(z, value, slots):
    shaped = value.reshape(z.devices, slots, z.local, z.width)
    return lax.all_to_all(shaped, AXES, split_axis=0, concat_axis=0, tiled=True)


def body(grid_field, inverses, slot_blocks, degree_start):
    rad, lm = lax.axis_size("rad"), lax.axis_size("lm")
    z = Sizes(rad * lm, grid_field, inverses, slot_blocks)
    choices = slot_choices(z)
    kernels = z.local % 16 == 0 and z.blocks % GROUP == 0 and rad % 4 == 0 and lm == PLANE // 2
    low, high = z.counts[z.degrees // 2 - 1 : z.degrees // 2 + 1]
    if not kernels or low + GIFT > choices[0] or high <= GIFT or z.capacity - choices[0] > GIFT:
        return plain_body(z, grid_field, inverses, degree_start)
    me = lax.axis_index(AXES).reshape(1).astype(jnp.int32)
    choice, place, mate = plan(z, degree_start, choices)
    routes = [functools.partial(route, z, slots) for slots in choices]
    return lax.switch(choice[0], routes, grid_field, inverses, degree_start, me, place, mate)


def route(z, slots, grid_field, inverses, degree_start, me, place, mate):
    (sent_0,) = pack(z, place, mate, grid_field, 0, slots, False)
    sent_1, holder = pack(z, place, mate, grid_field, 1, slots, True)
    sent_1, own, across, along, far = lax.optimization_barrier(
        (sent_1, *straight_inverses(inverses))
    )
    columns = [exchange(z, sent, slots) for sent in (sent_0, sent_1)]
    corner_0 = swap(across[:1], "rad", 1)
    even = [own, across, along]
    odd = other_core(even)
    pieces = lax.optimization_barrier((*even, corner_0, *odd, *other_core([corner_0]), far))
    solved_0 = solve(z, holder, degree_start, mate, me, columns[0], inverses, pieces, 0, slots)
    corner_1 = swap(along[1:], "lm", 2)
    pieces = (*even, corner_1, *odd, *other_core([corner_1]), far)
    solved_1 = solve(z, holder, degree_start, mate, me, columns[1], inverses, pieces, 1, slots)
    solved = [solved_0, solved_1]
    returned = [
        exchange(z, solved[f], slots).reshape(z.devices * slots, z.local, z.width)
        for f in range(z.fields)
    ]
    outside = [*beside(z, *rims(z, place, mate, returned[0], 0))]
    outs = unpack(z, place, mate, returned[0], 0, ())
    last, *outs = lax.optimization_barrier((returned[1], *outs))
    outside.extend(beside(z, *rims(z, place, mate, last, 1)))
    grid, slope = unpack(z, place, mate, last, 1, outs)
    return grid, edges(z, slope, grid, outside)


def plain_body(z, grid_field, inverses, degree_start):
    index = np.arange(z.degrees)
    counts = np.asarray(z.counts)
    degree_of = np.repeat(index, counts)
    place_in = np.arange(z.blocks) - np.asarray(z.starts)[degree_of]
    value = z.spacing * (index + 1) - 1
    slot_place = degree_start[degree_of] + jnp.asarray(place_in, jnp.int32)
    total = z.devices * z.capacity
    holder = jnp.full((total,), z.blocks, jnp.int32)
    holder = holder.at[slot_place].set(jnp.arange(z.blocks, dtype=jnp.int32))
    sent = jnp.take(grid_field, holder, axis=2, mode="fill", fill_value=0)
    sent = sent.reshape(z.fields, z.local, z.devices, z.capacity, z.width)
    columns = lax.all_to_all(sent, AXES, split_axis=2, concat_axis=1, tiled=True)
    columns = columns.reshape(z.fields, z.levels, z.capacity, z.width)
    device = lax.axis_index(AXES)
    mine = lax.dynamic_slice_in_dim(holder, device * z.capacity, z.capacity)
    order = jnp.asarray(place_in)[:, None] * OB + np.arange(z.width)[None, :] // 2
    live_table = (order <= jnp.asarray(value[degree_of])[:, None]).astype(jnp.float32)
    live = jnp.take(live_table, mine, axis=0, mode="fill", fill_value=0)
    factor = (value * (value + 1)).astype(np.float32)[degree_of]
    factor = jnp.take(jnp.asarray(factor), mine, mode="fill", fill_value=0)
    upper = jnp.take(jnp.asarray(degree_of >= z.degrees // 2), mine, mode="fill", fill_value=False)
    radius = inner_radius + shell_depth * jnp.arange(z.levels + 2, dtype=jnp.float32) / (z.levels + 1)
    here = radius[1:-1][None, :, None, None]
    padded = jnp.pad(columns.astype(jnp.float32), ((0, 0), (1, 1), (0, 0), (0, 0)))
    weighted = padded * radius[None, :, None, None]
    second = (weighted[:, 2:] - 2.0 * weighted[:, 1:-1] + weighted[:, :-2]) / here
    scaled = (shell_depth / (z.levels + 1)) / here
    centre = padded[:, 1:-1]
    strength = jnp.asarray(diffusion_numbers, jnp.float32)[:, None, None, None]
    angular = factor[None, None, :, None] * (scaled * scaled) * centre
    rhs = (centre + strength * (second - angular)) * live[None, None]

    def solve_slot(carry, at):
        matrix = lax.dynamic_index_in_dim(
            inverses, upper[at].astype(jnp.int32), 1, keepdims=False
        ).astype(jnp.float32)
        block = lax.dynamic_index_in_dim(rhs, at, 2, keepdims=False)
        product = jnp.einsum("fij,fjc->fic", matrix, block, precision=lax.Precision.HIGHEST)
        return carry, product.astype(jnp.bfloat16)

    solved = lax.scan(solve_slot, 0, jnp.arange(z.capacity))[1]
    solved = jnp.moveaxis(solved, 0, 2)
    solved = solved.reshape(z.fields, z.devices, z.local, z.capacity, z.width)
    returned = lax.all_to_all(solved, AXES, split_axis=1, concat_axis=3, tiled=True)
    returned = returned.reshape(z.fields, z.local, total, z.width)
    grid = jnp.take(returned, slot_place, axis=2)
    before, after = beside(z, grid[:, :1], grid[:, -1:])
    rimmed = jnp.concatenate([before, grid, after], axis=1).astype(jnp.float32)
    return grid, (0.5 * (rimmed[:, 2:] - rimmed[:, :-2])).astype(jnp.bfloat16)


def solution(mesh):
    in_specs = (P(None, AXES), P(None, AXES), P(), P())
    out_specs = (P(None, AXES), P(None, AXES))
    return jax.shard_map(body, mesh=mesh, in_specs=in_specs, out_specs=out_specs, check_vma=False)
```

```python
import functools

import jax
import jax.numpy as jnp
import numpy as np
from jax import lax
from jax.experimental import pallas as pl
from jax.experimental.pallas import tpu as pltpu
from jax.sharding import PartitionSpec as P

LMAX1 = 1024
OB = 64
AXES = ("rad", "lm")
PLANE = 8
GIFT = 8
GROUP = 16
VMEM = 48 << 20
MORE_VMEM = 60 << 20
RIDES = 8
PARTS = 4

inner_radius = 0.35
shell_depth = 0.65
diffusion_numbers = (0.9, 0.4)


def quotient(value, divisor, bound):
    numbers = np.arange(bound)
    for shift in range(24):
        factor = -(-(1 << shift) // divisor)
        if bound * factor < 2**31 and np.all(numbers * factor >> shift == numbers // divisor):
            return lax.shift_right_logical(value * factor, jnp.int32(shift))
    return lax.div(value, divisor)


class Sizes:
    def __init__(self, devices, grid_field, inverses, slot_blocks):
        self.devices = devices
        self.fields, self.local, self.blocks, self.width = grid_field.shape
        self.levels = inverses.shape[-1]
        self.capacity = slot_blocks.shape[1]
        self.degrees = 2 * devices
        self.spacing = LMAX1 // self.degrees
        self.group_size = OB * self.degrees // LMAX1
        index = np.arange(self.degrees)
        self.counts = [int(c) for c in index // self.group_size + 1]
        self.starts = [int(s) for s in np.cumsum(self.counts) - self.counts]
        self.partial = [q for q in range(self.degrees) if (q + 1) % self.group_size]

    def turns(self, q):
        return quotient(q, self.group_size, self.degrees)

    def owner(self, slot):
        return quotient(slot, self.capacity, self.devices * self.capacity)

    def last_block(self, q):
        turns = self.turns(q)
        rest = q - turns * self.group_size
        whole = lax.shift_right_logical(self.group_size * turns * (turns + 1), 1)
        return whole + rest * (turns + 1) + turns

    def last_live(self, q):
        return 2 * self.spacing * (q - self.turns(q) * self.group_size + 1)


def slot_choices(z):
    mean = -(-z.blocks // z.devices)
    return sorted({min(mean + extra, z.capacity) for extra in (0, 1, 2, 3)} | {z.capacity})


def plan_kernel(z, choices, start_ref, choice_ref, mate_ref, load_ref, high_ref, count_ref, stack_ref):
    half = z.degrees // 2
    planes = z.devices // PLANE
    kinds = z.group_size
    owner = [z.owner(start_ref[q]) for q in range(z.degrees)]
    for q in range(half, z.degrees):
        load_ref[owner[q]] = start_ref[q] - owner[q] * z.capacity + z.counts[q]
        high_ref[owner[q]] = q
    for i in range(planes * kinds):
        count_ref[i] = 0
    for q in range(z.degrees):
        mate_ref[q] = -1
    for q in z.partial:
        if q < half:
            kind = quotient(owner[q], PLANE, z.devices) * kinds + q % kinds
            stack_ref[kind * PLANE + count_ref[kind]] = q
            count_ref[kind] += 1
    for q in sorted(z.partial, key=lambda q: -(q % kinds)):
        if q < half:
            continue
        first_kind = quotient(owner[q], PLANE, z.devices) * kinds
        kind = jnp.int32(-1)
        for i in range(kinds - 1 - q % kinds):
            kind = jnp.where(count_ref[first_kind + i] > 0, first_kind + i, kind)

        @pl.when(kind >= 0)
        def _(kind=kind, q=q):
            left = count_ref[kind] - 1
            count_ref[kind] = left
            host = stack_ref[kind * PLANE + left]
            mate_ref[q] = host
            mate_ref[host] = q
            load_ref[owner[q]] -= 1

    totals = plane_totals(z, load_ref)
    most = functools.reduce(jnp.maximum, [totals[g] + totals[g + 1] for g in range(0, planes, 2)])
    highest = functools.reduce(jnp.maximum, totals)
    choice = jnp.int32(0)
    for i in range(1, len(choices)):
        tried = choices[i - 1]
        beyond = (most > 2 * PLANE * tried) | (highest > PLANE * tried + GIFT * PLANE // 2)
        choice = jnp.where(beyond, i, choice)
    choice_ref[0] = choice


def plane_totals(z, load_ref):
    return [
        sum(load_ref[g * PLANE + e] for e in range(PLANE)) for g in range(z.devices // PLANE)
    ]


def plan(z, degree_start, choices):
    smem = pl.BlockSpec(memory_space=pltpu.SMEM)
    kinds = z.devices // PLANE * z.group_size
    return pl.pallas_call(
        functools.partial(plan_kernel, z, choices),
        in_specs=[smem],
        out_specs=[smem] * 4,
        out_shape=[
            jax.ShapeDtypeStruct((size,), jnp.int32)
            for size in (1, z.degrees, z.devices, z.devices)
        ],
        scratch_shapes=[pltpu.SMEM((kinds,), jnp.int32), pltpu.SMEM((kinds * PLANE,), jnp.int32)],
        name="plan",
    )(degree_start)


def assign(z, slots, start_ref, mate_ref, load_ref, high_ref, place_ref, kept_ref, room_ref):
    totals = plane_totals(z, load_ref)
    for d in range(z.devices):
        excess = totals[d // PLANE] - PLANE * slots - GIFT * (d % PLANE // 2)
        gift = jnp.int32(0) if d % 2 else jnp.clip(excess, 0, GIFT)
        kept_ref[d] = load_ref[d] - gift
        room_ref[d ^ PLANE] = slots - gift
    for q in range(z.degrees):
        first = start_ref[q] + z.owner(start_ref[q]) * (slots - z.capacity)
        for p in range(z.counts[q]):
            place_ref[z.starts[q] + p] = first + p
    for d in range(z.devices):
        if d % PLANE == 0:
            spare = (jnp.int32(d), kept_ref[d])
        q = high_ref[d]
        last = z.last_block(q)
        first = last - z.turns(q)
        offset = start_ref[q] - d * z.capacity
        kept = kept_ref[d] - offset

        def move(state, first=first):
            p, device, slot = state
            place_ref[first + p] = device * slots + slot
            fits = slot < room_ref[device]
            after = device + 1
            return (
                jnp.where(fits, p + 1, p),
                jnp.where(fits, device, after),
                jnp.where(fits, slot + 1, kept_ref[jnp.minimum(after, z.devices - 1)]),
            )

        spare = lax.while_loop(
            lambda state, kept=kept: state[0] < kept, move, (room_ref[d] - offset, *spare)
        )[1:]
        host = mate_ref[q]
        if d % 2 == 0:
            other = d ^ PLANE
            given = other * slots + room_ref[other] - kept

            def give(p, carry, given=given, first=first):
                place_ref[first + p] = given + p
                return carry

            lax.fori_loop(kept, last - first + 1 - jnp.where(host >= 0, 1, 0), give, 0)
        start = start_ref[jnp.maximum(host, 0)]
        shared = start + z.owner(start) * (slots - z.capacity) + z.turns(host)
        place_ref[last] = jnp.where(host >= 0, shared, place_ref[last])


def swap(value, axis, bit):
    size = lax.axis_size(axis)
    return lax.ppermute(value, axis, [(i, i ^ bit) for i in range(size)])


def straight_inverses(inverses):
    own = inverses[:, 1]
    rad, lm = lax.axis_size("rad"), lax.axis_size("lm")
    facing = [(d, d ^ PLANE) for d in range(0, rad * lm, 2)]
    return own, swap(own, "lm", 2), swap(own, "rad", 1), lax.ppermute(own, AXES, facing)


def other_core(values):
    return [swap(value, "lm", 1) for value in values]


def riding(z, mate_ref, q):
    b, host = z.last_block(q), mate_ref[q]
    rides = host >= 0
    host = jnp.maximum(host, 0)
    return b, jnp.where(rides, z.last_block(host), b), jnp.where(rides, z.last_live(host), z.width)


def pack_kernel(z, f, slots, *refs):
    if f:
        place_ref, mate_ref, field_ref, out_ref, holder_ref, part_ref, wide_ref, sems = refs
    else:
        start_ref, mate_ref, load_ref, high_ref, field_ref, out_ref, place_ref = refs[:7]
        part_ref, wide_ref, sems, kept_ref, room_ref = refs[7:]
    pitch = z.blocks + 1
    some = z.local // PARTS
    copies = [
        pltpu.make_async_copy(
            field_ref.at[f, pl.ds(i * some, some)], part_ref.at[pl.ds(i * some, some)], sems.at[i]
        )
        for i in range(PARTS)
    ]
    for copy in copies:
        copy.start()
    if not f:
        assign(z, slots, start_ref, mate_ref, load_ref, high_ref, place_ref, kept_ref, room_ref)
    for level in range(z.local):
        if level % some == 0:
            copies[level // some].wait()
        wide_ref[pl.ds(level * pitch, z.blocks), :] = part_ref[level].astype(jnp.float32)

    def group(g, carry):
        for k in range(GROUP):
            b = g * GROUP + k
            tile = wide_ref[pl.ds(b, z.local, stride=pitch), :]
            out_ref[place_ref[b]] = tile.astype(jnp.bfloat16)
        return carry

    lax.fori_loop(0, z.blocks // GROUP, group, 0)
    column = lax.broadcasted_iota(jnp.int32, (z.local, z.width), 1)

    def ride(q, carry):
        b, host_block, live = riding(z, mate_ref, q)
        rider = pltpu.roll(wide_ref[pl.ds(b, z.local, stride=pitch), :], live, 1)
        tile = wide_ref[pl.ds(host_block, z.local, stride=pitch), :]
        out_ref[place_ref[b]] = jnp.where(column < live, tile, rider).astype(jnp.bfloat16)
        return carry

    lax.fori_loop(z.degrees // 2, z.degrees, ride, 0, unroll=RIDES)
    if not f:
        return

    def clear(k, carry):
        holder_ref[k] = 0
        return carry

    lax.fori_loop(0, z.devices * z.capacity, clear, 0, unroll=8)

    def degree(q, b):
        def block(p, inner):
            holder_ref[place_ref[b + p]] = q * OB + p
            return inner

        count = z.turns(q) + 1
        rides = (q >= z.degrees // 2) & (mate_ref[q] >= 0)
        lax.fori_loop(0, count - jnp.where(rides, 1, 0), block, 0)
        return b + count

    lax.fori_loop(0, z.degrees, degree, 0)


def pack(z, grid_field, f, slots, *tables):
    total = z.devices * slots
    smem = pl.BlockSpec(memory_space=pltpu.SMEM)
    table = jax.ShapeDtypeStruct((z.devices * z.capacity if f else z.blocks,), jnp.int32)
    return pl.pallas_call(
        functools.partial(pack_kernel, z, f, slots),
        in_specs=[smem] * len(tables) + [pl.BlockSpec(memory_space=pl.ANY)],
        out_specs=[pl.BlockSpec(memory_space=pltpu.VMEM), smem],
        out_shape=[jax.ShapeDtypeStruct((total, z.local, z.width), jnp.bfloat16), table],
        scratch_shapes=[
            pltpu.VMEM((z.local, z.blocks, z.width), jnp.bfloat16),
            pltpu.VMEM((z.local * (z.blocks + 1), z.width), jnp.float32),
            pltpu.SemaphoreType.DMA((PARTS,)),
        ]
        + [pltpu.SMEM((z.devices,), jnp.int32)] * (0 if f else 2),
        compiler_params=pltpu.CompilerParams(vmem_limit_bytes=VMEM),
        cost_estimate=pl.CostEstimate(flops=10**9, bytes_accessed=10**7, transcendentals=0),
        name=f"pack_{f}",
    )(*tables, grid_field)


def solve_kernel(z, f, slots, per_step, holder_ref, start_ref, mate_ref, me_ref, columns_ref, inverses_ref, *rest):
    (own, across, along, corner, own_odd, across_odd, along_odd, corner_odd, far) = rest[:9]
    out_ref, matrix_ref, square_ref, above_ref, below_ref, sems = rest[9:]
    strength = diffusion_numbers[f]
    step = pl.program_id(0)
    shape = (z.levels, z.width)
    me = me_ref[0]

    @pl.when(step == 0)
    def _():
        sources = [
            own.at[f], own_odd.at[f], across.at[f], across_odd.at[f],
            along.at[f], along_odd.at[f], corner.at[0], corner_odd.at[0],
            inverses_ref.at[f, 0], far.at[f],
        ]
        copies = [
            pltpu.make_async_copy(source, matrix_ref.at[i], sems.at[i])
            for i, source in enumerate(sources)
        ]
        for copy in copies:
            copy.start()
        level = lax.broadcasted_iota(jnp.int32, shape, 0)

        def radius(positions):
            return inner_radius + shell_depth * (positions + 1).astype(jnp.float32) / (z.levels + 1)

        here = radius(level)
        scaled = (shell_depth / (z.levels + 1)) / here
        square_ref[...] = strength * (scaled * scaled)
        above_ref[...] = jnp.where(level == z.levels - 1, 0.0, strength * radius(level + 1) / here)
        below_ref[...] = jnp.where(level == 0, 0.0, strength * radius(level - 1) / here)
        for copy in copies:
            copy.wait()

    column = lax.broadcasted_iota(jnp.int32, shape, 1)
    host = quotient(holder_ref[me * slots], OB, z.degrees * OB)
    rider = mate_ref[host]
    host_at = z.turns(host) - step * per_step
    rides = (rider >= 0) & (host_at >= 0) & (host_at < per_step)

    def block(i, carry):
        again = i >= per_step
        k = jnp.where(again, host_at, i)
        code = holder_ref[me * slots + jnp.minimum(step * per_step + k, slots - 1)]
        q = jnp.where(again, rider, quotient(code, OB, z.degrees * OB))
        value = z.spacing * (q + 1) - 1
        last = value - lax.rem(code, OB) * (z.width // 2)
        begin = jnp.where(again, z.last_live(host), 0)
        end = jnp.where(again, begin + z.last_live(rider), 2 * last + 2)
        offset = z.owner(start_ref[q]) ^ me
        which = jnp.where(offset < PLANE, offset, PLANE + 1)
        which = jnp.where(q >= z.degrees // 2, which, PLANE)
        factor = (value * (value + 1)).astype(jnp.float32)
        u = columns_ref[:, k].reshape(shape).astype(jnp.float32)
        u = jnp.where((column >= begin) & (column < end), u, 0.0)
        weight = (1.0 - 2.0 * strength) - factor * square_ref[...]
        rhs = weight * u
        rhs += above_ref[...] * pltpu.roll(u, z.levels - 1, 0)
        rhs += below_ref[...] * pltpu.roll(u, 1, 0)
        high = rhs.astype(jnp.bfloat16)
        low = (rhs - high.astype(jnp.float32)).astype(jnp.bfloat16)
        both = jnp.concatenate([high, low], axis=1)
        product = jnp.dot(matrix_ref[which], both, preferred_element_type=jnp.float32)
        solved = product[:, : z.width] + product[:, z.width :]
        earlier = out_ref[:, k].reshape(shape).astype(jnp.float32)
        solved = jnp.where(column >= begin, solved, earlier).astype(jnp.bfloat16)
        out_ref[:, k] = solved.reshape(z.devices, z.local, z.width)
        return carry

    lax.fori_loop(0, per_step + jnp.where(rides, 1, 0), block, 0)


def solve(z, holder, degree_start, mate, me, columns, inverses, pieces, f, slots):
    steps = pl.cdiv(slots, 5)
    per_step = pl.cdiv(slots, steps)
    block = (z.devices, per_step, z.local, z.width)
    spec = pl.BlockSpec(block, lambda i, *s: (0, i, 0, 0))
    return pl.pallas_call(
        functools.partial(solve_kernel, z, f, slots, per_step),
        grid_spec=pltpu.PrefetchScalarGridSpec(
            num_scalar_prefetch=4,
            grid=(steps,),
            in_specs=[spec] + [pl.BlockSpec(memory_space=pl.ANY)] * (1 + len(pieces)),
            out_specs=spec,
            scratch_shapes=[pltpu.VMEM((PLANE + 2, z.levels, z.levels), jnp.bfloat16)]
            + [pltpu.VMEM((z.levels, z.width), jnp.float32)] * 3
            + [pltpu.SemaphoreType.DMA((PLANE + 2,))],
        ),
        out_shape=jax.ShapeDtypeStruct(columns.shape, jnp.bfloat16),
        compiler_params=pltpu.CompilerParams(vmem_limit_bytes=VMEM),
        cost_estimate=pl.CostEstimate(flops=10**10, bytes_accessed=10**7, transcendentals=0),
        name=f"solve_{f}",
    )(holder, degree_start, mate, me, columns, inverses, *pieces)


def unpack_kernel(z, f, place_ref, mate_ref, returned_ref, *rest):
    grid_ref, slope_ref, level_ref, inner_ref, wide_ref, sems = rest[-6:]
    pitch = z.blocks + 1

    def gather(g, carry):
        for k in range(GROUP):
            b = g * GROUP + k
            tile = returned_ref[place_ref[b]].astype(jnp.float32)
            wide_ref[pl.ds(b, z.local, stride=pitch), :] = tile
        return carry

    lax.fori_loop(0, z.blocks // GROUP, gather, 0)
    column = lax.broadcasted_iota(jnp.int32, (z.local, z.width), 1)

    def ride(q, carry):
        b, host_block, live = riding(z, mate_ref, q)
        tile = returned_ref[place_ref[b]].astype(jnp.float32)
        rider = pltpu.roll(tile, z.width - live, 1)
        host_rows = pl.ds(host_block, z.local, stride=pitch)
        wide_ref[host_rows, :] = jnp.where(column < live, tile, 0.0)
        rows = pl.ds(b, z.local, stride=pitch)
        wide_ref[rows, :] = jnp.where(column < z.last_live(q), rider, 0.0)
        return carry

    lax.fori_loop(z.degrees // 2, z.degrees, ride, 0, unroll=RIDES)

    def group(g, carry):
        at = pl.multiple_of(g * GROUP, GROUP)
        rows = pl.ds(at, GROUP)
        value = [wide_ref[pl.ds(at + i * pitch, GROUP), :] for i in range(z.local)]
        for i in range(z.local):
            level_ref[i, rows, :] = value[i].astype(jnp.bfloat16)
        for i in range(1, z.local - 1):
            slope = 0.5 * (value[i + 1] - value[i - 1])
            inner_ref[i - 1, rows, :] = slope.astype(jnp.bfloat16)
        return carry

    groups = z.blocks // GROUP
    copies = []
    for i in range(PARTS):
        begin, end = i * groups // PARTS, (i + 1) * groups // PARTS
        lax.fori_loop(begin, end, group, 0)
        rows = pl.ds(begin * GROUP, (end - begin) * GROUP)
        copies += [
            pltpu.make_async_copy(
                level_ref.at[:, rows, :], grid_ref.at[f, :, rows, :], sems.at[2 * i]
            ),
            pltpu.make_async_copy(
                inner_ref.at[:, rows, :],
                slope_ref.at[f, pl.ds(1, z.local - 2), rows, :],
                sems.at[2 * i + 1],
            ),
        ]
        for copy in copies[-2:]:
            copy.start()
    for copy in copies:
        copy.wait()


def unpack(z, place, mate, returned, f, earlier):
    whole = jax.ShapeDtypeStruct((z.fields, z.local, z.blocks, z.width), jnp.bfloat16)
    smem, anywhere = pl.BlockSpec(memory_space=pltpu.SMEM), pl.BlockSpec(memory_space=pl.ANY)
    return pl.pallas_call(
        functools.partial(unpack_kernel, z, f),
        in_specs=[smem, smem, pl.BlockSpec(memory_space=pltpu.VMEM)] + [anywhere] * len(earlier),
        out_specs=[anywhere] * 2,
        out_shape=[whole, whole],
        scratch_shapes=[
            pltpu.VMEM((z.local, z.blocks, z.width), jnp.bfloat16),
            pltpu.VMEM((z.local - 2, z.blocks, z.width), jnp.bfloat16),
            pltpu.VMEM((z.local * (z.blocks + 1), z.width), jnp.float32),
            pltpu.SemaphoreType.DMA((2 * PARTS,)),
        ],
        input_output_aliases={3 + i: i for i in range(len(earlier))},
        compiler_params=pltpu.CompilerParams(vmem_limit_bytes=VMEM if earlier else MORE_VMEM),
        cost_estimate=pl.CostEstimate(flops=10**9, bytes_accessed=10**7, transcendentals=0),
        name=f"unpack_{f}",
    )(place, mate, returned, *earlier)


def rim_kernel(z, place_ref, mate_ref, returned_ref, first_ref, last_ref, first_wide_ref, last_wide_ref):
    sides = ((first_wide_ref, 0), (last_wide_ref, z.local - 1))

    def gather(g, carry):
        for k in range(GROUP):
            b = g * GROUP + k
            tile = returned_ref[place_ref[b]].astype(jnp.float32)
            for wide_ref, row in sides:
                wide_ref[pl.ds(b, 1), :] = tile[row : row + 1]
        return carry

    lax.fori_loop(0, z.blocks // GROUP, gather, 0)
    column = lax.broadcasted_iota(jnp.int32, (z.local, z.width), 1)

    def ride(q, carry):
        b, host_block, live = riding(z, mate_ref, q)
        tile = returned_ref[place_ref[b]].astype(jnp.float32)
        rider = pltpu.roll(tile, z.width - live, 1)
        rider = jnp.where(column < z.last_live(q), rider, 0.0)
        tile = jnp.where(column < live, tile, 0.0)
        for wide_ref, row in sides:
            wide_ref[pl.ds(host_block, 1), :] = tile[row : row + 1]
            wide_ref[pl.ds(b, 1), :] = rider[row : row + 1]
        return carry

    lax.fori_loop(z.degrees // 2, z.degrees, ride, 0, unroll=RIDES)
    first_ref[0] = first_wide_ref[...].astype(jnp.bfloat16)
    last_ref[0] = last_wide_ref[...].astype(jnp.bfloat16)


def rims(z, place, mate, returned, f):
    level = jax.ShapeDtypeStruct((1, z.blocks, z.width), jnp.bfloat16)
    spec = pl.BlockSpec(level.shape, lambda i, *s: (0, 0, 0))
    return pl.pallas_call(
        functools.partial(rim_kernel, z),
        grid_spec=pltpu.PrefetchScalarGridSpec(
            num_scalar_prefetch=2,
            grid=(1,),
            in_specs=[pl.BlockSpec(returned.shape, lambda i, *s: (0, 0, 0))],
            out_specs=[spec, spec],
            scratch_shapes=[pltpu.VMEM((z.blocks, z.width), jnp.float32)] * 2,
        ),
        out_shape=[level, level],
        compiler_params=pltpu.CompilerParams(vmem_limit_bytes=VMEM if f else MORE_VMEM),
        cost_estimate=pl.CostEstimate(flops=10**8, bytes_accessed=3 * 10**6, transcendentals=0),
        name=f"rims_{f}",
    )(place, mate, returned)


def edge_kernel(z, *refs):
    count = 4 * z.fields
    inner, outer, (_, slope_ref, edge_ref, sems) = refs[: count // 2], refs[count // 2 : count], refs[count:]
    copies = []
    for i in range(2 * z.fields):
        inside = inner[i][...].reshape(z.blocks, z.width).astype(jnp.float32)
        outside = outer[i][...].reshape(z.blocks, z.width).astype(jnp.float32)
        slope = inside - outside if i % 2 == 0 else outside - inside
        edge_ref[i] = (0.5 * slope).astype(jnp.bfloat16)
        level = i % 2 * (z.local - 1)
        copies.append(pltpu.make_async_copy(edge_ref.at[i], slope_ref.at[i // 2, level], sems.at[i]))
        copies[i].start()
    for copy in copies:
        copy.wait()


def edges(z, slope, grid, outside):
    def inner(f, level):
        return pl.BlockSpec((1, 1, z.blocks, z.width), lambda i: (f, level, 0, 0))

    inner_specs = [inner(f, level) for f in range(z.fields) for level in (1, z.local - 2)]
    outer_spec = pl.BlockSpec((1, z.blocks, z.width), lambda i: (0, 0, 0))
    count = len(inner_specs)
    return pl.pallas_call(
        functools.partial(edge_kernel, z),
        grid=(1,),
        in_specs=inner_specs + [outer_spec] * count + [pl.BlockSpec(memory_space=pl.ANY)],
        out_specs=pl.BlockSpec(memory_space=pl.ANY),
        out_shape=jax.ShapeDtypeStruct(slope.shape, slope.dtype),
        scratch_shapes=[
            pltpu.VMEM((count, z.blocks, z.width), jnp.bfloat16),
            pltpu.SemaphoreType.DMA((count,)),
        ],
        input_output_aliases={2 * count: 0},
        compiler_params=pltpu.CompilerParams(vmem_limit_bytes=VMEM),
        name="edges",
    )(*[grid] * count, *outside, slope)


def beside(z, first, last):
    up = [(i, i + 1) for i in range(z.devices - 1)]
    down = [(j, i) for i, j in up]
    return lax.ppermute(last, AXES, up), lax.ppermute(first, AXES, down)


def exchange(z, value, slots):
    shaped = value.reshape(z.devices, slots, z.local, z.width)
    return lax.all_to_all(shaped, AXES, split_axis=0, concat_axis=0, tiled=True)


def body(grid_field, inverses, slot_blocks, degree_start):
    rad, lm = lax.axis_size("rad"), lax.axis_size("lm")
    z = Sizes(rad * lm, grid_field, inverses, slot_blocks)
    choices = slot_choices(z)
    kernels = z.local % 16 == 0 and z.fields == 2 and z.blocks % GROUP == 0 and rad % 4 == 0 and lm == PLANE // 2
    low, high = z.counts[z.degrees // 2 - 1 : z.degrees // 2 + 1]
    if not kernels or low + GIFT > choices[0] or high <= GIFT or z.capacity - choices[0] > GIFT:
        return plain_body(z, grid_field, inverses, degree_start)
    me = lax.axis_index(AXES).reshape(1).astype(jnp.int32)
    choice, *tables = plan(z, degree_start, choices)
    routes = [functools.partial(route, z, slots) for slots in choices]
    return lax.switch(choice[0], routes, grid_field, inverses, degree_start, me, *tables)


def route(z, slots, grid_field, inverses, degree_start, me, mate, load, high):
    sent_0, place = pack(z, grid_field, 0, slots, degree_start, mate, load, high)
    sent_1, holder = pack(z, grid_field, 1, slots, place, mate)
    sent_1, own, across, along, far = lax.optimization_barrier(
        (sent_1, *straight_inverses(inverses))
    )
    columns = [exchange(z, sent, slots) for sent in (sent_0, sent_1)]
    corner_0 = swap(across[:1], "rad", 1)
    even = [own, across, along]
    odd = other_core(even)
    pieces = lax.optimization_barrier((*even, corner_0, *odd, *other_core([corner_0]), far))
    solved_0 = solve(z, holder, degree_start, mate, me, columns[0], inverses, pieces, 0, slots)
    corner_1 = swap(along[1:], "lm", 2)
    pieces = (*even, corner_1, *odd, *other_core([corner_1]), far)
    solved_1 = solve(z, holder, degree_start, mate, me, columns[1], inverses, pieces, 1, slots)
    solved = [solved_0, solved_1]
    returned = [
        exchange(z, solved[f], slots).reshape(z.devices * slots, z.local, z.width)
        for f in range(z.fields)
    ]
    outside = [*beside(z, *rims(z, place, mate, returned[0], 0))]
    outs = unpack(z, place, mate, returned[0], 0, ())
    last, *outs = lax.optimization_barrier((returned[1], *outs))
    outside.extend(beside(z, *rims(z, place, mate, last, 1)))
    grid, slope = unpack(z, place, mate, last, 1, outs)
    return grid, edges(z, slope, grid, outside)


def plain_body(z, grid_field, inverses, degree_start):
    index = np.arange(z.degrees)
    counts = np.asarray(z.counts)
    degree_of = np.repeat(index, counts)
    place_in = np.arange(z.blocks) - np.asarray(z.starts)[degree_of]
    value = z.spacing * (index + 1) - 1
    slot_place = degree_start[degree_of] + jnp.asarray(place_in, jnp.int32)
    total = z.devices * z.capacity
    holder = jnp.full((total,), z.blocks, jnp.int32)
    holder = holder.at[slot_place].set(jnp.arange(z.blocks, dtype=jnp.int32))
    sent = jnp.take(grid_field, holder, axis=2, mode="fill", fill_value=0)
    sent = sent.reshape(z.fields, z.local, z.devices, z.capacity, z.width)
    columns = lax.all_to_all(sent, AXES, split_axis=2, concat_axis=1, tiled=True)
    columns = columns.reshape(z.fields, z.levels, z.capacity, z.width)
    device = lax.axis_index(AXES)
    mine = lax.dynamic_slice_in_dim(holder, device * z.capacity, z.capacity)
    order = jnp.asarray(place_in)[:, None] * OB + np.arange(z.width)[None, :] // 2
    live_table = (order <= jnp.asarray(value[degree_of])[:, None]).astype(jnp.float32)
    live = jnp.take(live_table, mine, axis=0, mode="fill", fill_value=0)
    factor = (value * (value + 1)).astype(np.float32)[degree_of]
    factor = jnp.take(jnp.asarray(factor), mine, mode="fill", fill_value=0)
    upper = jnp.take(jnp.asarray(degree_of >= z.degrees // 2), mine, mode="fill", fill_value=False)
    radius = inner_radius + shell_depth * jnp.arange(z.levels + 2, dtype=jnp.float32) / (z.levels + 1)
    here = radius[1:-1][None, :, None, None]
    padded = jnp.pad(columns.astype(jnp.float32), ((0, 0), (1, 1), (0, 0), (0, 0)))
    weighted = padded * radius[None, :, None, None]
    second = (weighted[:, 2:] - 2.0 * weighted[:, 1:-1] + weighted[:, :-2]) / here
    scaled = (shell_depth / (z.levels + 1)) / here
    centre = padded[:, 1:-1]
    strength = jnp.asarray(diffusion_numbers, jnp.float32)[:, None, None, None]
    angular = factor[None, None, :, None] * (scaled * scaled) * centre
    rhs = (centre + strength * (second - angular)) * live[None, None]

    def solve_slot(carry, at):
        matrix = lax.dynamic_index_in_dim(
            inverses, upper[at].astype(jnp.int32), 1, keepdims=False
        ).astype(jnp.float32)
        block = lax.dynamic_index_in_dim(rhs, at, 2, keepdims=False)
        product = jnp.einsum("fij,fjc->fic", matrix, block, precision=lax.Precision.HIGHEST)
        return carry, product.astype(jnp.bfloat16)

    solved = lax.scan(solve_slot, 0, jnp.arange(z.capacity))[1]
    solved = jnp.moveaxis(solved, 0, 2)
    solved = solved.reshape(z.fields, z.devices, z.local, z.capacity, z.width)
    returned = lax.all_to_all(solved, AXES, split_axis=1, concat_axis=3, tiled=True)
    returned = returned.reshape(z.fields, z.local, total, z.width)
    grid = jnp.take(returned, slot_place, axis=2)
    before, after = beside(z, grid[:, :1], grid[:, -1:])
    rimmed = jnp.concatenate([before, grid, after], axis=1).astype(jnp.float32)
    return grid, (0.5 * (rimmed[:, 2:] - rimmed[:, :-2])).astype(jnp.bfloat16)


def solution(mesh):
    in_specs = (P(None, AXES), P(None, AXES), P(), P())
    out_specs = (P(None, AXES), P(None, AXES))
    return jax.shard_map(body, mesh=mesh, in_specs=in_specs, out_specs=out_specs, check_vma=False)
```

```python
import functools

import jax
import jax.numpy as jnp
import numpy as np
from jax import lax
from jax.experimental import pallas as pl
from jax.experimental.pallas import tpu as pltpu
from jax.sharding import PartitionSpec as P

LMAX1 = 1024
OB = 64
AXES = ("rad", "lm")
PLANE = 8
GIFT = 8
GROUP = 16
BATCH = 34
VMEM = 48 << 20
MORE_VMEM = 60 << 20
RIDES = 16
PARTS = 4

inner_radius = 0.35
shell_depth = 0.65
diffusion_numbers = (0.9, 0.4)


def quotient(value, divisor, bound):
    numbers = np.arange(bound)
    for shift in range(24):
        factor = -(-(1 << shift) // divisor)
        if bound * factor < 2**31 and np.all(numbers * factor >> shift == numbers // divisor):
            return lax.shift_right_logical(value * factor, jnp.int32(shift))
    return lax.div(value, divisor)


class Sizes:
    def __init__(self, devices, grid_field, inverses, slot_blocks):
        self.devices = devices
        self.fields, self.local, self.blocks, self.width = grid_field.shape
        self.levels = inverses.shape[-1]
        self.capacity = slot_blocks.shape[1]
        self.degrees = 2 * devices
        self.spacing = LMAX1 // self.degrees
        self.group_size = OB * self.degrees // LMAX1
        index = np.arange(self.degrees)
        self.counts = [int(c) for c in index // self.group_size + 1]
        self.starts = [int(s) for s in np.cumsum(self.counts) - self.counts]
        self.partial = [q for q in range(self.degrees) if (q + 1) % self.group_size]

    def turns(self, q):
        return quotient(q, self.group_size, self.degrees)

    def owner(self, slot):
        return quotient(slot, self.capacity, self.devices * self.capacity)

    def last_block(self, q):
        turns = self.turns(q)
        rest = q - turns * self.group_size
        whole = lax.shift_right_logical(self.group_size * turns * (turns + 1), 1)
        return whole + rest * (turns + 1) + turns

    def last_live(self, q):
        return 2 * self.spacing * (q - self.turns(q) * self.group_size + 1)


def slot_choices(z):
    mean = -(-z.blocks // z.devices)
    return sorted({min(mean + extra, z.capacity) for extra in (0, 1, 2, 3)} | {z.capacity})


def plan_kernel(z, choices, start_ref, choice_ref, mate_ref, load_ref, high_ref, count_ref, stack_ref):
    half = z.degrees // 2
    planes = z.devices // PLANE
    kinds = z.group_size
    owner = [z.owner(start_ref[q]) for q in range(z.degrees)]
    for q in range(half, z.degrees):
        load_ref[owner[q]] = start_ref[q] - owner[q] * z.capacity + z.counts[q]
        high_ref[owner[q]] = q
    for i in range(planes * kinds):
        count_ref[i] = 0
    for q in range(z.degrees):
        mate_ref[q] = -1
    for q in z.partial:
        if q < half:
            kind = quotient(owner[q], PLANE, z.devices) * kinds + q % kinds
            stack_ref[kind * PLANE + count_ref[kind]] = q
            count_ref[kind] += 1
    for q in sorted(z.partial, key=lambda q: -(q % kinds)):
        if q < half:
            continue
        first_kind = quotient(owner[q], PLANE, z.devices) * kinds
        kind = jnp.int32(-1)
        for i in range(kinds - 1 - q % kinds):
            kind = jnp.where(count_ref[first_kind + i] > 0, first_kind + i, kind)

        @pl.when(kind >= 0)
        def _(kind=kind, q=q):
            left = count_ref[kind] - 1
            count_ref[kind] = left
            host = stack_ref[kind * PLANE + left]
            mate_ref[q] = host
            mate_ref[host] = q
            load_ref[owner[q]] -= 1

    totals = plane_totals(z, load_ref)
    most = functools.reduce(jnp.maximum, [totals[g] + totals[g + 1] for g in range(0, planes, 2)])
    highest = functools.reduce(jnp.maximum, totals)
    choice = jnp.int32(0)
    for i in range(1, len(choices)):
        tried = choices[i - 1]
        beyond = (most > 2 * PLANE * tried) | (highest > PLANE * tried + GIFT * PLANE // 2)
        choice = jnp.where(beyond, i, choice)
    choice_ref[0] = choice


def plane_totals(z, load_ref):
    return [
        sum(load_ref[g * PLANE + e] for e in range(PLANE)) for g in range(z.devices // PLANE)
    ]


def plan(z, degree_start, choices):
    smem = pl.BlockSpec(memory_space=pltpu.SMEM)
    kinds = z.devices // PLANE * z.group_size
    return pl.pallas_call(
        functools.partial(plan_kernel, z, choices),
        in_specs=[smem],
        out_specs=[smem] * 4,
        out_shape=[
            jax.ShapeDtypeStruct((size,), jnp.int32)
            for size in (1, z.degrees, z.devices, z.devices)
        ],
        scratch_shapes=[pltpu.SMEM((kinds,), jnp.int32), pltpu.SMEM((kinds * PLANE,), jnp.int32)],
        name="plan",
    )(degree_start)


def assign(z, slots, start_ref, mate_ref, load_ref, high_ref, place_ref, kept_ref, room_ref):
    totals = plane_totals(z, load_ref)
    for d in range(z.devices):
        excess = totals[d // PLANE] - PLANE * slots - GIFT * (d % PLANE // 2)
        gift = jnp.int32(0) if d % 2 else jnp.clip(excess, 0, GIFT)
        kept_ref[d] = load_ref[d] - gift
        room_ref[d ^ PLANE] = slots - gift
    for q in range(z.degrees):
        first = start_ref[q] + z.owner(start_ref[q]) * (slots - z.capacity)
        for p in range(z.counts[q]):
            place_ref[z.starts[q] + p] = first + p
    for d in range(z.devices):
        if d % PLANE == 0:
            spare = (jnp.int32(d), kept_ref[d])
        q = high_ref[d]
        last = z.last_block(q)
        first = last - z.turns(q)
        offset = start_ref[q] - d * z.capacity
        kept = kept_ref[d] - offset

        def move(state, first=first):
            p, device, slot = state
            place_ref[first + p] = device * slots + slot
            fits = slot < room_ref[device]
            after = device + 1
            return (
                jnp.where(fits, p + 1, p),
                jnp.where(fits, device, after),
                jnp.where(fits, slot + 1, kept_ref[jnp.minimum(after, z.devices - 1)]),
            )

        spare = lax.while_loop(
            lambda state, kept=kept: state[0] < kept, move, (room_ref[d] - offset, *spare)
        )[1:]
        host = mate_ref[q]
        if d % 2 == 0:
            other = d ^ PLANE
            given = other * slots + room_ref[other] - kept

            def give(p, carry, given=given, first=first):
                place_ref[first + p] = given + p
                return carry

            lax.fori_loop(kept, last - first + 1 - jnp.where(host >= 0, 1, 0), give, 0)
        start = start_ref[jnp.maximum(host, 0)]
        shared = start + z.owner(start) * (slots - z.capacity) + z.turns(host)
        place_ref[last] = jnp.where(host >= 0, shared, place_ref[last])


def swap(value, axis, bit):
    size = lax.axis_size(axis)
    return lax.ppermute(value, axis, [(i, i ^ bit) for i in range(size)])


def straight_inverses(inverses):
    own = inverses[:, 1]
    rad, lm = lax.axis_size("rad"), lax.axis_size("lm")
    facing = [(d, d ^ PLANE) for d in range(0, rad * lm, 2)]
    return own, swap(own, "lm", 2), swap(own, "rad", 1), lax.ppermute(own, AXES, facing)


def other_core(values):
    return [swap(value, "lm", 1) for value in values]


def riding(z, mate_ref, q):
    b, host = z.last_block(q), mate_ref[q]
    rides = host >= 0
    host = jnp.maximum(host, 0)
    return b, jnp.where(rides, z.last_block(host), b), jnp.where(rides, z.last_live(host), z.width)


def pack_kernel(z, f, slots, *refs):
    if f:
        place_ref, mate_ref, field_ref, out_ref, holder_ref, part_ref, wide_ref, sems = refs
    else:
        start_ref, mate_ref, load_ref, high_ref, field_ref, out_ref, place_ref = refs[:7]
        part_ref, wide_ref, sems, kept_ref, room_ref = refs[7:]
    pitch = z.blocks + 1
    some = z.local // PARTS
    copies = [
        pltpu.make_async_copy(
            field_ref.at[f, pl.ds(i * some, some)], part_ref.at[pl.ds(i * some, some)], sems.at[i]
        )
        for i in range(PARTS)
    ]
    for copy in copies:
        copy.start()
    if not f:
        assign(z, slots, start_ref, mate_ref, load_ref, high_ref, place_ref, kept_ref, room_ref)
    for level in range(z.local):
        if level % some == 0:
            copies[level // some].wait()
        wide_ref[pl.ds(level * pitch, z.blocks), :] = part_ref[level].astype(jnp.float32)

    def group(g, carry):
        for k in range(BATCH):
            b = g * BATCH + k
            tile = wide_ref[pl.ds(b, z.local, stride=pitch), :]
            out_ref[place_ref[b]] = tile.astype(jnp.bfloat16)
        return carry

    lax.fori_loop(0, z.blocks // BATCH, group, 0)
    column = lax.broadcasted_iota(jnp.int32, (z.local, z.width), 1)

    def ride(q, carry):
        b, host_block, live = riding(z, mate_ref, q)
        rider = pltpu.roll(wide_ref[pl.ds(b, z.local, stride=pitch), :], live, 1)
        tile = wide_ref[pl.ds(host_block, z.local, stride=pitch), :]
        out_ref[place_ref[b]] = jnp.where(column < live, tile, rider).astype(jnp.bfloat16)
        return carry

    lax.fori_loop(z.degrees // 2, z.degrees, ride, 0, unroll=RIDES)
    if not f:
        return

    def clear(k, carry):
        holder_ref[k] = 0
        return carry

    lax.fori_loop(0, z.devices * z.capacity, clear, 0, unroll=8)

    def degree(q, b):
        def block(p, inner):
            holder_ref[place_ref[b + p]] = q * OB + p
            return inner

        count = z.turns(q) + 1
        rides = (q >= z.degrees // 2) & (mate_ref[q] >= 0)
        lax.fori_loop(0, count - jnp.where(rides, 1, 0), block, 0)
        return b + count

    lax.fori_loop(0, z.degrees, degree, 0)


def pack(z, grid_field, f, slots, *tables):
    total = z.devices * slots
    smem = pl.BlockSpec(memory_space=pltpu.SMEM)
    table = jax.ShapeDtypeStruct((z.devices * z.capacity if f else z.blocks,), jnp.int32)
    return pl.pallas_call(
        functools.partial(pack_kernel, z, f, slots),
        in_specs=[smem] * len(tables) + [pl.BlockSpec(memory_space=pl.ANY)],
        out_specs=[pl.BlockSpec(memory_space=pltpu.VMEM), smem],
        out_shape=[jax.ShapeDtypeStruct((total, z.local, z.width), jnp.bfloat16), table],
        scratch_shapes=[
            pltpu.VMEM((z.local, z.blocks, z.width), jnp.bfloat16),
            pltpu.VMEM((z.local * (z.blocks + 1), z.width), jnp.float32),
            pltpu.SemaphoreType.DMA((PARTS,)),
        ]
        + [pltpu.SMEM((z.devices,), jnp.int32)] * (0 if f else 2),
        compiler_params=pltpu.CompilerParams(vmem_limit_bytes=VMEM),
        cost_estimate=pl.CostEstimate(flops=10**9, bytes_accessed=10**7, transcendentals=0),
        name=f"pack_{f}",
    )(*tables, grid_field)


def solve_kernel(z, f, slots, per_step, holder_ref, start_ref, mate_ref, me_ref, columns_ref, inverses_ref, *rest):
    (own, across, along, corner, own_odd, across_odd, along_odd, corner_odd, far) = rest[:9]
    out_ref, matrix_ref, square_ref, above_ref, below_ref, sems = rest[9:]
    strength = diffusion_numbers[f]
    step = pl.program_id(0)
    shape = (z.levels, z.width)
    me = me_ref[0]

    @pl.when(step == 0)
    def _():
        sources = [
            own.at[f], own_odd.at[f], across.at[f], across_odd.at[f],
            along.at[f], along_odd.at[f], corner.at[0], corner_odd.at[0],
            inverses_ref.at[f, 0], far.at[f],
        ]
        copies = [
            pltpu.make_async_copy(source, matrix_ref.at[i], sems.at[i])
            for i, source in enumerate(sources)
        ]
        for copy in copies:
            copy.start()
        level = lax.broadcasted_iota(jnp.int32, shape, 0)

        def radius(positions):
            return inner_radius + shell_depth * (positions + 1).astype(jnp.float32) / (z.levels + 1)

        here = radius(level)
        scaled = (shell_depth / (z.levels + 1)) / here
        square_ref[...] = strength * (scaled * scaled)
        above_ref[...] = jnp.where(level == z.levels - 1, 0.0, strength * radius(level + 1) / here)
        below_ref[...] = jnp.where(level == 0, 0.0, strength * radius(level - 1) / here)
        for copy in copies:
            copy.wait()

    column = lax.broadcasted_iota(jnp.int32, shape, 1)
    host = quotient(holder_ref[me * slots], OB, z.degrees * OB)
    rider = mate_ref[host]
    host_at = z.turns(host) - step * per_step
    rides = (rider >= 0) & (host_at >= 0) & (host_at < per_step)

    def block(i, carry):
        again = i >= per_step
        k = jnp.where(again, host_at, i)
        code = holder_ref[me * slots + jnp.minimum(step * per_step + k, slots - 1)]
        q = jnp.where(again, rider, quotient(code, OB, z.degrees * OB))
        value = z.spacing * (q + 1) - 1
        last = value - lax.rem(code, OB) * (z.width // 2)
        begin = jnp.where(again, z.last_live(host), 0)
        end = jnp.where(again, begin + z.last_live(rider), 2 * last + 2)
        offset = z.owner(start_ref[q]) ^ me
        which = jnp.where(offset < PLANE, offset, PLANE + 1)
        which = jnp.where(q >= z.degrees // 2, which, PLANE)
        factor = (value * (value + 1)).astype(jnp.float32)
        u = columns_ref[:, k].reshape(shape).astype(jnp.float32)
        u = jnp.where((column >= begin) & (column < end), u, 0.0)
        weight = (1.0 - 2.0 * strength) - factor * square_ref[...]
        rhs = weight * u
        rhs += above_ref[...] * pltpu.roll(u, z.levels - 1, 0)
        rhs += below_ref[...] * pltpu.roll(u, 1, 0)
        high = rhs.astype(jnp.bfloat16)
        low = (rhs - high.astype(jnp.float32)).astype(jnp.bfloat16)
        both = jnp.concatenate([high, low], axis=1)
        product = jnp.dot(matrix_ref[which], both, preferred_element_type=jnp.float32)
        solved = product[:, : z.width] + product[:, z.width :]
        earlier = out_ref[:, k].reshape(shape).astype(jnp.float32)
        solved = jnp.where(column >= begin, solved, earlier).astype(jnp.bfloat16)
        out_ref[:, k] = solved.reshape(z.devices, z.local, z.width)
        return carry

    lax.fori_loop(0, per_step + jnp.where(rides, 1, 0), block, 0)


def solve(z, holder, degree_start, mate, me, columns, inverses, pieces, f, slots):
    steps = pl.cdiv(slots, 5)
    per_step = pl.cdiv(slots, steps)
    block = (z.devices, per_step, z.local, z.width)
    spec = pl.BlockSpec(block, lambda i, *s: (0, i, 0, 0))
    return pl.pallas_call(
        functools.partial(solve_kernel, z, f, slots, per_step),
        grid_spec=pltpu.PrefetchScalarGridSpec(
            num_scalar_prefetch=4,
            grid=(steps,),
            in_specs=[spec] + [pl.BlockSpec(memory_space=pl.ANY)] * (1 + len(pieces)),
            out_specs=spec,
            scratch_shapes=[pltpu.VMEM((PLANE + 2, z.levels, z.levels), jnp.bfloat16)]
            + [pltpu.VMEM((z.levels, z.width), jnp.float32)] * 3
            + [pltpu.SemaphoreType.DMA((PLANE + 2,))],
        ),
        out_shape=jax.ShapeDtypeStruct(columns.shape, jnp.bfloat16),
        compiler_params=pltpu.CompilerParams(vmem_limit_bytes=VMEM),
        cost_estimate=pl.CostEstimate(flops=10**10, bytes_accessed=10**7, transcendentals=0),
        name=f"solve_{f}",
    )(holder, degree_start, mate, me, columns, inverses, *pieces)


def edge_slopes(z, second, before_last, before, after):
    def wide(ref):
        return ref[...].reshape(z.blocks, z.width).astype(jnp.float32)

    first = 0.5 * (wide(second) - wide(before))
    last = 0.5 * (wide(after) - wide(before_last))
    return first.astype(jnp.bfloat16), last.astype(jnp.bfloat16)


def unpack_kernel(z, f, place_ref, mate_ref, returned_ref, *rest):
    if f:
        earlier_ref, _, before_ref, after_ref, grid_ref, slope_ref, second_ref, before_last_ref = rest[:8]
        edge_ref, edge_sems = rest[-2:]
    else:
        grid_ref, slope_ref = rest[:2]
    level_ref, inner_ref, wide_ref, sems = rest[8 if f else 2 :][:4]
    pitch = z.blocks + 1
    ends = [
        pltpu.make_async_copy(
            earlier_ref.at[f - 1, level], edge_ref.at[i], edge_sems.at[i]
        )
        for i, level in enumerate((1, z.local - 2))
    ] if f else []
    for copy in ends:
        copy.start()

    def gather(g, carry):
        for k in range(BATCH):
            b = g * BATCH + k
            tile = returned_ref[place_ref[b]].astype(jnp.float32)
            wide_ref[pl.ds(b, z.local, stride=pitch), :] = tile
        return carry

    lax.fori_loop(0, z.blocks // BATCH, gather, 0)
    column = lax.broadcasted_iota(jnp.int32, (z.local, z.width), 1)

    def ride(q, carry):
        b, host_block, live = riding(z, mate_ref, q)
        tile = returned_ref[place_ref[b]].astype(jnp.float32)
        rider = pltpu.roll(tile, z.width - live, 1)
        host_rows = pl.ds(host_block, z.local, stride=pitch)
        wide_ref[host_rows, :] = jnp.where(column < live, tile, 0.0)
        rows = pl.ds(b, z.local, stride=pitch)
        wide_ref[rows, :] = jnp.where(column < z.last_live(q), rider, 0.0)
        return carry

    lax.fori_loop(z.degrees // 2, z.degrees, ride, 0, unroll=RIDES)

    def group(g, carry):
        at = pl.multiple_of(g * GROUP, GROUP)
        rows = pl.ds(at, GROUP)
        value = [wide_ref[pl.ds(at + i * pitch, GROUP), :] for i in range(z.local)]
        for i in range(z.local):
            level_ref[i, rows, :] = value[i].astype(jnp.bfloat16)
        for i in range(1, z.local - 1):
            slope = 0.5 * (value[i + 1] - value[i - 1])
            inner_ref[i - 1, rows, :] = slope.astype(jnp.bfloat16)
        if f:
            second_ref[rows, :] = value[1].astype(jnp.bfloat16)
            before_last_ref[rows, :] = value[-2].astype(jnp.bfloat16)
        return carry

    groups = z.blocks // GROUP
    copies = []
    for i in range(PARTS):
        begin, end = i * groups // PARTS, (i + 1) * groups // PARTS
        lax.fori_loop(begin, end, group, 0)
        rows = pl.ds(begin * GROUP, (end - begin) * GROUP)
        copies += [
            pltpu.make_async_copy(
                level_ref.at[:, rows, :], grid_ref.at[f, :, rows, :], sems.at[2 * i]
            ),
            pltpu.make_async_copy(
                inner_ref.at[:, rows, :],
                slope_ref.at[f, pl.ds(1, z.local - 2), rows, :],
                sems.at[2 * i + 1],
            ),
        ]
        for copy in copies[-2:]:
            copy.start()
    if f:
        for copy in ends:
            copy.wait()
        slopes = edge_slopes(z, edge_ref.at[0], edge_ref.at[1], before_ref, after_ref)
        for i, level in enumerate((0, z.local - 1)):
            edge_ref[2 + i] = slopes[i]
            copy = pltpu.make_async_copy(
                edge_ref.at[2 + i], slope_ref.at[f - 1, level], edge_sems.at[2 + i]
            )
            copy.start()
            copies.append(copy)
    for copy in copies:
        copy.wait()


def unpack(z, place, mate, returned, f, earlier):
    whole = jax.ShapeDtypeStruct((z.fields, z.local, z.blocks, z.width), jnp.bfloat16)
    level = jax.ShapeDtypeStruct((z.blocks, z.width), jnp.bfloat16)
    smem, anywhere = pl.BlockSpec(memory_space=pltpu.SMEM), pl.BlockSpec(memory_space=pl.ANY)
    vmem = pl.BlockSpec(memory_space=pltpu.VMEM)
    edge_scratch = [
        pltpu.VMEM((4, z.blocks, z.width), jnp.bfloat16),
        pltpu.SemaphoreType.DMA((4,)),
    ]
    return pl.pallas_call(
        functools.partial(unpack_kernel, z, f),
        in_specs=[smem, smem, vmem] + [anywhere, anywhere, vmem, vmem] * min(f, 1),
        out_specs=[anywhere] * 2 + [vmem] * 2 * min(f, 1),
        out_shape=[whole] * 2 + [level] * 2 * min(f, 1),
        scratch_shapes=[
            pltpu.VMEM((z.local, z.blocks, z.width), jnp.bfloat16),
            pltpu.VMEM((z.local - 2, z.blocks, z.width), jnp.bfloat16),
            pltpu.VMEM((z.local * (z.blocks + 1), z.width), jnp.float32),
            pltpu.SemaphoreType.DMA((2 * PARTS,)),
        ]
        + edge_scratch * min(f, 1),
        input_output_aliases={3: 0, 4: 1} if f else {},
        compiler_params=pltpu.CompilerParams(vmem_limit_bytes=VMEM if f else MORE_VMEM),
        cost_estimate=pl.CostEstimate(flops=10**9, bytes_accessed=10**7, transcendentals=0),
        name=f"unpack_{f}",
    )(place, mate, returned, *earlier)


def rim_kernel(z, place_ref, mate_ref, returned_ref, first_ref, last_ref, first_wide_ref, last_wide_ref):
    sides = ((first_wide_ref, 0), (last_wide_ref, z.local - 1))

    def gather(g, carry):
        for k in range(BATCH):
            b = g * BATCH + k
            tile = returned_ref[place_ref[b]].astype(jnp.float32)
            for wide_ref, row in sides:
                wide_ref[pl.ds(b, 1), :] = tile[row : row + 1]
        return carry

    lax.fori_loop(0, z.blocks // BATCH, gather, 0)
    column = lax.broadcasted_iota(jnp.int32, (z.local, z.width), 1)

    def ride(q, carry):
        b, host_block, live = riding(z, mate_ref, q)
        tile = returned_ref[place_ref[b]].astype(jnp.float32)
        rider = pltpu.roll(tile, z.width - live, 1)
        rider = jnp.where(column < z.last_live(q), rider, 0.0)
        tile = jnp.where(column < live, tile, 0.0)
        for wide_ref, row in sides:
            wide_ref[pl.ds(host_block, 1), :] = tile[row : row + 1]
            wide_ref[pl.ds(b, 1), :] = rider[row : row + 1]
        return carry

    lax.fori_loop(z.degrees // 2, z.degrees, ride, 0, unroll=RIDES)
    first_ref[0] = first_wide_ref[...].astype(jnp.bfloat16)
    last_ref[0] = last_wide_ref[...].astype(jnp.bfloat16)


def rims(z, place, mate, returned, f):
    level = jax.ShapeDtypeStruct((1, z.blocks, z.width), jnp.bfloat16)
    spec = pl.BlockSpec(level.shape, lambda i, *s: (0, 0, 0))
    return pl.pallas_call(
        functools.partial(rim_kernel, z),
        grid_spec=pltpu.PrefetchScalarGridSpec(
            num_scalar_prefetch=2,
            grid=(1,),
            in_specs=[pl.BlockSpec(returned.shape, lambda i, *s: (0, 0, 0))],
            out_specs=[spec, spec],
            scratch_shapes=[pltpu.VMEM((z.blocks, z.width), jnp.float32)] * 2,
        ),
        out_shape=[level, level],
        compiler_params=pltpu.CompilerParams(vmem_limit_bytes=VMEM if f else MORE_VMEM),
        cost_estimate=pl.CostEstimate(flops=10**8, bytes_accessed=3 * 10**6, transcendentals=0),
        name=f"rims_{f}",
    )(place, mate, returned)


def edge_kernel(z, f, second_ref, before_last_ref, before_ref, after_ref, _, slope_ref, edge_ref, sems):
    slopes = edge_slopes(z, second_ref, before_last_ref, before_ref, after_ref)
    copies = []
    for i, level in enumerate((0, z.local - 1)):
        edge_ref[i] = slopes[i]
        copies.append(pltpu.make_async_copy(edge_ref.at[i], slope_ref.at[f, level], sems.at[i]))
        copies[i].start()
    for copy in copies:
        copy.wait()


def edges(z, slope, inside, outside, f):
    vmem, anywhere = pl.BlockSpec(memory_space=pltpu.VMEM), pl.BlockSpec(memory_space=pl.ANY)
    return pl.pallas_call(
        functools.partial(edge_kernel, z, f),
        in_specs=[vmem] * 4 + [anywhere],
        out_specs=anywhere,
        out_shape=jax.ShapeDtypeStruct(slope.shape, slope.dtype),
        scratch_shapes=[
            pltpu.VMEM((2, z.blocks, z.width), jnp.bfloat16),
            pltpu.SemaphoreType.DMA((2,)),
        ],
        input_output_aliases={4: 0},
        compiler_params=pltpu.CompilerParams(vmem_limit_bytes=VMEM),
        name=f"edges_{f}",
    )(*inside, *outside, slope)


def beside(z, first, last):
    up = [(i, i + 1) for i in range(z.devices - 1)]
    down = [(j, i) for i, j in up]
    return lax.ppermute(last, AXES, up), lax.ppermute(first, AXES, down)


def exchange(z, value, slots):
    shaped = value.reshape(z.devices, slots, z.local, z.width)
    return lax.all_to_all(shaped, AXES, split_axis=0, concat_axis=0, tiled=True)


def body(grid_field, inverses, slot_blocks, degree_start):
    rad, lm = lax.axis_size("rad"), lax.axis_size("lm")
    z = Sizes(rad * lm, grid_field, inverses, slot_blocks)
    choices = slot_choices(z)
    kernels = z.local % 16 == 0 and z.fields == 2 and z.blocks % GROUP == 0 and rad % 4 == 0 and lm == PLANE // 2
    low, high = z.counts[z.degrees // 2 - 1 : z.degrees // 2 + 1]
    if not kernels or low + GIFT > choices[0] or high <= GIFT or z.capacity - choices[0] > GIFT:
        return plain_body(z, grid_field, inverses, degree_start)
    me = lax.axis_index(AXES).reshape(1).astype(jnp.int32)
    choice, *tables = plan(z, degree_start, choices)
    routes = [functools.partial(route, z, slots) for slots in choices]
    return lax.switch(choice[0], routes, grid_field, inverses, degree_start, me, *tables)


def route(z, slots, grid_field, inverses, degree_start, me, mate, load, high):
    sent_0, place = pack(z, grid_field, 0, slots, degree_start, mate, load, high)
    sent_1, holder = pack(z, grid_field, 1, slots, place, mate)
    sent_1, own, across, along, far = lax.optimization_barrier(
        (sent_1, *straight_inverses(inverses))
    )
    columns = [exchange(z, sent, slots) for sent in (sent_0, sent_1)]
    corner_0 = swap(across[:1], "rad", 1)
    even = [own, across, along]
    odd = other_core(even)
    pieces = lax.optimization_barrier((*even, corner_0, *odd, *other_core([corner_0]), far))
    solved_0 = solve(z, holder, degree_start, mate, me, columns[0], inverses, pieces, 0, slots)
    corner_1 = swap(along[1:], "lm", 2)
    pieces = (*even, corner_1, *odd, *other_core([corner_1]), far)
    solved_1 = solve(z, holder, degree_start, mate, me, columns[1], inverses, pieces, 1, slots)
    solved = [solved_0, solved_1]
    returned = [
        exchange(z, solved[f], slots).reshape(z.devices * slots, z.local, z.width)
        for f in range(z.fields)
    ]
    outside = beside(z, *rims(z, place, mate, returned[0], 0))
    outs = unpack(z, place, mate, returned[0], 0, ())
    last, *outs = lax.optimization_barrier((returned[1], *outs))
    last_outside = beside(z, *rims(z, place, mate, last, 1))
    grid, slope, *inside = unpack(z, place, mate, last, 1, (*outs, *outside))
    return grid, edges(z, slope, inside, last_outside, 1)


def plain_body(z, grid_field, inverses, degree_start):
    index = np.arange(z.degrees)
    counts = np.asarray(z.counts)
    degree_of = np.repeat(index, counts)
    place_in = np.arange(z.blocks) - np.asarray(z.starts)[degree_of]
    value = z.spacing * (index + 1) - 1
    slot_place = degree_start[degree_of] + jnp.asarray(place_in, jnp.int32)
    total = z.devices * z.capacity
    holder = jnp.full((total,), z.blocks, jnp.int32)
    holder = holder.at[slot_place].set(jnp.arange(z.blocks, dtype=jnp.int32))
    sent = jnp.take(grid_field, holder, axis=2, mode="fill", fill_value=0)
    sent = sent.reshape(z.fields, z.local, z.devices, z.capacity, z.width)
    columns = lax.all_to_all(sent, AXES, split_axis=2, concat_axis=1, tiled=True)
    columns = columns.reshape(z.fields, z.levels, z.capacity, z.width)
    device = lax.axis_index(AXES)
    mine = lax.dynamic_slice_in_dim(holder, device * z.capacity, z.capacity)
    order = jnp.asarray(place_in)[:, None] * OB + np.arange(z.width)[None, :] // 2
    live_table = (order <= jnp.asarray(value[degree_of])[:, None]).astype(jnp.float32)
    live = jnp.take(live_table, mine, axis=0, mode="fill", fill_value=0)
    factor = (value * (value + 1)).astype(np.float32)[degree_of]
    factor = jnp.take(jnp.asarray(factor), mine, mode="fill", fill_value=0)
    upper = jnp.take(jnp.asarray(degree_of >= z.degrees // 2), mine, mode="fill", fill_value=False)
    radius = inner_radius + shell_depth * jnp.arange(z.levels + 2, dtype=jnp.float32) / (z.levels + 1)
    here = radius[1:-1][None, :, None, None]
    padded = jnp.pad(columns.astype(jnp.float32), ((0, 0), (1, 1), (0, 0), (0, 0)))
    weighted = padded * radius[None, :, None, None]
    second = (weighted[:, 2:] - 2.0 * weighted[:, 1:-1] + weighted[:, :-2]) / here
    scaled = (shell_depth / (z.levels + 1)) / here
    centre = padded[:, 1:-1]
    strength = jnp.asarray(diffusion_numbers, jnp.float32)[:, None, None, None]
    angular = factor[None, None, :, None] * (scaled * scaled) * centre
    rhs = (centre + strength * (second - angular)) * live[None, None]

    def solve_slot(carry, at):
        matrix = lax.dynamic_index_in_dim(
            inverses, upper[at].astype(jnp.int32), 1, keepdims=False
        ).astype(jnp.float32)
        block = lax.dynamic_index_in_dim(rhs, at, 2, keepdims=False)
        product = jnp.einsum("fij,fjc->fic", matrix, block, precision=lax.Precision.HIGHEST)
        return carry, product.astype(jnp.bfloat16)

    solved = lax.scan(solve_slot, 0, jnp.arange(z.capacity))[1]
    solved = jnp.moveaxis(solved, 0, 2)
    solved = solved.reshape(z.fields, z.devices, z.local, z.capacity, z.width)
    returned = lax.all_to_all(solved, AXES, split_axis=1, concat_axis=3, tiled=True)
    returned = returned.reshape(z.fields, z.local, total, z.width)
    grid = jnp.take(returned, slot_place, axis=2)
    before, after = beside(z, grid[:, :1], grid[:, -1:])
    rimmed = jnp.concatenate([before, grid, after], axis=1).astype(jnp.float32)
    return grid, (0.5 * (rimmed[:, 2:] - rimmed[:, :-2])).astype(jnp.bfloat16)


def solution(mesh):
    in_specs = (P(None, AXES), P(None, AXES), P(), P())
    out_specs = (P(None, AXES), P(None, AXES))
    return jax.shard_map(body, mesh=mesh, in_specs=in_specs, out_specs=out_specs, check_vma=False)
```

```python
import functools

import jax
import jax.numpy as jnp
import numpy as np
from jax import lax
from jax.experimental import pallas as pl
from jax.experimental.pallas import tpu as pltpu
from jax.sharding import PartitionSpec as P

LMAX1 = 1024
OB = 64
AXES = ("rad", "lm")
PLANE = 8
GIFT = 8
GROUP = 16
BATCH = 34
VMEM = 48 << 20
MORE_VMEM = 60 << 20
RIDES = 16
PARTS = 4

inner_radius = 0.35
shell_depth = 0.65
diffusion_numbers = (0.9, 0.4)


def quotient(value, divisor, bound):
    numbers = np.arange(bound)
    for shift in range(24):
        factor = -(-(1 << shift) // divisor)
        if bound * factor < 2**31 and np.all(numbers * factor >> shift == numbers // divisor):
            return lax.shift_right_logical(value * factor, jnp.int32(shift))
    return lax.div(value, divisor)


class Sizes:
    def __init__(self, devices, grid_field, inverses, slot_blocks):
        self.devices = devices
        self.fields, self.local, self.blocks, self.width = grid_field.shape
        self.levels = inverses.shape[-1]
        self.capacity = slot_blocks.shape[1]
        self.degrees = 2 * devices
        self.spacing = LMAX1 // self.degrees
        self.group_size = OB * self.degrees // LMAX1
        index = np.arange(self.degrees)
        self.counts = [int(c) for c in index // self.group_size + 1]
        self.starts = [int(s) for s in np.cumsum(self.counts) - self.counts]
        self.partial = [q for q in range(self.degrees) if (q + 1) % self.group_size]

    def turns(self, q):
        return quotient(q, self.group_size, self.degrees)

    def owner(self, slot):
        return quotient(slot, self.capacity, self.devices * self.capacity)

    def last_block(self, q):
        turns = self.turns(q)
        rest = q - turns * self.group_size
        whole = lax.shift_right_logical(self.group_size * turns * (turns + 1), 1)
        return whole + rest * (turns + 1) + turns

    def last_live(self, q):
        return 2 * self.spacing * (q - self.turns(q) * self.group_size + 1)


def slot_choices(z):
    mean = -(-z.blocks // z.devices)
    return sorted({min(mean + extra, z.capacity) for extra in (0, 1, 2, 3)} | {z.capacity})


def plan_kernel(z, choices, start_ref, choice_ref, mate_ref, load_ref, high_ref, count_ref, stack_ref):
    half = z.degrees // 2
    planes = z.devices // PLANE
    kinds = z.group_size
    owner = [z.owner(start_ref[q]) for q in range(z.degrees)]
    for q in range(half, z.degrees):
        load_ref[owner[q]] = start_ref[q] - owner[q] * z.capacity + z.counts[q]
        high_ref[owner[q]] = q
    for i in range(planes * kinds):
        count_ref[i] = 0
    for q in range(z.degrees):
        mate_ref[q] = -1
    for q in z.partial:
        if q < half:
            kind = quotient(owner[q], PLANE, z.devices) * kinds + q % kinds
            stack_ref[kind * PLANE + count_ref[kind]] = q
            count_ref[kind] += 1
    for q in sorted(z.partial, key=lambda q: -(q % kinds)):
        if q < half:
            continue
        first_kind = quotient(owner[q], PLANE, z.devices) * kinds
        kind = jnp.int32(-1)
        for i in range(kinds - 1 - q % kinds):
            kind = jnp.where(count_ref[first_kind + i] > 0, first_kind + i, kind)

        @pl.when(kind >= 0)
        def _(kind=kind, q=q):
            left = count_ref[kind] - 1
            count_ref[kind] = left
            host = stack_ref[kind * PLANE + left]
            mate_ref[q] = host
            mate_ref[host] = q
            load_ref[owner[q]] -= 1

    totals = plane_totals(z, load_ref)
    most = functools.reduce(jnp.maximum, [totals[g] + totals[g + 1] for g in range(0, planes, 2)])
    highest = functools.reduce(jnp.maximum, totals)
    choice = jnp.int32(0)
    for i in range(1, len(choices)):
        tried = choices[i - 1]
        beyond = (most > 2 * PLANE * tried) | (highest > PLANE * tried + GIFT * PLANE // 2)
        choice = jnp.where(beyond, i, choice)
    choice_ref[0] = choice


def plane_totals(z, load_ref):
    return [
        sum(load_ref[g * PLANE + e] for e in range(PLANE)) for g in range(z.devices // PLANE)
    ]


def plan(z, degree_start, choices):
    smem = pl.BlockSpec(memory_space=pltpu.SMEM)
    kinds = z.devices // PLANE * z.group_size
    return pl.pallas_call(
        functools.partial(plan_kernel, z, choices),
        in_specs=[smem],
        out_specs=[smem] * 4,
        out_shape=[
            jax.ShapeDtypeStruct((size,), jnp.int32)
            for size in (1, z.degrees, z.devices, z.devices)
        ],
        scratch_shapes=[pltpu.SMEM((kinds,), jnp.int32), pltpu.SMEM((kinds * PLANE,), jnp.int32)],
        name="plan",
    )(degree_start)


def assign(z, slots, start_ref, mate_ref, load_ref, high_ref, place_ref, kept_ref, room_ref):
    totals = plane_totals(z, load_ref)
    for d in range(z.devices):
        excess = totals[d // PLANE] - PLANE * slots - GIFT * (d % PLANE // 2)
        gift = jnp.int32(0) if d % 2 else jnp.clip(excess, 0, GIFT)
        kept_ref[d] = load_ref[d] - gift
        room_ref[d ^ PLANE] = slots - gift
    for q in range(z.degrees):
        first = start_ref[q] + z.owner(start_ref[q]) * (slots - z.capacity)
        for p in range(z.counts[q]):
            place_ref[z.starts[q] + p] = first + p
    for d in range(z.devices):
        if d % PLANE == 0:
            spare = (jnp.int32(d), kept_ref[d])
        q = high_ref[d]
        last = z.last_block(q)
        first = last - z.turns(q)
        offset = start_ref[q] - d * z.capacity
        kept = kept_ref[d] - offset

        def move(state, first=first):
            p, device, slot = state
            place_ref[first + p] = device * slots + slot
            fits = slot < room_ref[device]
            after = device + 1
            return (
                jnp.where(fits, p + 1, p),
                jnp.where(fits, device, after),
                jnp.where(fits, slot + 1, kept_ref[jnp.minimum(after, z.devices - 1)]),
            )

        spare = lax.while_loop(
            lambda state, kept=kept: state[0] < kept, move, (room_ref[d] - offset, *spare)
        )[1:]
        host = mate_ref[q]
        if d % 2 == 0:
            other = d ^ PLANE
            given = other * slots + room_ref[other] - kept

            def give(p, carry, given=given, first=first):
                place_ref[first + p] = given + p
                return carry

            lax.fori_loop(kept, last - first + 1 - jnp.where(host >= 0, 1, 0), give, 0)
        start = start_ref[jnp.maximum(host, 0)]
        shared = start + z.owner(start) * (slots - z.capacity) + z.turns(host)
        place_ref[last] = jnp.where(host >= 0, shared, place_ref[last])


def swap(value, axis, bit):
    size = lax.axis_size(axis)
    return lax.ppermute(value, axis, [(i, i ^ bit) for i in range(size)])


def straight_inverses(inverses):
    own = inverses[:, 1]
    rad, lm = lax.axis_size("rad"), lax.axis_size("lm")
    facing = [(d, d ^ PLANE) for d in range(0, rad * lm, 2)]
    return own, swap(own, "lm", 2), swap(own, "rad", 1), lax.ppermute(own, AXES, facing)


def other_core(values):
    return [swap(value, "lm", 1) for value in values]


def riding(z, mate_ref, q):
    b, host = z.last_block(q), mate_ref[q]
    rides = host >= 0
    host = jnp.maximum(host, 0)
    return b, jnp.where(rides, z.last_block(host), b), jnp.where(rides, z.last_live(host), z.width)


def pack_kernel(z, f, slots, *refs):
    if f:
        place_ref, mate_ref, field_ref, out_ref, holder_ref, part_ref, wide_ref, sems = refs
    else:
        start_ref, mate_ref, load_ref, high_ref, field_ref, out_ref, place_ref = refs[:7]
        part_ref, wide_ref, sems, kept_ref, room_ref = refs[7:]
    pitch = z.blocks + 1
    some = z.local // PARTS
    copies = [
        pltpu.make_async_copy(
            field_ref.at[f, pl.ds(i * some, some)], part_ref.at[pl.ds(i * some, some)], sems.at[i]
        )
        for i in range(PARTS)
    ]
    for copy in copies:
        copy.start()
    if not f:
        assign(z, slots, start_ref, mate_ref, load_ref, high_ref, place_ref, kept_ref, room_ref)
    for level in range(z.local):
        if level % some == 0:
            copies[level // some].wait()
        wide_ref[pl.ds(level * pitch, z.blocks), :] = part_ref[level].astype(jnp.float32)

    def group(g, carry):
        for k in range(BATCH):
            b = g * BATCH + k
            tile = wide_ref[pl.ds(b, z.local, stride=pitch), :]
            out_ref[place_ref[b]] = tile.astype(jnp.bfloat16)
        return carry

    lax.fori_loop(0, z.blocks // BATCH, group, 0)
    column = lax.broadcasted_iota(jnp.int32, (z.local, z.width), 1)

    def ride(q, carry):
        b, host_block, live = riding(z, mate_ref, q)
        rider = pltpu.roll(wide_ref[pl.ds(b, z.local, stride=pitch), :], live, 1)
        tile = wide_ref[pl.ds(host_block, z.local, stride=pitch), :]
        out_ref[place_ref[b]] = jnp.where(column < live, tile, rider).astype(jnp.bfloat16)
        return carry

    lax.fori_loop(z.degrees // 2, z.degrees, ride, 0, unroll=RIDES)
    if not f:
        return

    def clear(k, carry):
        holder_ref[k] = 0
        return carry

    lax.fori_loop(0, z.devices * z.capacity, clear, 0, unroll=8)

    def degree(q, b):
        def block(p, inner):
            holder_ref[place_ref[b + p]] = q * OB + p
            return inner

        count = z.turns(q) + 1
        rides = (q >= z.degrees // 2) & (mate_ref[q] >= 0)
        lax.fori_loop(0, count - jnp.where(rides, 1, 0), block, 0)
        return b + count

    lax.fori_loop(0, z.degrees, degree, 0)


def pack(z, grid_field, f, slots, *tables):
    total = z.devices * slots
    smem = pl.BlockSpec(memory_space=pltpu.SMEM)
    table = jax.ShapeDtypeStruct((z.devices * z.capacity if f else z.blocks,), jnp.int32)
    return pl.pallas_call(
        functools.partial(pack_kernel, z, f, slots),
        in_specs=[smem] * len(tables) + [pl.BlockSpec(memory_space=pl.ANY)],
        out_specs=[pl.BlockSpec(memory_space=pltpu.VMEM), smem],
        out_shape=[jax.ShapeDtypeStruct((total, z.local, z.width), jnp.bfloat16), table],
        scratch_shapes=[
            pltpu.VMEM((z.local, z.blocks, z.width), jnp.bfloat16),
            pltpu.VMEM(((z.local + 1) * (z.blocks + 1), z.width), jnp.float32),
            pltpu.SemaphoreType.DMA((PARTS,)),
        ]
        + [pltpu.SMEM((z.devices,), jnp.int32)] * (0 if f else 2),
        compiler_params=pltpu.CompilerParams(vmem_limit_bytes=VMEM),
        cost_estimate=pl.CostEstimate(flops=10**9, bytes_accessed=10**7, transcendentals=0),
        name=f"pack_{f}",
    )(*tables, grid_field)


def solve_kernel(z, f, slots, per_step, holder_ref, start_ref, mate_ref, me_ref, columns_ref, inverses_ref, *rest):
    (own, across, along, corner, own_odd, across_odd, along_odd, corner_odd, far) = rest[:9]
    out_ref, matrix_ref, square_ref, above_ref, below_ref, sems = rest[9:]
    strength = diffusion_numbers[f]
    step = pl.program_id(0)
    shape = (z.levels, z.width)
    me = me_ref[0]

    @pl.when(step == 0)
    def _():
        sources = [
            own.at[f], own_odd.at[f], across.at[f], across_odd.at[f],
            along.at[f], along_odd.at[f], corner.at[0], corner_odd.at[0],
            inverses_ref.at[f, 0], far.at[f],
        ]
        copies = [
            pltpu.make_async_copy(source, matrix_ref.at[i], sems.at[i])
            for i, source in enumerate(sources)
        ]
        for copy in copies:
            copy.start()
        level = lax.broadcasted_iota(jnp.int32, shape, 0)

        def radius(positions):
            return inner_radius + shell_depth * (positions + 1).astype(jnp.float32) / (z.levels + 1)

        here = radius(level)
        scaled = (shell_depth / (z.levels + 1)) / here
        square_ref[...] = strength * (scaled * scaled)
        above_ref[...] = jnp.where(level == z.levels - 1, 0.0, strength * radius(level + 1) / here)
        below_ref[...] = jnp.where(level == 0, 0.0, strength * radius(level - 1) / here)
        for copy in copies:
            copy.wait()

    column = lax.broadcasted_iota(jnp.int32, shape, 1)
    host = quotient(holder_ref[me * slots], OB, z.degrees * OB)
    rider = mate_ref[host]
    host_at = z.turns(host) - step * per_step
    rides = (rider >= 0) & (host_at >= 0) & (host_at < per_step)

    def block(i, carry):
        again = i >= per_step
        k = jnp.where(again, host_at, i)
        code = holder_ref[me * slots + jnp.minimum(step * per_step + k, slots - 1)]
        q = jnp.where(again, rider, quotient(code, OB, z.degrees * OB))
        value = z.spacing * (q + 1) - 1
        last = value - lax.rem(code, OB) * (z.width // 2)
        begin = jnp.where(again, z.last_live(host), 0)
        end = jnp.where(again, begin + z.last_live(rider), 2 * last + 2)
        offset = z.owner(start_ref[q]) ^ me
        which = jnp.where(offset < PLANE, offset, PLANE + 1)
        which = jnp.where(q >= z.degrees // 2, which, PLANE)
        factor = (value * (value + 1)).astype(jnp.float32)
        u = columns_ref[:, k].reshape(shape).astype(jnp.float32)
        u = jnp.where((column >= begin) & (column < end), u, 0.0)
        weight = (1.0 - 2.0 * strength) - factor * square_ref[...]
        rhs = weight * u
        rhs += above_ref[...] * pltpu.roll(u, z.levels - 1, 0)
        rhs += below_ref[...] * pltpu.roll(u, 1, 0)
        high = rhs.astype(jnp.bfloat16)
        low = (rhs - high.astype(jnp.float32)).astype(jnp.bfloat16)
        both = jnp.concatenate([high, low], axis=1)
        product = jnp.dot(matrix_ref[which], both, preferred_element_type=jnp.float32)
        solved = product[:, : z.width] + product[:, z.width :]
        earlier = out_ref[:, k].reshape(shape).astype(jnp.float32)
        solved = jnp.where(column >= begin, solved, earlier).astype(jnp.bfloat16)
        out_ref[:, k] = solved.reshape(z.devices, z.local, z.width)
        return carry

    lax.fori_loop(0, per_step + jnp.where(rides, 1, 0), block, 0)


def solve(z, holder, degree_start, mate, me, columns, inverses, pieces, f, slots):
    steps = pl.cdiv(slots, 5)
    per_step = pl.cdiv(slots, steps)
    block = (z.devices, per_step, z.local, z.width)
    spec = pl.BlockSpec(block, lambda i, *s: (0, i, 0, 0))
    return pl.pallas_call(
        functools.partial(solve_kernel, z, f, slots, per_step),
        grid_spec=pltpu.PrefetchScalarGridSpec(
            num_scalar_prefetch=4,
            grid=(steps,),
            in_specs=[spec] + [pl.BlockSpec(memory_space=pl.ANY)] * (1 + len(pieces)),
            out_specs=spec,
            scratch_shapes=[pltpu.VMEM((PLANE + 2, z.levels, z.levels), jnp.bfloat16)]
            + [pltpu.VMEM((z.levels, z.width), jnp.float32)] * 3
            + [pltpu.SemaphoreType.DMA((PLANE + 2,))],
        ),
        out_shape=jax.ShapeDtypeStruct(columns.shape, jnp.bfloat16),
        compiler_params=pltpu.CompilerParams(vmem_limit_bytes=VMEM),
        cost_estimate=pl.CostEstimate(flops=10**10, bytes_accessed=10**7, transcendentals=0),
        name=f"solve_{f}",
    )(holder, degree_start, mate, me, columns, inverses, *pieces)


def edge_slopes(z, second, before_last, before, after):
    def wide(ref):
        return ref[...].reshape(z.blocks, z.width).astype(jnp.float32)

    first = 0.5 * (wide(second) - wide(before))
    last = 0.5 * (wide(after) - wide(before_last))
    return first.astype(jnp.bfloat16), last.astype(jnp.bfloat16)


def unpack_kernel(z, f, place_ref, mate_ref, returned_ref, *rest):
    if f:
        earlier_ref, _, before_ref, after_ref, grid_ref, slope_ref, second_ref, before_last_ref = rest[:8]
        edge_ref, edge_sems = rest[-2:]
    else:
        grid_ref, slope_ref = rest[:2]
    level_ref, inner_ref, wide_ref, sems = rest[8 if f else 2 :][:4]
    pitch = z.blocks + 1
    ends = [
        pltpu.make_async_copy(
            earlier_ref.at[f - 1, level], edge_ref.at[i], edge_sems.at[i]
        )
        for i, level in enumerate((1, z.local - 2))
    ] if f else []
    for copy in ends:
        copy.start()

    def gather(g, carry):
        for k in range(BATCH):
            b = g * BATCH + k
            tile = returned_ref[place_ref[b]].astype(jnp.float32)
            wide_ref[pl.ds(b, z.local, stride=pitch), :] = tile
        return carry

    lax.fori_loop(0, z.blocks // BATCH, gather, 0)
    column = lax.broadcasted_iota(jnp.int32, (z.local, z.width), 1)

    def ride(q, carry):
        b, host_block, live = riding(z, mate_ref, q)
        tile = returned_ref[place_ref[b]].astype(jnp.float32)
        rider = pltpu.roll(tile, z.width - live, 1)
        host_rows = pl.ds(host_block, z.local, stride=pitch)
        wide_ref[host_rows, :] = jnp.where(column < live, tile, 0.0)
        rows = pl.ds(b, z.local, stride=pitch)
        wide_ref[rows, :] = jnp.where(column < z.last_live(q), rider, 0.0)
        return carry

    lax.fori_loop(z.degrees // 2, z.degrees, ride, 0, unroll=RIDES)

    def group(g, carry):
        at = pl.multiple_of(g * GROUP, GROUP)
        rows = pl.ds(at, GROUP)
        value = [wide_ref[pl.ds(at + i * pitch, GROUP), :] for i in range(z.local)]
        for i in range(z.local):
            level_ref[i, rows, :] = value[i].astype(jnp.bfloat16)
        for i in range(1, z.local - 1):
            slope = 0.5 * (value[i + 1] - value[i - 1])
            inner_ref[i - 1, rows, :] = slope.astype(jnp.bfloat16)
        if f:
            second_ref[rows, :] = value[1].astype(jnp.bfloat16)
            before_last_ref[rows, :] = value[-2].astype(jnp.bfloat16)
        return carry

    groups = z.blocks // GROUP
    copies = []
    for i in range(PARTS):
        begin, end = i * groups // PARTS, (i + 1) * groups // PARTS
        lax.fori_loop(begin, end, group, 0)
        rows = pl.ds(begin * GROUP, (end - begin) * GROUP)
        copies += [
            pltpu.make_async_copy(
                level_ref.at[:, rows, :], grid_ref.at[f, :, rows, :], sems.at[2 * i]
            ),
            pltpu.make_async_copy(
                inner_ref.at[:, rows, :],
                slope_ref.at[f, pl.ds(1, z.local - 2), rows, :],
                sems.at[2 * i + 1],
            ),
        ]
        for copy in copies[-2:]:
            copy.start()
    if f:
        for copy in ends:
            copy.wait()
        slopes = edge_slopes(z, edge_ref.at[0], edge_ref.at[1], before_ref, after_ref)
        for i, level in enumerate((0, z.local - 1)):
            edge_ref[2 + i] = slopes[i]
            copy = pltpu.make_async_copy(
                edge_ref.at[2 + i], slope_ref.at[f - 1, level], edge_sems.at[2 + i]
            )
            copy.start()
            copies.append(copy)
    for copy in copies:
        copy.wait()


def unpack(z, place, mate, returned, f, earlier):
    whole = jax.ShapeDtypeStruct((z.fields, z.local, z.blocks, z.width), jnp.bfloat16)
    level = jax.ShapeDtypeStruct((z.blocks, z.width), jnp.bfloat16)
    smem, anywhere = pl.BlockSpec(memory_space=pltpu.SMEM), pl.BlockSpec(memory_space=pl.ANY)
    vmem = pl.BlockSpec(memory_space=pltpu.VMEM)
    edge_scratch = [
        pltpu.VMEM((4, z.blocks, z.width), jnp.bfloat16),
        pltpu.SemaphoreType.DMA((4,)),
    ]
    return pl.pallas_call(
        functools.partial(unpack_kernel, z, f),
        in_specs=[smem, smem, vmem] + [anywhere, anywhere, vmem, vmem] * min(f, 1),
        out_specs=[anywhere] * 2 + [vmem] * 2 * min(f, 1),
        out_shape=[whole] * 2 + [level] * 2 * min(f, 1),
        scratch_shapes=[
            pltpu.VMEM((z.local, z.blocks, z.width), jnp.bfloat16),
            pltpu.VMEM((z.local - 2, z.blocks, z.width), jnp.bfloat16),
            pltpu.VMEM(((z.local + 1) * (z.blocks + 1), z.width), jnp.float32),
            pltpu.SemaphoreType.DMA((2 * PARTS,)),
        ]
        + edge_scratch * min(f, 1),
        input_output_aliases={3: 0, 4: 1} if f else {},
        compiler_params=pltpu.CompilerParams(vmem_limit_bytes=VMEM if f else MORE_VMEM),
        cost_estimate=pl.CostEstimate(flops=10**9, bytes_accessed=10**7, transcendentals=0),
        name=f"unpack_{f}",
    )(place, mate, returned, *earlier)


def rim_kernel(z, place_ref, mate_ref, returned_ref, first_ref, last_ref, first_wide_ref, last_wide_ref):
    sides = ((first_wide_ref, 0), (last_wide_ref, z.local - 1))

    def gather(g, carry):
        for k in range(BATCH):
            b = g * BATCH + k
            tile = returned_ref[place_ref[b]].astype(jnp.float32)
            for wide_ref, row in sides:
                wide_ref[pl.ds(b, 1), :] = tile[row : row + 1]
        return carry

    lax.fori_loop(0, z.blocks // BATCH, gather, 0)
    column = lax.broadcasted_iota(jnp.int32, (z.local, z.width), 1)

    def ride(q, carry):
        b, host_block, live = riding(z, mate_ref, q)
        tile = returned_ref[place_ref[b]].astype(jnp.float32)
        rider = pltpu.roll(tile, z.width - live, 1)
        rider = jnp.where(column < z.last_live(q), rider, 0.0)
        tile = jnp.where(column < live, tile, 0.0)
        for wide_ref, row in sides:
            wide_ref[pl.ds(host_block, 1), :] = tile[row : row + 1]
            wide_ref[pl.ds(b, 1), :] = rider[row : row + 1]
        return carry

    lax.fori_loop(z.degrees // 2, z.degrees, ride, 0, unroll=RIDES)
    first_ref[0] = first_wide_ref[...].astype(jnp.bfloat16)
    last_ref[0] = last_wide_ref[...].astype(jnp.bfloat16)


def rims(z, place, mate, returned, f):
    level = jax.ShapeDtypeStruct((1, z.blocks, z.width), jnp.bfloat16)
    spec = pl.BlockSpec(level.shape, lambda i, *s: (0, 0, 0))
    return pl.pallas_call(
        functools.partial(rim_kernel, z),
        grid_spec=pltpu.PrefetchScalarGridSpec(
            num_scalar_prefetch=2,
            grid=(1,),
            in_specs=[pl.BlockSpec(returned.shape, lambda i, *s: (0, 0, 0))],
            out_specs=[spec, spec],
            scratch_shapes=[pltpu.VMEM((z.blocks, z.width), jnp.float32)] * 2,
        ),
        out_shape=[level, level],
        compiler_params=pltpu.CompilerParams(vmem_limit_bytes=VMEM if f else MORE_VMEM),
        cost_estimate=pl.CostEstimate(flops=10**8, bytes_accessed=3 * 10**6, transcendentals=0),
        name=f"rims_{f}",
    )(place, mate, returned)


def edge_kernel(z, f, second_ref, before_last_ref, before_ref, after_ref, _, slope_ref, edge_ref, sems):
    slopes = edge_slopes(z, second_ref, before_last_ref, before_ref, after_ref)
    copies = []
    for i, level in enumerate((0, z.local - 1)):
        edge_ref[i] = slopes[i]
        copies.append(pltpu.make_async_copy(edge_ref.at[i], slope_ref.at[f, level], sems.at[i]))
        copies[i].start()
    for copy in copies:
        copy.wait()


def edges(z, slope, inside, outside, f):
    vmem, anywhere = pl.BlockSpec(memory_space=pltpu.VMEM), pl.BlockSpec(memory_space=pl.ANY)
    return pl.pallas_call(
        functools.partial(edge_kernel, z, f),
        in_specs=[vmem] * 4 + [anywhere],
        out_specs=anywhere,
        out_shape=jax.ShapeDtypeStruct(slope.shape, slope.dtype),
        scratch_shapes=[
            pltpu.VMEM((2, z.blocks, z.width), jnp.bfloat16),
            pltpu.SemaphoreType.DMA((2,)),
        ],
        input_output_aliases={4: 0},
        compiler_params=pltpu.CompilerParams(vmem_limit_bytes=VMEM),
        name=f"edges_{f}",
    )(*inside, *outside, slope)


def beside(z, first, last):
    up = [(i, i + 1) for i in range(z.devices - 1)]
    down = [(j, i) for i, j in up]
    return lax.ppermute(last, AXES, up), lax.ppermute(first, AXES, down)


def exchange(z, value, slots):
    shaped = value.reshape(z.devices, slots, z.local, z.width)
    return lax.all_to_all(shaped, AXES, split_axis=0, concat_axis=0, tiled=True)


def body(grid_field, inverses, slot_blocks, degree_start):
    rad, lm = lax.axis_size("rad"), lax.axis_size("lm")
    z = Sizes(rad * lm, grid_field, inverses, slot_blocks)
    choices = slot_choices(z)
    kernels = z.local % 16 == 0 and z.fields == 2 and z.blocks % GROUP == 0 and rad % 4 == 0 and lm == PLANE // 2
    low, high = z.counts[z.degrees // 2 - 1 : z.degrees // 2 + 1]
    if not kernels or low + GIFT > choices[0] or high <= GIFT or z.capacity - choices[0] > GIFT:
        return plain_body(z, grid_field, inverses, degree_start)
    me = lax.axis_index(AXES).reshape(1).astype(jnp.int32)
    choice, *tables = plan(z, degree_start, choices)
    routes = [functools.partial(route, z, slots) for slots in choices]
    return lax.switch(choice[0], routes, grid_field, inverses, degree_start, me, *tables)


def route(z, slots, grid_field, inverses, degree_start, me, mate, load, high):
    sent_0, place = pack(z, grid_field, 0, slots, degree_start, mate, load, high)
    sent_1, holder = pack(z, grid_field, 1, slots, place, mate)
    sent_1, own, across, along, far = lax.optimization_barrier(
        (sent_1, *straight_inverses(inverses))
    )
    columns = [exchange(z, sent, slots) for sent in (sent_0, sent_1)]
    corner_0 = swap(across[:1], "rad", 1)
    even = [own, across, along]
    odd = other_core(even)
    pieces = lax.optimization_barrier((*even, corner_0, *odd, *other_core([corner_0]), far))
    solved_0 = solve(z, holder, degree_start, mate, me, columns[0], inverses, pieces, 0, slots)
    corner_1 = swap(along[1:], "lm", 2)
    pieces = (*even, corner_1, *odd, *other_core([corner_1]), far)
    solved_1 = solve(z, holder, degree_start, mate, me, columns[1], inverses, pieces, 1, slots)
    solved = [solved_0, solved_1]
    returned = [
        exchange(z, solved[f], slots).reshape(z.devices * slots, z.local, z.width)
        for f in range(z.fields)
    ]
    outside = beside(z, *rims(z, place, mate, returned[0], 0))
    outs = unpack(z, place, mate, returned[0], 0, ())
    last, *outs = lax.optimization_barrier((returned[1], *outs))
    last_outside = beside(z, *rims(z, place, mate, last, 1))
    grid, slope, *inside = unpack(z, place, mate, last, 1, (*outs, *outside))
    return grid, edges(z, slope, inside, last_outside, 1)


def plain_body(z, grid_field, inverses, degree_start):
    index = np.arange(z.degrees)
    counts = np.asarray(z.counts)
    degree_of = np.repeat(index, counts)
    place_in = np.arange(z.blocks) - np.asarray(z.starts)[degree_of]
    value = z.spacing * (index + 1) - 1
    slot_place = degree_start[degree_of] + jnp.asarray(place_in, jnp.int32)
    total = z.devices * z.capacity
    holder = jnp.full((total,), z.blocks, jnp.int32)
    holder = holder.at[slot_place].set(jnp.arange(z.blocks, dtype=jnp.int32))
    sent = jnp.take(grid_field, holder, axis=2, mode="fill", fill_value=0)
    sent = sent.reshape(z.fields, z.local, z.devices, z.capacity, z.width)
    columns = lax.all_to_all(sent, AXES, split_axis=2, concat_axis=1, tiled=True)
    columns = columns.reshape(z.fields, z.levels, z.capacity, z.width)
    device = lax.axis_index(AXES)
    mine = lax.dynamic_slice_in_dim(holder, device * z.capacity, z.capacity)
    order = jnp.asarray(place_in)[:, None] * OB + np.arange(z.width)[None, :] // 2
    live_table = (order <= jnp.asarray(value[degree_of])[:, None]).astype(jnp.float32)
    live = jnp.take(live_table, mine, axis=0, mode="fill", fill_value=0)
    factor = (value * (value + 1)).astype(np.float32)[degree_of]
    factor = jnp.take(jnp.asarray(factor), mine, mode="fill", fill_value=0)
    upper = jnp.take(jnp.asarray(degree_of >= z.degrees // 2), mine, mode="fill", fill_value=False)
    radius = inner_radius + shell_depth * jnp.arange(z.levels + 2, dtype=jnp.float32) / (z.levels + 1)
    here = radius[1:-1][None, :, None, None]
    padded = jnp.pad(columns.astype(jnp.float32), ((0, 0), (1, 1), (0, 0), (0, 0)))
    weighted = padded * radius[None, :, None, None]
    second = (weighted[:, 2:] - 2.0 * weighted[:, 1:-1] + weighted[:, :-2]) / here
    scaled = (shell_depth / (z.levels + 1)) / here
    centre = padded[:, 1:-1]
    strength = jnp.asarray(diffusion_numbers, jnp.float32)[:, None, None, None]
    angular = factor[None, None, :, None] * (scaled * scaled) * centre
    rhs = (centre + strength * (second - angular)) * live[None, None]

    def solve_slot(carry, at):
        matrix = lax.dynamic_index_in_dim(
            inverses, upper[at].astype(jnp.int32), 1, keepdims=False
        ).astype(jnp.float32)
        block = lax.dynamic_index_in_dim(rhs, at, 2, keepdims=False)
        product = jnp.einsum("fij,fjc->fic", matrix, block, precision=lax.Precision.HIGHEST)
        return carry, product.astype(jnp.bfloat16)

    solved = lax.scan(solve_slot, 0, jnp.arange(z.capacity))[1]
    solved = jnp.moveaxis(solved, 0, 2)
    solved = solved.reshape(z.fields, z.devices, z.local, z.capacity, z.width)
    returned = lax.all_to_all(solved, AXES, split_axis=1, concat_axis=3, tiled=True)
    returned = returned.reshape(z.fields, z.local, total, z.width)
    grid = jnp.take(returned, slot_place, axis=2)
    before, after = beside(z, grid[:, :1], grid[:, -1:])
    rimmed = jnp.concatenate([before, grid, after], axis=1).astype(jnp.float32)
    return grid, (0.5 * (rimmed[:, 2:] - rimmed[:, :-2])).astype(jnp.bfloat16)


def solution(mesh):
    in_specs = (P(None, AXES), P(None, AXES), P(), P())
    out_specs = (P(None, AXES), P(None, AXES))
    return jax.shard_map(body, mesh=mesh, in_specs=in_specs, out_specs=out_specs, check_vma=False)
```

```python
import functools

import jax
import jax.numpy as jnp
import numpy as np
from jax import lax
from jax.experimental import pallas as pl
from jax.experimental.pallas import tpu as pltpu
from jax.sharding import PartitionSpec as P

LMAX1 = 1024
OB = 64
AXES = ("rad", "lm")
PLANE = 8
GIFT = 8
GROUP = 16
BATCH = 68
VMEM = 48 << 20
MORE_VMEM = 60 << 20
RIDES = 32
PARTS = 4

inner_radius = 0.35
shell_depth = 0.65
diffusion_numbers = (0.9, 0.4)


def quotient(value, divisor, bound):
    numbers = np.arange(bound)
    for shift in range(24):
        factor = -(-(1 << shift) // divisor)
        if bound * factor < 2**31 and np.all(numbers * factor >> shift == numbers // divisor):
            return lax.shift_right_logical(value * factor, jnp.int32(shift))
    return lax.div(value, divisor)


class Sizes:
    def __init__(self, devices, grid_field, inverses, slot_blocks):
        self.devices = devices
        self.fields, self.local, self.blocks, self.width = grid_field.shape
        self.levels = inverses.shape[-1]
        self.capacity = slot_blocks.shape[1]
        self.degrees = 2 * devices
        self.spacing = LMAX1 // self.degrees
        self.group_size = OB * self.degrees // LMAX1
        index = np.arange(self.degrees)
        self.counts = [int(c) for c in index // self.group_size + 1]
        self.starts = [int(s) for s in np.cumsum(self.counts) - self.counts]
        self.partial = [q for q in range(self.degrees) if (q + 1) % self.group_size]

    def turns(self, q):
        return quotient(q, self.group_size, self.degrees)

    def owner(self, slot):
        return quotient(slot, self.capacity, self.devices * self.capacity)

    def last_block(self, q):
        turns = self.turns(q)
        rest = q - turns * self.group_size
        whole = lax.shift_right_logical(self.group_size * turns * (turns + 1), 1)
        return whole + rest * (turns + 1) + turns

    def last_live(self, q):
        return 2 * self.spacing * (q - self.turns(q) * self.group_size + 1)


def slot_choices(z):
    mean = -(-z.blocks // z.devices)
    return sorted({min(mean + extra, z.capacity) for extra in (0, 1, 2, 3)} | {z.capacity})


def plan_kernel(z, choices, start_ref, choice_ref, mate_ref, load_ref, high_ref, count_ref, stack_ref):
    half = z.degrees // 2
    planes = z.devices // PLANE
    kinds = z.group_size
    owner = [z.owner(start_ref[q]) for q in range(z.degrees)]
    for q in range(half, z.degrees):
        load_ref[owner[q]] = start_ref[q] - owner[q] * z.capacity + z.counts[q]
        high_ref[owner[q]] = q
    for i in range(planes * kinds):
        count_ref[i] = 0
    for q in range(z.degrees):
        mate_ref[q] = -1
    for q in z.partial:
        if q < half:
            kind = quotient(owner[q], PLANE, z.devices) * kinds + q % kinds
            stack_ref[kind * PLANE + count_ref[kind]] = q
            count_ref[kind] += 1
    for q in sorted(z.partial, key=lambda q: -(q % kinds)):
        if q < half:
            continue
        first_kind = quotient(owner[q], PLANE, z.devices) * kinds
        kind = jnp.int32(-1)
        for i in range(kinds - 1 - q % kinds):
            kind = jnp.where(count_ref[first_kind + i] > 0, first_kind + i, kind)

        @pl.when(kind >= 0)
        def _(kind=kind, q=q):
            left = count_ref[kind] - 1
            count_ref[kind] = left
            host = stack_ref[kind * PLANE + left]
            mate_ref[q] = host
            mate_ref[host] = q
            load_ref[owner[q]] -= 1

    totals = plane_totals(z, load_ref)
    most = functools.reduce(jnp.maximum, [totals[g] + totals[g + 1] for g in range(0, planes, 2)])
    highest = functools.reduce(jnp.maximum, totals)
    choice = jnp.int32(0)
    for i in range(1, len(choices)):
        tried = choices[i - 1]
        beyond = (most > 2 * PLANE * tried) | (highest > PLANE * tried + GIFT * PLANE // 2)
        choice = jnp.where(beyond, i, choice)
    choice_ref[0] = choice


def plane_totals(z, load_ref):
    return [
        sum(load_ref[g * PLANE + e] for e in range(PLANE)) for g in range(z.devices // PLANE)
    ]


def plan(z, degree_start, choices):
    smem = pl.BlockSpec(memory_space=pltpu.SMEM)
    kinds = z.devices // PLANE * z.group_size
    return pl.pallas_call(
        functools.partial(plan_kernel, z, choices),
        in_specs=[smem],
        out_specs=[smem] * 4,
        out_shape=[
            jax.ShapeDtypeStruct((size,), jnp.int32)
            for size in (1, z.degrees, z.devices, z.devices)
        ],
        scratch_shapes=[pltpu.SMEM((kinds,), jnp.int32), pltpu.SMEM((kinds * PLANE,), jnp.int32)],
        name="plan",
    )(degree_start)


def assign(z, slots, start_ref, mate_ref, load_ref, high_ref, place_ref, kept_ref, room_ref):
    totals = plane_totals(z, load_ref)
    for d in range(z.devices):
        excess = totals[d // PLANE] - PLANE * slots - GIFT * (d % PLANE // 2)
        gift = jnp.int32(0) if d % 2 else jnp.clip(excess, 0, GIFT)
        kept_ref[d] = load_ref[d] - gift
        room_ref[d ^ PLANE] = slots - gift
    for q in range(z.degrees):
        first = start_ref[q] + z.owner(start_ref[q]) * (slots - z.capacity)
        for p in range(z.counts[q]):
            place_ref[z.starts[q] + p] = first + p
    for d in range(z.devices):
        if d % PLANE == 0:
            spare = (jnp.int32(d), kept_ref[d])
        q = high_ref[d]
        last = z.last_block(q)
        first = last - z.turns(q)
        offset = start_ref[q] - d * z.capacity
        kept = kept_ref[d] - offset

        def move(state, first=first):
            p, device, slot = state
            place_ref[first + p] = device * slots + slot
            fits = slot < room_ref[device]
            after = device + 1
            return (
                jnp.where(fits, p + 1, p),
                jnp.where(fits, device, after),
                jnp.where(fits, slot + 1, kept_ref[jnp.minimum(after, z.devices - 1)]),
            )

        spare = lax.while_loop(
            lambda state, kept=kept: state[0] < kept, move, (room_ref[d] - offset, *spare)
        )[1:]
        host = mate_ref[q]
        if d % 2 == 0:
            other = d ^ PLANE
            given = other * slots + room_ref[other] - kept

            def give(p, carry, given=given, first=first):
                place_ref[first + p] = given + p
                return carry

            lax.fori_loop(kept, last - first + 1 - jnp.where(host >= 0, 1, 0), give, 0)
        start = start_ref[jnp.maximum(host, 0)]
        shared = start + z.owner(start) * (slots - z.capacity) + z.turns(host)
        place_ref[last] = jnp.where(host >= 0, shared, place_ref[last])


def swap(value, axis, bit):
    size = lax.axis_size(axis)
    return lax.ppermute(value, axis, [(i, i ^ bit) for i in range(size)])


def straight_inverses(inverses):
    own = inverses[:, 1]
    rad, lm = lax.axis_size("rad"), lax.axis_size("lm")
    facing = [(d, d ^ PLANE) for d in range(0, rad * lm, 2)]
    return own, swap(own, "lm", 2), swap(own, "rad", 1), lax.ppermute(own, AXES, facing)


def other_core(values):
    return [swap(value, "lm", 1) for value in values]


def riding(z, mate_ref, q):
    b, host = z.last_block(q), mate_ref[q]
    rides = host >= 0
    host = jnp.maximum(host, 0)
    return b, jnp.where(rides, z.last_block(host), b), jnp.where(rides, z.last_live(host), z.width)


def pack_kernel(z, f, slots, *refs):
    if f:
        place_ref, mate_ref, field_ref, out_ref, holder_ref, part_ref, wide_ref, sems = refs
    else:
        start_ref, mate_ref, load_ref, high_ref, field_ref, out_ref, place_ref = refs[:7]
        part_ref, wide_ref, sems, kept_ref, room_ref = refs[7:]
    pitch = z.blocks + 1
    some = z.local // PARTS
    copies = [
        pltpu.make_async_copy(
            field_ref.at[f, pl.ds(i * some, some)], part_ref.at[pl.ds(i * some, some)], sems.at[i]
        )
        for i in range(PARTS)
    ]
    for copy in copies:
        copy.start()
    if not f:
        assign(z, slots, start_ref, mate_ref, load_ref, high_ref, place_ref, kept_ref, room_ref)
    for level in range(z.local):
        if level % some == 0:
            copies[level // some].wait()
        wide_ref[pl.ds(level * pitch, z.blocks), :] = part_ref[level].astype(jnp.float32)

    def group(g, carry):
        for k in range(BATCH):
            b = g * BATCH + k
            tile = wide_ref[pl.ds(b, z.local, stride=pitch), :]
            out_ref[place_ref[b]] = tile.astype(jnp.bfloat16)
        return carry

    lax.fori_loop(0, z.blocks // BATCH, group, 0)
    column = lax.broadcasted_iota(jnp.int32, (z.local, z.width), 1)

    def ride(q, carry):
        b, host_block, live = riding(z, mate_ref, q)
        rider = pltpu.roll(wide_ref[pl.ds(b, z.local, stride=pitch), :], live, 1)
        tile = wide_ref[pl.ds(host_block, z.local, stride=pitch), :]
        out_ref[place_ref[b]] = jnp.where(column < live, tile, rider).astype(jnp.bfloat16)
        return carry

    lax.fori_loop(z.degrees // 2, z.degrees, ride, 0, unroll=RIDES)
    if not f:
        return

    def clear(k, carry):
        holder_ref[k] = 0
        return carry

    lax.fori_loop(0, z.devices * z.capacity, clear, 0, unroll=8)

    def degree(q, b):
        def block(p, inner):
            holder_ref[place_ref[b + p]] = q * OB + p
            return inner

        count = z.turns(q) + 1
        rides = (q >= z.degrees // 2) & (mate_ref[q] >= 0)
        lax.fori_loop(0, count - jnp.where(rides, 1, 0), block, 0)
        return b + count

    lax.fori_loop(0, z.degrees, degree, 0)


def pack(z, grid_field, f, slots, *tables):
    total = z.devices * slots
    smem = pl.BlockSpec(memory_space=pltpu.SMEM)
    table = jax.ShapeDtypeStruct((z.devices * z.capacity if f else z.blocks,), jnp.int32)
    return pl.pallas_call(
        functools.partial(pack_kernel, z, f, slots),
        in_specs=[smem] * len(tables) + [pl.BlockSpec(memory_space=pl.ANY)],
        out_specs=[pl.BlockSpec(memory_space=pltpu.VMEM), smem],
        out_shape=[jax.ShapeDtypeStruct((total, z.local, z.width), jnp.bfloat16), table],
        scratch_shapes=[
            pltpu.VMEM((z.local, z.blocks, z.width), jnp.bfloat16),
            pltpu.VMEM(((z.local + 1) * (z.blocks + 1), z.width), jnp.float32),
            pltpu.SemaphoreType.DMA((PARTS,)),
        ]
        + [pltpu.SMEM((z.devices,), jnp.int32)] * (0 if f else 2),
        compiler_params=pltpu.CompilerParams(vmem_limit_bytes=VMEM),
        cost_estimate=pl.CostEstimate(flops=10**9, bytes_accessed=10**7, transcendentals=0),
        name=f"pack_{f}",
    )(*tables, grid_field)


def solve_kernel(z, f, slots, per_step, holder_ref, start_ref, mate_ref, me_ref, columns_ref, inverses_ref, *rest):
    (own, across, along, corner, own_odd, across_odd, along_odd, corner_odd, far) = rest[:9]
    out_ref, matrix_ref, square_ref, above_ref, below_ref, sems = rest[9:]
    strength = diffusion_numbers[f]
    step = pl.program_id(0)
    shape = (z.levels, z.width)
    me = me_ref[0]

    @pl.when(step == 0)
    def _():
        sources = [
            own.at[f], own_odd.at[f], across.at[f], across_odd.at[f],
            along.at[f], along_odd.at[f], corner.at[0], corner_odd.at[0],
            inverses_ref.at[f, 0], far.at[f],
        ]
        copies = [
            pltpu.make_async_copy(source, matrix_ref.at[i], sems.at[i])
            for i, source in enumerate(sources)
        ]
        for copy in copies:
            copy.start()
        level = lax.broadcasted_iota(jnp.int32, shape, 0)

        def radius(positions):
            return inner_radius + shell_depth * (positions + 1).astype(jnp.float32) / (z.levels + 1)

        here = radius(level)
        scaled = (shell_depth / (z.levels + 1)) / here
        square_ref[...] = strength * (scaled * scaled)
        above_ref[...] = jnp.where(level == z.levels - 1, 0.0, strength * radius(level + 1) / here)
        below_ref[...] = jnp.where(level == 0, 0.0, strength * radius(level - 1) / here)
        for copy in copies:
            copy.wait()

    column = lax.broadcasted_iota(jnp.int32, shape, 1)
    host = quotient(holder_ref[me * slots], OB, z.degrees * OB)
    rider = mate_ref[host]
    host_at = z.turns(host) - step * per_step
    rides = (rider >= 0) & (host_at >= 0) & (host_at < per_step)

    def block(i, carry):
        again = i >= per_step
        k = jnp.where(again, host_at, i)
        code = holder_ref[me * slots + jnp.minimum(step * per_step + k, slots - 1)]
        q = jnp.where(again, rider, quotient(code, OB, z.degrees * OB))
        value = z.spacing * (q + 1) - 1
        last = value - lax.rem(code, OB) * (z.width // 2)
        begin = jnp.where(again, z.last_live(host), 0)
        end = jnp.where(again, begin + z.last_live(rider), 2 * last + 2)
        offset = z.owner(start_ref[q]) ^ me
        which = jnp.where(offset < PLANE, offset, PLANE + 1)
        which = jnp.where(q >= z.degrees // 2, which, PLANE)
        factor = (value * (value + 1)).astype(jnp.float32)
        u = columns_ref[:, k].reshape(shape).astype(jnp.float32)
        u = jnp.where((column >= begin) & (column < end), u, 0.0)
        weight = (1.0 - 2.0 * strength) - factor * square_ref[...]
        rhs = weight * u
        rhs += above_ref[...] * pltpu.roll(u, z.levels - 1, 0)
        rhs += below_ref[...] * pltpu.roll(u, 1, 0)
        high = rhs.astype(jnp.bfloat16)
        low = (rhs - high.astype(jnp.float32)).astype(jnp.bfloat16)
        both = jnp.concatenate([high, low], axis=1)
        product = jnp.dot(matrix_ref[which], both, preferred_element_type=jnp.float32)
        solved = product[:, : z.width] + product[:, z.width :]
        earlier = out_ref[:, k].reshape(shape).astype(jnp.float32)
        solved = jnp.where(column >= begin, solved, earlier).astype(jnp.bfloat16)
        out_ref[:, k] = solved.reshape(z.devices, z.local, z.width)
        return carry

    lax.fori_loop(0, per_step + jnp.where(rides, 1, 0), block, 0)


def solve(z, holder, degree_start, mate, me, columns, inverses, pieces, f, slots):
    steps = pl.cdiv(slots, 9)
    per_step = pl.cdiv(slots, steps)
    block = (z.devices, per_step, z.local, z.width)
    spec = pl.BlockSpec(block, lambda i, *s: (0, i, 0, 0))
    return pl.pallas_call(
        functools.partial(solve_kernel, z, f, slots, per_step),
        grid_spec=pltpu.PrefetchScalarGridSpec(
            num_scalar_prefetch=4,
            grid=(steps,),
            in_specs=[spec] + [pl.BlockSpec(memory_space=pl.ANY)] * (1 + len(pieces)),
            out_specs=spec,
            scratch_shapes=[pltpu.VMEM((PLANE + 2, z.levels, z.levels), jnp.bfloat16)]
            + [pltpu.VMEM((z.levels, z.width), jnp.float32)] * 3
            + [pltpu.SemaphoreType.DMA((PLANE + 2,))],
        ),
        out_shape=jax.ShapeDtypeStruct(columns.shape, jnp.bfloat16),
        compiler_params=pltpu.CompilerParams(vmem_limit_bytes=VMEM),
        cost_estimate=pl.CostEstimate(flops=10**10, bytes_accessed=10**7, transcendentals=0),
        name=f"solve_{f}",
    )(holder, degree_start, mate, me, columns, inverses, *pieces)


def edge_slopes(z, second, before_last, before, after):
    def wide(ref):
        return ref[...].reshape(z.blocks, z.width).astype(jnp.float32)

    first = 0.5 * (wide(second) - wide(before))
    last = 0.5 * (wide(after) - wide(before_last))
    return first.astype(jnp.bfloat16), last.astype(jnp.bfloat16)


def unpack_kernel(z, f, place_ref, mate_ref, returned_ref, *rest):
    if f:
        earlier_ref, _, before_ref, after_ref, grid_ref, slope_ref, second_ref, before_last_ref = rest[:8]
        edge_ref, edge_sems = rest[-2:]
    else:
        grid_ref, slope_ref = rest[:2]
    level_ref, inner_ref, wide_ref, sems = rest[8 if f else 2 :][:4]
    pitch = z.blocks + 1
    ends = [
        pltpu.make_async_copy(
            earlier_ref.at[f - 1, level], edge_ref.at[i], edge_sems.at[i]
        )
        for i, level in enumerate((1, z.local - 2))
    ] if f else []
    for copy in ends:
        copy.start()

    def gather(g, carry):
        for k in range(BATCH):
            b = g * BATCH + k
            tile = returned_ref[place_ref[b]].astype(jnp.float32)
            wide_ref[pl.ds(b, z.local, stride=pitch), :] = tile
        return carry

    lax.fori_loop(0, z.blocks // BATCH, gather, 0)
    column = lax.broadcasted_iota(jnp.int32, (z.local, z.width), 1)

    def ride(q, carry):
        b, host_block, live = riding(z, mate_ref, q)
        tile = returned_ref[place_ref[b]].astype(jnp.float32)
        rider = pltpu.roll(tile, z.width - live, 1)
        host_rows = pl.ds(host_block, z.local, stride=pitch)
        wide_ref[host_rows, :] = jnp.where(column < live, tile, 0.0)
        rows = pl.ds(b, z.local, stride=pitch)
        wide_ref[rows, :] = jnp.where(column < z.last_live(q), rider, 0.0)
        return carry

    lax.fori_loop(z.degrees // 2, z.degrees, ride, 0, unroll=RIDES)

    def group(g, carry):
        at = pl.multiple_of(g * GROUP, GROUP)
        rows = pl.ds(at, GROUP)
        value = [wide_ref[pl.ds(at + i * pitch, GROUP), :] for i in range(z.local)]
        for i in range(z.local):
            level_ref[i, rows, :] = value[i].astype(jnp.bfloat16)
        for i in range(1, z.local - 1):
            slope = 0.5 * (value[i + 1] - value[i - 1])
            inner_ref[i - 1, rows, :] = slope.astype(jnp.bfloat16)
        if f:
            second_ref[rows, :] = value[1].astype(jnp.bfloat16)
            before_last_ref[rows, :] = value[-2].astype(jnp.bfloat16)
        return carry

    groups = z.blocks // GROUP
    copies = []
    for i in range(PARTS):
        begin, end = i * groups // PARTS, (i + 1) * groups // PARTS
        lax.fori_loop(begin, end, group, 0, unroll=2)
        rows = pl.ds(begin * GROUP, (end - begin) * GROUP)
        copies += [
            pltpu.make_async_copy(
                level_ref.at[:, rows, :], grid_ref.at[f, :, rows, :], sems.at[2 * i]
            ),
            pltpu.make_async_copy(
                inner_ref.at[:, rows, :],
                slope_ref.at[f, pl.ds(1, z.local - 2), rows, :],
                sems.at[2 * i + 1],
            ),
        ]
        for copy in copies[-2:]:
            copy.start()
    if f:
        for copy in ends:
            copy.wait()
        slopes = edge_slopes(z, edge_ref.at[0], edge_ref.at[1], before_ref, after_ref)
        for i, level in enumerate((0, z.local - 1)):
            edge_ref[2 + i] = slopes[i]
            copy = pltpu.make_async_copy(
                edge_ref.at[2 + i], slope_ref.at[f - 1, level], edge_sems.at[2 + i]
            )
            copy.start()
            copies.append(copy)
    for copy in copies:
        copy.wait()


def unpack(z, place, mate, returned, f, earlier):
    whole = jax.ShapeDtypeStruct((z.fields, z.local, z.blocks, z.width), jnp.bfloat16)
    level = jax.ShapeDtypeStruct((z.blocks, z.width), jnp.bfloat16)
    smem, anywhere = pl.BlockSpec(memory_space=pltpu.SMEM), pl.BlockSpec(memory_space=pl.ANY)
    vmem = pl.BlockSpec(memory_space=pltpu.VMEM)
    edge_scratch = [
        pltpu.VMEM((4, z.blocks, z.width), jnp.bfloat16),
        pltpu.SemaphoreType.DMA((4,)),
    ]
    return pl.pallas_call(
        functools.partial(unpack_kernel, z, f),
        in_specs=[smem, smem, vmem] + [anywhere, anywhere, vmem, vmem] * min(f, 1),
        out_specs=[anywhere] * 2 + [vmem] * 2 * min(f, 1),
        out_shape=[whole] * 2 + [level] * 2 * min(f, 1),
        scratch_shapes=[
            pltpu.VMEM((z.local, z.blocks, z.width), jnp.bfloat16),
            pltpu.VMEM((z.local - 2, z.blocks, z.width), jnp.bfloat16),
            pltpu.VMEM(((z.local + 1) * (z.blocks + 1), z.width), jnp.float32),
            pltpu.SemaphoreType.DMA((2 * PARTS,)),
        ]
        + edge_scratch * min(f, 1),
        input_output_aliases={3: 0, 4: 1} if f else {},
        compiler_params=pltpu.CompilerParams(vmem_limit_bytes=VMEM if f else MORE_VMEM),
        cost_estimate=pl.CostEstimate(flops=10**9, bytes_accessed=10**7, transcendentals=0),
        name=f"unpack_{f}",
    )(place, mate, returned, *earlier)


def rim_kernel(z, place_ref, mate_ref, returned_ref, first_ref, last_ref, first_wide_ref, last_wide_ref):
    sides = ((first_wide_ref, 0), (last_wide_ref, z.local - 1))

    def gather(g, carry):
        for k in range(BATCH):
            b = g * BATCH + k
            tile = returned_ref[place_ref[b]].astype(jnp.float32)
            for wide_ref, row in sides:
                wide_ref[pl.ds(b, 1), :] = tile[row : row + 1]
        return carry

    lax.fori_loop(0, z.blocks // BATCH, gather, 0)
    column = lax.broadcasted_iota(jnp.int32, (z.local, z.width), 1)

    def ride(q, carry):
        b, host_block, live = riding(z, mate_ref, q)
        tile = returned_ref[place_ref[b]].astype(jnp.float32)
        rider = pltpu.roll(tile, z.width - live, 1)
        rider = jnp.where(column < z.last_live(q), rider, 0.0)
        tile = jnp.where(column < live, tile, 0.0)
        for wide_ref, row in sides:
            wide_ref[pl.ds(host_block, 1), :] = tile[row : row + 1]
            wide_ref[pl.ds(b, 1), :] = rider[row : row + 1]
        return carry

    lax.fori_loop(z.degrees // 2, z.degrees, ride, 0, unroll=RIDES)
    first_ref[0] = first_wide_ref[...].astype(jnp.bfloat16)
    last_ref[0] = last_wide_ref[...].astype(jnp.bfloat16)


def rims(z, place, mate, returned, f):
    level = jax.ShapeDtypeStruct((1, z.blocks, z.width), jnp.bfloat16)
    spec = pl.BlockSpec(level.shape, lambda i, *s: (0, 0, 0))
    return pl.pallas_call(
        functools.partial(rim_kernel, z),
        grid_spec=pltpu.PrefetchScalarGridSpec(
            num_scalar_prefetch=2,
            grid=(1,),
            in_specs=[pl.BlockSpec(returned.shape, lambda i, *s: (0, 0, 0))],
            out_specs=[spec, spec],
            scratch_shapes=[pltpu.VMEM((z.blocks, z.width), jnp.float32)] * 2,
        ),
        out_shape=[level, level],
        compiler_params=pltpu.CompilerParams(vmem_limit_bytes=VMEM if f else MORE_VMEM),
        cost_estimate=pl.CostEstimate(flops=10**8, bytes_accessed=3 * 10**6, transcendentals=0),
        name=f"rims_{f}",
    )(place, mate, returned)


def edge_kernel(z, f, second_ref, before_last_ref, before_ref, after_ref, _, slope_ref, edge_ref, sems):
    slopes = edge_slopes(z, second_ref, before_last_ref, before_ref, after_ref)
    copies = []
    for i, level in enumerate((0, z.local - 1)):
        edge_ref[i] = slopes[i]
        copies.append(pltpu.make_async_copy(edge_ref.at[i], slope_ref.at[f, level], sems.at[i]))
        copies[i].start()
    for copy in copies:
        copy.wait()


def edges(z, slope, inside, outside, f):
    vmem, anywhere = pl.BlockSpec(memory_space=pltpu.VMEM), pl.BlockSpec(memory_space=pl.ANY)
    return pl.pallas_call(
        functools.partial(edge_kernel, z, f),
        in_specs=[vmem] * 4 + [anywhere],
        out_specs=anywhere,
        out_shape=jax.ShapeDtypeStruct(slope.shape, slope.dtype),
        scratch_shapes=[
            pltpu.VMEM((2, z.blocks, z.width), jnp.bfloat16),
            pltpu.SemaphoreType.DMA((2,)),
        ],
        input_output_aliases={4: 0},
        compiler_params=pltpu.CompilerParams(vmem_limit_bytes=VMEM),
        name=f"edges_{f}",
    )(*inside, *outside, slope)


def beside(z, first, last):
    up = [(i, i + 1) for i in range(z.devices - 1)]
    down = [(j, i) for i, j in up]
    return lax.ppermute(last, AXES, up), lax.ppermute(first, AXES, down)


def exchange(z, value, slots):
    shaped = value.reshape(z.devices, slots, z.local, z.width)
    return lax.all_to_all(shaped, AXES, split_axis=0, concat_axis=0, tiled=True)


def body(grid_field, inverses, slot_blocks, degree_start):
    rad, lm = lax.axis_size("rad"), lax.axis_size("lm")
    z = Sizes(rad * lm, grid_field, inverses, slot_blocks)
    choices = slot_choices(z)
    kernels = z.local % 16 == 0 and z.fields == 2 and z.blocks % GROUP == 0 and z.blocks % BATCH == 0 and rad % 4 == 0 and lm == PLANE // 2
    low, high = z.counts[z.degrees // 2 - 1 : z.degrees // 2 + 1]
    if not kernels or low + GIFT > choices[0] or high <= GIFT or z.capacity - choices[0] > GIFT:
        return plain_body(z, grid_field, inverses, degree_start)
    me = lax.axis_index(AXES).reshape(1).astype(jnp.int32)
    choice, *tables = plan(z, degree_start, choices)
    routes = [functools.partial(route, z, slots) for slots in choices]
    return lax.switch(choice[0], routes, grid_field, inverses, degree_start, me, *tables)


def route(z, slots, grid_field, inverses, degree_start, me, mate, load, high):
    sent_0, place = pack(z, grid_field, 0, slots, degree_start, mate, load, high)
    sent_1, holder = pack(z, grid_field, 1, slots, place, mate)
    sent_1, own, across, along, far = lax.optimization_barrier(
        (sent_1, *straight_inverses(inverses))
    )
    columns = [exchange(z, sent, slots) for sent in (sent_0, sent_1)]
    corner_0 = swap(across[:1], "rad", 1)
    even = [own, across, along]
    odd = other_core(even)
    pieces = lax.optimization_barrier((*even, corner_0, *odd, *other_core([corner_0]), far))
    solved_0 = solve(z, holder, degree_start, mate, me, columns[0], inverses, pieces, 0, slots)
    corner_1 = swap(along[1:], "lm", 2)
    pieces = (*even, corner_1, *odd, *other_core([corner_1]), far)
    solved_1 = solve(z, holder, degree_start, mate, me, columns[1], inverses, pieces, 1, slots)
    solved = [solved_0, solved_1]
    returned = [
        exchange(z, solved[f], slots).reshape(z.devices * slots, z.local, z.width)
        for f in range(z.fields)
    ]
    outside = beside(z, *rims(z, place, mate, returned[0], 0))
    outs = unpack(z, place, mate, returned[0], 0, ())
    last, *outs = lax.optimization_barrier((returned[1], *outs))
    last_outside = beside(z, *rims(z, place, mate, last, 1))
    grid, slope, *inside = unpack(z, place, mate, last, 1, (*outs, *outside))
    return grid, edges(z, slope, inside, last_outside, 1)


def plain_body(z, grid_field, inverses, degree_start):
    index = np.arange(z.degrees)
    counts = np.asarray(z.counts)
    degree_of = np.repeat(index, counts)
    place_in = np.arange(z.blocks) - np.asarray(z.starts)[degree_of]
    value = z.spacing * (index + 1) - 1
    slot_place = degree_start[degree_of] + jnp.asarray(place_in, jnp.int32)
    total = z.devices * z.capacity
    holder = jnp.full((total,), z.blocks, jnp.int32)
    holder = holder.at[slot_place].set(jnp.arange(z.blocks, dtype=jnp.int32))
    sent = jnp.take(grid_field, holder, axis=2, mode="fill", fill_value=0)
    sent = sent.reshape(z.fields, z.local, z.devices, z.capacity, z.width)
    columns = lax.all_to_all(sent, AXES, split_axis=2, concat_axis=1, tiled=True)
    columns = columns.reshape(z.fields, z.levels, z.capacity, z.width)
    device = lax.axis_index(AXES)
    mine = lax.dynamic_slice_in_dim(holder, device * z.capacity, z.capacity)
    order = jnp.asarray(place_in)[:, None] * OB + np.arange(z.width)[None, :] // 2
    live_table = (order <= jnp.asarray(value[degree_of])[:, None]).astype(jnp.float32)
    live = jnp.take(live_table, mine, axis=0, mode="fill", fill_value=0)
    factor = (value * (value + 1)).astype(np.float32)[degree_of]
    factor = jnp.take(jnp.asarray(factor), mine, mode="fill", fill_value=0)
    upper = jnp.take(jnp.asarray(degree_of >= z.degrees // 2), mine, mode="fill", fill_value=False)
    radius = inner_radius + shell_depth * jnp.arange(z.levels + 2, dtype=jnp.float32) / (z.levels + 1)
    here = radius[1:-1][None, :, None, None]
    padded = jnp.pad(columns.astype(jnp.float32), ((0, 0), (1, 1), (0, 0), (0, 0)))
    weighted = padded * radius[None, :, None, None]
    second = (weighted[:, 2:] - 2.0 * weighted[:, 1:-1] + weighted[:, :-2]) / here
    scaled = (shell_depth / (z.levels + 1)) / here
    centre = padded[:, 1:-1]
    strength = jnp.asarray(diffusion_numbers, jnp.float32)[:, None, None, None]
    angular = factor[None, None, :, None] * (scaled * scaled) * centre
    rhs = (centre + strength * (second - angular)) * live[None, None]

    def solve_slot(carry, at):
        matrix = lax.dynamic_index_in_dim(
            inverses, upper[at].astype(jnp.int32), 1, keepdims=False
        ).astype(jnp.float32)
        block = lax.dynamic_index_in_dim(rhs, at, 2, keepdims=False)
        product = jnp.einsum("fij,fjc->fic", matrix, block, precision=lax.Precision.HIGHEST)
        return carry, product.astype(jnp.bfloat16)

    solved = lax.scan(solve_slot, 0, jnp.arange(z.capacity))[1]
    solved = jnp.moveaxis(solved, 0, 2)
    solved = solved.reshape(z.fields, z.devices, z.local, z.capacity, z.width)
    returned = lax.all_to_all(solved, AXES, split_axis=1, concat_axis=3, tiled=True)
    returned = returned.reshape(z.fields, z.local, total, z.width)
    grid = jnp.take(returned, slot_place, axis=2)
    before, after = beside(z, grid[:, :1], grid[:, -1:])
    rimmed = jnp.concatenate([before, grid, after], axis=1).astype(jnp.float32)
    return grid, (0.5 * (rimmed[:, 2:] - rimmed[:, :-2])).astype(jnp.bfloat16)


def solution(mesh):
    in_specs = (P(None, AXES), P(None, AXES), P(), P())
    out_specs = (P(None, AXES), P(None, AXES))
    return jax.shard_map(body, mesh=mesh, in_specs=in_specs, out_specs=out_specs, check_vma=False)
```

```python
import functools

import jax
import jax.numpy as jnp
import numpy as np
from jax import lax
from jax.experimental import pallas as pl
from jax.experimental.pallas import tpu as pltpu
from jax.sharding import PartitionSpec as P

LMAX1 = 1024
OB = 64
AXES = ("rad", "lm")
PLANE = 8
GIFT = 8
GROUP = 16
BATCH = 68
VMEM = 48 << 20
MORE_VMEM = 60 << 20
RIDES = 32
PARTS = 4

inner_radius = 0.35
shell_depth = 0.65
diffusion_numbers = (0.9, 0.4)


def quotient(value, divisor, bound):
    numbers = np.arange(bound)
    for shift in range(24):
        factor = -(-(1 << shift) // divisor)
        if bound * factor < 2**31 and np.all(numbers * factor >> shift == numbers // divisor):
            return lax.shift_right_logical(value * factor, jnp.int32(shift))
    return lax.div(value, divisor)


class Sizes:
    def __init__(self, devices, grid_field, inverses, slot_blocks):
        self.devices = devices
        self.fields, self.local, self.blocks, self.width = grid_field.shape
        self.levels = inverses.shape[-1]
        self.capacity = slot_blocks.shape[1]
        self.degrees = 2 * devices
        self.spacing = LMAX1 // self.degrees
        self.group_size = OB * self.degrees // LMAX1
        index = np.arange(self.degrees)
        self.counts = [int(c) for c in index // self.group_size + 1]
        self.starts = [int(s) for s in np.cumsum(self.counts) - self.counts]
        self.partial = [q for q in range(self.degrees) if (q + 1) % self.group_size]

    def turns(self, q):
        return quotient(q, self.group_size, self.degrees)

    def owner(self, slot):
        return quotient(slot, self.capacity, self.devices * self.capacity)

    def last_block(self, q):
        turns = self.turns(q)
        rest = q - turns * self.group_size
        whole = lax.shift_right_logical(self.group_size * turns * (turns + 1), 1)
        return whole + rest * (turns + 1) + turns

    def last_live(self, q):
        return 2 * self.spacing * (q - self.turns(q) * self.group_size + 1)


def slot_choices(z):
    mean = -(-z.blocks // z.devices)
    return sorted({min(mean + extra, z.capacity) for extra in (0, 1, 2)} | {z.capacity})


def plan_kernel(z, choices, start_ref, choice_ref, mate_ref, load_ref, high_ref, count_ref, stack_ref):
    half = z.degrees // 2
    planes = z.devices // PLANE
    kinds = z.group_size
    owner = [z.owner(start_ref[q]) for q in range(z.degrees)]
    for q in range(half, z.degrees):
        load_ref[owner[q]] = start_ref[q] - owner[q] * z.capacity + z.counts[q]
        high_ref[owner[q]] = q
    for i in range(planes * kinds):
        count_ref[i] = 0
    for q in range(z.degrees):
        mate_ref[q] = -1
    for q in z.partial:
        if q < half:
            kind = quotient(owner[q], PLANE, z.devices) * kinds + q % kinds
            stack_ref[kind * PLANE + count_ref[kind]] = q
            count_ref[kind] += 1
    for q in sorted(z.partial, key=lambda q: -(q % kinds)):
        if q < half:
            continue
        first_kind = quotient(owner[q], PLANE, z.devices) * kinds
        kind = jnp.int32(-1)
        for i in range(kinds - 1 - q % kinds):
            kind = jnp.where(count_ref[first_kind + i] > 0, first_kind + i, kind)

        @pl.when(kind >= 0)
        def _(kind=kind, q=q):
            left = count_ref[kind] - 1
            count_ref[kind] = left
            host = stack_ref[kind * PLANE + left]
            mate_ref[q] = host
            mate_ref[host] = q
            load_ref[owner[q]] -= 1

    totals = plane_totals(z, load_ref)
    most = functools.reduce(jnp.maximum, [totals[g] + totals[g + 1] for g in range(0, planes, 2)])
    highest = functools.reduce(jnp.maximum, totals)
    choice = jnp.int32(0)
    for i in range(1, len(choices)):
        tried = choices[i - 1]
        beyond = (most > 2 * PLANE * tried) | (highest > PLANE * tried + GIFT * PLANE // 2)
        choice = jnp.where(beyond, i, choice)
    choice_ref[0] = choice


def plane_totals(z, load_ref):
    return [
        sum(load_ref[g * PLANE + e] for e in range(PLANE)) for g in range(z.devices // PLANE)
    ]


def plan(z, degree_start, choices):
    smem = pl.BlockSpec(memory_space=pltpu.SMEM)
    kinds = z.devices // PLANE * z.group_size
    return pl.pallas_call(
        functools.partial(plan_kernel, z, choices),
        in_specs=[smem],
        out_specs=[smem] * 4,
        out_shape=[
            jax.ShapeDtypeStruct((size,), jnp.int32)
            for size in (1, z.degrees, z.devices, z.devices)
        ],
        scratch_shapes=[pltpu.SMEM((kinds,), jnp.int32), pltpu.SMEM((kinds * PLANE,), jnp.int32)],
        name="plan",
    )(degree_start)


def assign(z, slots, start_ref, mate_ref, load_ref, high_ref, place_ref, kept_ref, room_ref):
    totals = plane_totals(z, load_ref)
    for d in range(z.devices):
        excess = totals[d // PLANE] - PLANE * slots - GIFT * (d % PLANE // 2)
        gift = jnp.int32(0) if d % 2 else jnp.clip(excess, 0, GIFT)
        kept_ref[d] = load_ref[d] - gift
        room_ref[d ^ PLANE] = slots - gift
    for q in range(z.degrees):
        first = start_ref[q] + z.owner(start_ref[q]) * (slots - z.capacity)
        for p in range(z.counts[q]):
            place_ref[z.starts[q] + p] = first + p
    for d in range(z.devices):
        if d % PLANE == 0:
            spare = (jnp.int32(d), kept_ref[d])
        q = high_ref[d]
        last = z.last_block(q)
        first = last - z.turns(q)
        offset = start_ref[q] - d * z.capacity
        kept = kept_ref[d] - offset

        def move(state, first=first):
            p, device, slot = state
            place_ref[first + p] = device * slots + slot
            fits = slot < room_ref[device]
            after = device + 1
            return (
                jnp.where(fits, p + 1, p),
                jnp.where(fits, device, after),
                jnp.where(fits, slot + 1, kept_ref[jnp.minimum(after, z.devices - 1)]),
            )

        spare = lax.while_loop(
            lambda state, kept=kept: state[0] < kept, move, (room_ref[d] - offset, *spare)
        )[1:]
        host = mate_ref[q]
        if d % 2 == 0:
            other = d ^ PLANE
            given = other * slots + room_ref[other] - kept

            def give(p, carry, given=given, first=first):
                place_ref[first + p] = given + p
                return carry

            lax.fori_loop(kept, last - first + 1 - jnp.where(host >= 0, 1, 0), give, 0)
        start = start_ref[jnp.maximum(host, 0)]
        shared = start + z.owner(start) * (slots - z.capacity) + z.turns(host)
        place_ref[last] = jnp.where(host >= 0, shared, place_ref[last])


def swap(value, axis, bit):
    size = lax.axis_size(axis)
    return lax.ppermute(value, axis, [(i, i ^ bit) for i in range(size)])


def straight_inverses(inverses):
    own = inverses[:, 1]
    rad, lm = lax.axis_size("rad"), lax.axis_size("lm")
    facing = [(d, d ^ PLANE) for d in range(0, rad * lm, 2)]
    return own, swap(own, "lm", 2), swap(own, "rad", 1), lax.ppermute(own, AXES, facing)


def other_core(values):
    return [swap(value, "lm", 1) for value in values]


def riding(z, mate_ref, q):
    b, host = z.last_block(q), mate_ref[q]
    rides = host >= 0
    host = jnp.maximum(host, 0)
    return b, jnp.where(rides, z.last_block(host), b), jnp.where(rides, z.last_live(host), z.width)


def pack_kernel(z, f, slots, *refs):
    if f:
        place_ref, mate_ref, field_ref, out_ref, holder_ref, part_ref, wide_ref, sems = refs
    else:
        start_ref, mate_ref, load_ref, high_ref, field_ref, out_ref, place_ref = refs[:7]
        part_ref, wide_ref, sems, kept_ref, room_ref = refs[7:]
    pitch = z.blocks + 1
    some = z.local // PARTS
    copies = [
        pltpu.make_async_copy(
            field_ref.at[f, pl.ds(i * some, some)], part_ref.at[pl.ds(i * some, some)], sems.at[i]
        )
        for i in range(PARTS)
    ]
    for copy in copies:
        copy.start()
    if not f:
        assign(z, slots, start_ref, mate_ref, load_ref, high_ref, place_ref, kept_ref, room_ref)
    for level in range(z.local):
        if level % some == 0:
            copies[level // some].wait()
        wide_ref[pl.ds(level * pitch, z.blocks), :] = part_ref[level].astype(jnp.float32)

    def group(g, carry):
        for k in range(BATCH):
            b = g * BATCH + k
            tile = wide_ref[pl.ds(b, z.local, stride=pitch), :]
            out_ref[place_ref[b]] = tile.astype(jnp.bfloat16)
        return carry

    lax.fori_loop(0, z.blocks // BATCH, group, 0)
    column = lax.broadcasted_iota(jnp.int32, (z.local, z.width), 1)

    def ride(q, carry):
        b, host_block, live = riding(z, mate_ref, q)
        rider = pltpu.roll(wide_ref[pl.ds(b, z.local, stride=pitch), :], live, 1)
        tile = wide_ref[pl.ds(host_block, z.local, stride=pitch), :]
        out_ref[place_ref[b]] = jnp.where(column < live, tile, rider).astype(jnp.bfloat16)
        return carry

    lax.fori_loop(z.degrees // 2, z.degrees, ride, 0, unroll=RIDES)
    if not f:
        return

    def clear(k, carry):
        holder_ref[k] = 0
        return carry

    lax.fori_loop(0, z.devices * z.capacity, clear, 0, unroll=8)

    def degree(q, b):
        def block(p, inner):
            holder_ref[place_ref[b + p]] = q * OB + p
            return inner

        count = z.turns(q) + 1
        rides = (q >= z.degrees // 2) & (mate_ref[q] >= 0)
        lax.fori_loop(0, count - jnp.where(rides, 1, 0), block, 0)
        return b + count

    lax.fori_loop(0, z.degrees, degree, 0)


def pack(z, grid_field, f, slots, *tables):
    total = z.devices * slots
    smem = pl.BlockSpec(memory_space=pltpu.SMEM)
    table = jax.ShapeDtypeStruct((z.devices * z.capacity if f else z.blocks,), jnp.int32)
    return pl.pallas_call(
        functools.partial(pack_kernel, z, f, slots),
        in_specs=[smem] * len(tables) + [pl.BlockSpec(memory_space=pl.ANY)],
        out_specs=[pl.BlockSpec(memory_space=pltpu.VMEM), smem],
        out_shape=[jax.ShapeDtypeStruct((total, z.local, z.width), jnp.bfloat16), table],
        scratch_shapes=[
            pltpu.VMEM((z.local, z.blocks, z.width), jnp.bfloat16),
            pltpu.VMEM(((z.local + 1) * (z.blocks + 1), z.width), jnp.float32),
            pltpu.SemaphoreType.DMA((PARTS,)),
        ]
        + [pltpu.SMEM((z.devices,), jnp.int32)] * (0 if f else 2),
        compiler_params=pltpu.CompilerParams(vmem_limit_bytes=VMEM),
        cost_estimate=pl.CostEstimate(flops=10**9, bytes_accessed=10**7, transcendentals=0),
        name=f"pack_{f}",
    )(*tables, grid_field)


def solve_kernel(z, f, slots, per_step, holder_ref, start_ref, mate_ref, me_ref, columns_ref, inverses_ref, *rest):
    (own, across, along, corner, own_odd, across_odd, along_odd, corner_odd, far) = rest[:9]
    out_ref, matrix_ref, square_ref, above_ref, below_ref, sems = rest[9:]
    strength = diffusion_numbers[f]
    step = pl.program_id(0)
    shape = (z.levels, z.width)
    me = me_ref[0]

    @pl.when(step == 0)
    def _():
        sources = [
            own.at[f], own_odd.at[f], across.at[f], across_odd.at[f],
            along.at[f], along_odd.at[f], corner.at[0], corner_odd.at[0],
            inverses_ref.at[f, 0], far.at[f],
        ]
        copies = [
            pltpu.make_async_copy(source, matrix_ref.at[i], sems.at[i])
            for i, source in enumerate(sources)
        ]
        for copy in copies:
            copy.start()
        level = lax.broadcasted_iota(jnp.int32, shape, 0)

        def radius(positions):
            return inner_radius + shell_depth * (positions + 1).astype(jnp.float32) / (z.levels + 1)

        here = radius(level)
        scaled = (shell_depth / (z.levels + 1)) / here
        square_ref[...] = strength * (scaled * scaled)
        above_ref[...] = jnp.where(level == z.levels - 1, 0.0, strength * radius(level + 1) / here)
        below_ref[...] = jnp.where(level == 0, 0.0, strength * radius(level - 1) / here)
        for copy in copies:
            copy.wait()

    column = lax.broadcasted_iota(jnp.int32, shape, 1)
    host = quotient(holder_ref[me * slots], OB, z.degrees * OB)
    rider = mate_ref[host]
    host_at = z.turns(host) - step * per_step
    rides = (rider >= 0) & (host_at >= 0) & (host_at < per_step)

    def block(i, carry):
        again = i >= per_step
        k = jnp.where(again, host_at, i)
        code = holder_ref[me * slots + jnp.minimum(step * per_step + k, slots - 1)]
        q = jnp.where(again, rider, quotient(code, OB, z.degrees * OB))
        value = z.spacing * (q + 1) - 1
        last = value - lax.rem(code, OB) * (z.width // 2)
        begin = jnp.where(again, z.last_live(host), 0)
        end = jnp.where(again, begin + z.last_live(rider), 2 * last + 2)
        offset = z.owner(start_ref[q]) ^ me
        which = jnp.where(offset < PLANE, offset, PLANE + 1)
        which = jnp.where(q >= z.degrees // 2, which, PLANE)
        factor = (value * (value + 1)).astype(jnp.float32)
        u = columns_ref[:, k].reshape(shape).astype(jnp.float32)
        u = jnp.where((column >= begin) & (column < end), u, 0.0)
        weight = (1.0 - 2.0 * strength) - factor * square_ref[...]
        rhs = weight * u
        rhs += above_ref[...] * pltpu.roll(u, z.levels - 1, 0)
        rhs += below_ref[...] * pltpu.roll(u, 1, 0)
        high = rhs.astype(jnp.bfloat16)
        low = (rhs - high.astype(jnp.float32)).astype(jnp.bfloat16)
        both = jnp.concatenate([high, low], axis=1)
        product = jnp.dot(matrix_ref[which], both, preferred_element_type=jnp.float32)
        solved = product[:, : z.width] + product[:, z.width :]
        earlier = out_ref[:, k].reshape(shape).astype(jnp.float32)
        solved = jnp.where(column >= begin, solved, earlier).astype(jnp.bfloat16)
        out_ref[:, k] = solved.reshape(z.devices, z.local, z.width)
        return carry

    lax.fori_loop(0, per_step + jnp.where(rides, 1, 0), block, 0)


def solve(z, holder, degree_start, mate, me, columns, inverses, pieces, f, slots):
    steps = pl.cdiv(slots, 9)
    per_step = pl.cdiv(slots, steps)
    block = (z.devices, per_step, z.local, z.width)
    spec = pl.BlockSpec(block, lambda i, *s: (0, i, 0, 0))
    return pl.pallas_call(
        functools.partial(solve_kernel, z, f, slots, per_step),
        grid_spec=pltpu.PrefetchScalarGridSpec(
            num_scalar_prefetch=4,
            grid=(steps,),
            in_specs=[spec] + [pl.BlockSpec(memory_space=pl.ANY)] * (1 + len(pieces)),
            out_specs=spec,
            scratch_shapes=[pltpu.VMEM((PLANE + 2, z.levels, z.levels), jnp.bfloat16)]
            + [pltpu.VMEM((z.levels, z.width), jnp.float32)] * 3
            + [pltpu.SemaphoreType.DMA((PLANE + 2,))],
        ),
        out_shape=jax.ShapeDtypeStruct(columns.shape, jnp.bfloat16),
        compiler_params=pltpu.CompilerParams(vmem_limit_bytes=VMEM),
        cost_estimate=pl.CostEstimate(flops=10**10, bytes_accessed=10**7, transcendentals=0),
        name=f"solve_{f}",
    )(holder, degree_start, mate, me, columns, inverses, *pieces)


def edge_slopes(z, second, before_last, before, after):
    def wide(ref):
        return ref[...].reshape(z.blocks, z.width).astype(jnp.float32)

    first = 0.5 * (wide(second) - wide(before))
    last = 0.5 * (wide(after) - wide(before_last))
    return first.astype(jnp.bfloat16), last.astype(jnp.bfloat16)


def unpack_kernel(z, f, place_ref, mate_ref, returned_ref, *rest):
    if f:
        earlier_ref, _, before_ref, after_ref, grid_ref, slope_ref, second_ref, before_last_ref = rest[:8]
        edge_ref, edge_sems = rest[-2:]
    else:
        grid_ref, slope_ref = rest[:2]
    level_ref, inner_ref, wide_ref, sems = rest[8 if f else 2 :][:4]
    pitch = z.blocks + 1
    ends = [
        pltpu.make_async_copy(
            earlier_ref.at[f - 1, level], edge_ref.at[i], edge_sems.at[i]
        )
        for i, level in enumerate((1, z.local - 2))
    ] if f else []
    for copy in ends:
        copy.start()

    def gather(g, carry):
        for k in range(BATCH):
            b = g * BATCH + k
            tile = returned_ref[place_ref[b]].astype(jnp.float32)
            wide_ref[pl.ds(b, z.local, stride=pitch), :] = tile
        return carry

    lax.fori_loop(0, z.blocks // BATCH, gather, 0)
    column = lax.broadcasted_iota(jnp.int32, (z.local, z.width), 1)

    def ride(q, carry):
        b, host_block, live = riding(z, mate_ref, q)
        tile = returned_ref[place_ref[b]].astype(jnp.float32)
        rider = pltpu.roll(tile, z.width - live, 1)
        host_rows = pl.ds(host_block, z.local, stride=pitch)
        wide_ref[host_rows, :] = jnp.where(column < live, tile, 0.0)
        rows = pl.ds(b, z.local, stride=pitch)
        wide_ref[rows, :] = jnp.where(column < z.last_live(q), rider, 0.0)
        return carry

    lax.fori_loop(z.degrees // 2, z.degrees, ride, 0, unroll=RIDES)

    def group(g, carry):
        at = pl.multiple_of(g * GROUP, GROUP)
        rows = pl.ds(at, GROUP)
        value = [wide_ref[pl.ds(at + i * pitch, GROUP), :] for i in range(z.local)]
        for i in range(z.local):
            level_ref[i, rows, :] = value[i].astype(jnp.bfloat16)
        for i in range(1, z.local - 1):
            slope = 0.5 * (value[i + 1] - value[i - 1])
            inner_ref[i - 1, rows, :] = slope.astype(jnp.bfloat16)
        if f:
            second_ref[rows, :] = value[1].astype(jnp.bfloat16)
            before_last_ref[rows, :] = value[-2].astype(jnp.bfloat16)
        return carry

    groups = z.blocks // GROUP
    copies = []
    for i in range(PARTS):
        begin, end = i * groups // PARTS, (i + 1) * groups // PARTS
        lax.fori_loop(begin, end, group, 0, unroll=2)
        rows = pl.ds(begin * GROUP, (end - begin) * GROUP)
        copies += [
            pltpu.make_async_copy(
                level_ref.at[:, rows, :], grid_ref.at[f, :, rows, :], sems.at[2 * i]
            ),
            pltpu.make_async_copy(
                inner_ref.at[:, rows, :],
                slope_ref.at[f, pl.ds(1, z.local - 2), rows, :],
                sems.at[2 * i + 1],
            ),
        ]
        for copy in copies[-2:]:
            copy.start()
    if f:
        for copy in ends:
            copy.wait()
        slopes = edge_slopes(z, edge_ref.at[0], edge_ref.at[1], before_ref, after_ref)
        for i, level in enumerate((0, z.local - 1)):
            edge_ref[2 + i] = slopes[i]
            copy = pltpu.make_async_copy(
                edge_ref.at[2 + i], slope_ref.at[f - 1, level], edge_sems.at[2 + i]
            )
            copy.start()
            copies.append(copy)
    for copy in copies:
        copy.wait()


def unpack(z, place, mate, returned, f, earlier):
    whole = jax.ShapeDtypeStruct((z.fields, z.local, z.blocks, z.width), jnp.bfloat16)
    level = jax.ShapeDtypeStruct((z.blocks, z.width), jnp.bfloat16)
    smem, anywhere = pl.BlockSpec(memory_space=pltpu.SMEM), pl.BlockSpec(memory_space=pl.ANY)
    vmem = pl.BlockSpec(memory_space=pltpu.VMEM)
    edge_scratch = [
        pltpu.VMEM((4, z.blocks, z.width), jnp.bfloat16),
        pltpu.SemaphoreType.DMA((4,)),
    ]
    return pl.pallas_call(
        functools.partial(unpack_kernel, z, f),
        in_specs=[smem, smem, vmem] + [anywhere, anywhere, vmem, vmem] * min(f, 1),
        out_specs=[anywhere] * 2 + [vmem] * 2 * min(f, 1),
        out_shape=[whole] * 2 + [level] * 2 * min(f, 1),
        scratch_shapes=[
            pltpu.VMEM((z.local, z.blocks, z.width), jnp.bfloat16),
            pltpu.VMEM((z.local - 2, z.blocks, z.width), jnp.bfloat16),
            pltpu.VMEM(((z.local + 1) * (z.blocks + 1), z.width), jnp.float32),
            pltpu.SemaphoreType.DMA((2 * PARTS,)),
        ]
        + edge_scratch * min(f, 1),
        input_output_aliases={3: 0, 4: 1} if f else {},
        compiler_params=pltpu.CompilerParams(vmem_limit_bytes=VMEM if f else MORE_VMEM),
        cost_estimate=pl.CostEstimate(flops=10**9, bytes_accessed=10**7, transcendentals=0),
        name=f"unpack_{f}",
    )(place, mate, returned, *earlier)


def rim_kernel(z, place_ref, mate_ref, returned_ref, first_ref, last_ref, first_wide_ref, last_wide_ref):
    sides = ((first_wide_ref, 0), (last_wide_ref, z.local - 1))

    def gather(g, carry):
        for k in range(BATCH):
            b = g * BATCH + k
            tile = returned_ref[place_ref[b]].astype(jnp.float32)
            for wide_ref, row in sides:
                wide_ref[pl.ds(b, 1), :] = tile[row : row + 1]
        return carry

    lax.fori_loop(0, z.blocks // BATCH, gather, 0)
    column = lax.broadcasted_iota(jnp.int32, (z.local, z.width), 1)

    def ride(q, carry):
        b, host_block, live = riding(z, mate_ref, q)
        tile = returned_ref[place_ref[b]].astype(jnp.float32)
        rider = pltpu.roll(tile, z.width - live, 1)
        rider = jnp.where(column < z.last_live(q), rider, 0.0)
        tile = jnp.where(column < live, tile, 0.0)
        for wide_ref, row in sides:
            wide_ref[pl.ds(host_block, 1), :] = tile[row : row + 1]
            wide_ref[pl.ds(b, 1), :] = rider[row : row + 1]
        return carry

    lax.fori_loop(z.degrees // 2, z.degrees, ride, 0, unroll=RIDES)
    first_ref[0] = first_wide_ref[...].astype(jnp.bfloat16)
    last_ref[0] = last_wide_ref[...].astype(jnp.bfloat16)


def rims(z, place, mate, returned, f):
    level = jax.ShapeDtypeStruct((1, z.blocks, z.width), jnp.bfloat16)
    spec = pl.BlockSpec(level.shape, lambda i, *s: (0, 0, 0))
    return pl.pallas_call(
        functools.partial(rim_kernel, z),
        grid_spec=pltpu.PrefetchScalarGridSpec(
            num_scalar_prefetch=2,
            grid=(1,),
            in_specs=[pl.BlockSpec(returned.shape, lambda i, *s: (0, 0, 0))],
            out_specs=[spec, spec],
            scratch_shapes=[pltpu.VMEM((z.blocks, z.width), jnp.float32)] * 2,
        ),
        out_shape=[level, level],
        compiler_params=pltpu.CompilerParams(vmem_limit_bytes=VMEM if f else MORE_VMEM),
        cost_estimate=pl.CostEstimate(flops=10**8, bytes_accessed=3 * 10**6, transcendentals=0),
        name=f"rims_{f}",
    )(place, mate, returned)


def edge_kernel(z, f, second_ref, before_last_ref, before_ref, after_ref, _, slope_ref, edge_ref, sems):
    slopes = edge_slopes(z, second_ref, before_last_ref, before_ref, after_ref)
    copies = []
    for i, level in enumerate((0, z.local - 1)):
        edge_ref[i] = slopes[i]
        copies.append(pltpu.make_async_copy(edge_ref.at[i], slope_ref.at[f, level], sems.at[i]))
        copies[i].start()
    for copy in copies:
        copy.wait()


def edges(z, slope, inside, outside, f):
    vmem, anywhere = pl.BlockSpec(memory_space=pltpu.VMEM), pl.BlockSpec(memory_space=pl.ANY)
    return pl.pallas_call(
        functools.partial(edge_kernel, z, f),
        in_specs=[vmem] * 4 + [anywhere],
        out_specs=anywhere,
        out_shape=jax.ShapeDtypeStruct(slope.shape, slope.dtype),
        scratch_shapes=[
            pltpu.VMEM((2, z.blocks, z.width), jnp.bfloat16),
            pltpu.SemaphoreType.DMA((2,)),
        ],
        input_output_aliases={4: 0},
        compiler_params=pltpu.CompilerParams(vmem_limit_bytes=VMEM),
        name=f"edges_{f}",
    )(*inside, *outside, slope)


def beside(z, first, last):
    up = [(i, i + 1) for i in range(z.devices - 1)]
    down = [(j, i) for i, j in up]
    return lax.ppermute(last, AXES, up), lax.ppermute(first, AXES, down)


def exchange(z, value, slots):
    shaped = value.reshape(z.devices, slots, z.local, z.width)
    return lax.all_to_all(shaped, AXES, split_axis=0, concat_axis=0, tiled=True)


def body(grid_field, inverses, slot_blocks, degree_start):
    rad, lm = lax.axis_size("rad"), lax.axis_size("lm")
    z = Sizes(rad * lm, grid_field, inverses, slot_blocks)
    choices = slot_choices(z)
    kernels = z.local % 16 == 0 and z.fields == 2 and z.blocks % GROUP == 0 and z.blocks % BATCH == 0 and rad % 4 == 0 and lm == PLANE // 2
    low, high = z.counts[z.degrees // 2 - 1 : z.degrees // 2 + 1]
    if not kernels or low + GIFT > choices[0] or high <= GIFT or z.capacity - choices[0] > GIFT:
        return plain_body(z, grid_field, inverses, degree_start)
    me = lax.axis_index(AXES).reshape(1).astype(jnp.int32)
    choice, *tables = plan(z, degree_start, choices)
    routes = [functools.partial(route, z, slots) for slots in choices]
    return lax.switch(choice[0], routes, grid_field, inverses, degree_start, me, *tables)


def route(z, slots, grid_field, inverses, degree_start, me, mate, load, high):
    sent_0, place = pack(z, grid_field, 0, slots, degree_start, mate, load, high)
    sent_1, holder = pack(z, grid_field, 1, slots, place, mate)
    sent_1, own, across, along, far = lax.optimization_barrier(
        (sent_1, *straight_inverses(inverses))
    )
    columns = [exchange(z, sent, slots) for sent in (sent_0, sent_1)]
    corner_0 = swap(across[:1], "rad", 1)
    even = [own, across, along]
    odd = other_core(even)
    pieces = lax.optimization_barrier((*even, corner_0, *odd, *other_core([corner_0]), far))
    solved_0 = solve(z, holder, degree_start, mate, me, columns[0], inverses, pieces, 0, slots)
    corner_1 = swap(along[1:], "lm", 2)
    pieces = (*even, corner_1, *odd, *other_core([corner_1]), far)
    solved_1 = solve(z, holder, degree_start, mate, me, columns[1], inverses, pieces, 1, slots)
    solved = [solved_0, solved_1]
    returned = [
        exchange(z, solved[f], slots).reshape(z.devices * slots, z.local, z.width)
        for f in range(z.fields)
    ]
    outside = beside(z, *rims(z, place, mate, returned[0], 0))
    outs = unpack(z, place, mate, returned[0], 0, ())
    last, *outs = lax.optimization_barrier((returned[1], *outs))
    last_outside = beside(z, *rims(z, place, mate, last, 1))
    grid, slope, *inside = unpack(z, place, mate, last, 1, (*outs, *outside))
    return grid, edges(z, slope, inside, last_outside, 1)


def plain_body(z, grid_field, inverses, degree_start):
    index = np.arange(z.degrees)
    counts = np.asarray(z.counts)
    degree_of = np.repeat(index, counts)
    place_in = np.arange(z.blocks) - np.asarray(z.starts)[degree_of]
    value = z.spacing * (index + 1) - 1
    slot_place = degree_start[degree_of] + jnp.asarray(place_in, jnp.int32)
    total = z.devices * z.capacity
    holder = jnp.full((total,), z.blocks, jnp.int32)
    holder = holder.at[slot_place].set(jnp.arange(z.blocks, dtype=jnp.int32))
    sent = jnp.take(grid_field, holder, axis=2, mode="fill", fill_value=0)
    sent = sent.reshape(z.fields, z.local, z.devices, z.capacity, z.width)
    columns = lax.all_to_all(sent, AXES, split_axis=2, concat_axis=1, tiled=True)
    columns = columns.reshape(z.fields, z.levels, z.capacity, z.width)
    device = lax.axis_index(AXES)
    mine = lax.dynamic_slice_in_dim(holder, device * z.capacity, z.capacity)
    order = jnp.asarray(place_in)[:, None] * OB + np.arange(z.width)[None, :] // 2
    live_table = (order <= jnp.asarray(value[degree_of])[:, None]).astype(jnp.float32)
    live = jnp.take(live_table, mine, axis=0, mode="fill", fill_value=0)
    factor = (value * (value + 1)).astype(np.float32)[degree_of]
    factor = jnp.take(jnp.asarray(factor), mine, mode="fill", fill_value=0)
    upper = jnp.take(jnp.asarray(degree_of >= z.degrees // 2), mine, mode="fill", fill_value=False)
    radius = inner_radius + shell_depth * jnp.arange(z.levels + 2, dtype=jnp.float32) / (z.levels + 1)
    here = radius[1:-1][None, :, None, None]
    padded = jnp.pad(columns.astype(jnp.float32), ((0, 0), (1, 1), (0, 0), (0, 0)))
    weighted = padded * radius[None, :, None, None]
    second = (weighted[:, 2:] - 2.0 * weighted[:, 1:-1] + weighted[:, :-2]) / here
    scaled = (shell_depth / (z.levels + 1)) / here
    centre = padded[:, 1:-1]
    strength = jnp.asarray(diffusion_numbers, jnp.float32)[:, None, None, None]
    angular = factor[None, None, :, None] * (scaled * scaled) * centre
    rhs = (centre + strength * (second - angular)) * live[None, None]

    def solve_slot(carry, at):
        matrix = lax.dynamic_index_in_dim(
            inverses, upper[at].astype(jnp.int32), 1, keepdims=False
        ).astype(jnp.float32)
        block = lax.dynamic_index_in_dim(rhs, at, 2, keepdims=False)
        product = jnp.einsum("fij,fjc->fic", matrix, block, precision=lax.Precision.HIGHEST)
        return carry, product.astype(jnp.bfloat16)

    solved = lax.scan(solve_slot, 0, jnp.arange(z.capacity))[1]
    solved = jnp.moveaxis(solved, 0, 2)
    solved = solved.reshape(z.fields, z.devices, z.local, z.capacity, z.width)
    returned = lax.all_to_all(solved, AXES, split_axis=1, concat_axis=3, tiled=True)
    returned = returned.reshape(z.fields, z.local, total, z.width)
    grid = jnp.take(returned, slot_place, axis=2)
    before, after = beside(z, grid[:, :1], grid[:, -1:])
    rimmed = jnp.concatenate([before, grid, after], axis=1).astype(jnp.float32)
    return grid, (0.5 * (rimmed[:, 2:] - rimmed[:, :-2])).astype(jnp.bfloat16)


def solution(mesh):
    in_specs = (P(None, AXES), P(None, AXES), P(), P())
    out_specs = (P(None, AXES), P(None, AXES))
    return jax.shard_map(body, mesh=mesh, in_specs=in_specs, out_specs=out_specs, check_vma=False)
```
